32 devices in a mesh: dp: 16 (over z, y, x), tensor: 2 (over core).
Axes of the slice: x: 2, y: 2, z: 4, core: 2. Of those that a mesh axis runs over, the one named last changes fastest.
Arguments:
- hidden_in: bfloat16 [16, 1024, 768], P(None, 'dp'), may hold values from -6 to 6
- teacher: bfloat16 [16, 1024, 768], P(None, 'dp', 'tensor'), may hold values from -6 to 6
- loss_mask: int32 [16, 1024], P(None, 'dp'), may hold values from 0 to 1, as said below
- lengths: int32 [16], replicated, may hold values from 768 to 1024, as said below
- dealing: int32 [16], replicated, may hold values from 0 to 15, each once
- norm_gain: float32 [768], replicated, may hold values from 0.5 to 1.5
- w_gate: bfloat16 [768, 1536], P(None, 'tensor'), may hold values from -0.21875 to 0.21875
- w_value: bfloat16 [768, 1536], P(None, 'tensor'), may hold values from -0.21875 to 0.21875
- w_state: bfloat16 [768, 256], replicated, may hold values from -0.21875 to 0.21875
- w_step: bfloat16 [768, 2, 24], P(None, None, 'tensor'), may hold values from -0.21875 to 0.21875
- step_bias: float32 [2, 24], P(None, 'tensor'), may hold values from -4 to -1
- conv_value: float32 [4, 1536], P(None, 'tensor'), may hold values from -0.5 to 0.5
- conv_vbias: float32 [1536], P('tensor'), may hold values from -0.5 to 0.5
- conv_state: float32 [4, 256], replicated, may hold values from -0.5 to 0.5
- conv_sbias: float32 [256], replicated, may hold values from -0.5 to 0.5
- decay_log: float32 [24], P('tensor'), may hold values from -4 to 2
- skip_gain: float32 [24], P('tensor'), may hold values from 0.5 to 1.5
- out_gain: float32 [1536], P('tensor'), may hold values from 0.5 to 1.5
- w_out: bfloat16 [1536, 768], P('tensor'), may hold values from -0.15625 to 0.15625
Outputs:
- layer_out: bfloat16 [16, 1024, 768], P('dp', None, 'tensor')
- grad_in: bfloat16 [16, 1024, 768], P(None, 'dp', 'tensor')
- grad_norm_gain: float32 [768], replicated
- grad_w_gate: float32 [768, 1536], P(None, 'tensor')
- grad_w_value: float32 [768, 1536], P(None, 'tensor')
- grad_w_state: float32 [768, 256], replicated
- grad_w_step: float32 [768, 2, 24], P(None, None, 'tensor')
- grad_step_bias: float32 [2, 24], P(None, 'tensor')
- grad_conv_value: float32 [4, 1536], P(None, 'tensor')
- grad_conv_vbias: float32 [1536], P('tensor')
- grad_conv_state: float32 [4, 256], replicated
- grad_conv_sbias: float32 [256], replicated
- grad_decay_log: float32 [24], P('tensor')
- grad_skip_gain: float32 [24], P('tensor')
- grad_out_gain: float32 [1536], P('tensor')
- grad_w_out: float32 [1536, 768], P('tensor')
The draws below stay inside these ranges and needn't reach their ends.
Inputs may be any that keep to these rules, and one draw needn't show every extreme that they name: `lengths`: the number of real tokens of each sequence; positions from it on are padding; some sequence has 1024 and some has 768. `loss_mask`: 1 marks a token that counts in the loss; position 0 of every sequence is marked. A permutation of 0 .. 15; slot j of the dealt order holds sequence dealing[j], and slots j .. are those of index j of dp.
All inputs are finite; a program needn't handle non-finite values.
Results may differ from the reference program's by a relative error of at most 0.0095.
Values may be sent and summed in bfloat16 or wider, within the bound.
No kernel may reach another device: no remote copies, remote signals or barrier semaphores. Data moves between devices by JAX's collectives and lax.ppermute only.
A program may use at most 192 MiB of HBM per device.

```python
import jax
import jax.numpy as jnp
from jax import lax

D = 768
INNER = 1536
H = 24
P_SIZE = 64
N = 64
Q = 128
KW = 4
LEN = 1024
SEQ_DEV = 1
SEQS = 16


def draw_lengths(key, part):
    first, second = jax.random.split(key)
    values = jax.random.randint(first, (SEQS,), 3 * LEN // 4, LEN + 1)
    spots = jax.random.permutation(second, SEQS)
    values = values.at[spots[0]].set(LEN)
    values = values.at[spots[1]].set(3 * LEN // 4)
    return values.astype(jnp.int32)


def draw_loss_mask(key, part):
    positions = lax.broadcasted_iota(jnp.int32, (SEQS, LEN), 1)
    chance = 200 + 600 * positions // LEN
    rolls = jax.random.randint(key, (SEQS, LEN), 0, 1000)
    marked = (rolls < chance).astype(jnp.int32)
    return jnp.where(positions == 0, 1, marked).astype(jnp.int32)


def level_of(stream_key, shape, shards, low, largest):
    factor_of = 1.0
    for axis_at, blocks in shards:
        draws = jax.random.uniform(jax.random.fold_in(jax.random.fold_in(stream_key, 6), axis_at), (blocks,), jnp.float32, low / len(shards), largest / len(shards))
        factor_of = factor_of * jnp.repeat(jnp.exp(draws), shape[axis_at] // blocks).reshape((-1,) + (1,) * (len(shape) - 1 - axis_at))
    return factor_of


def normal_values(rng, dims, spread, bound, pieces=(), dtype=jnp.bfloat16):
    result = jax.random.normal(rng, dims, jnp.float32) * spread
    if len(pieces) > 0:
        result = level_of(rng, dims, pieces, -0.22, 0.18) * result
    return jnp.clip(result, min=-bound, max=bound).astype(dtype)


def setup_inputs(seed: int = 0) -> dict:
    splits = jax.random.split(jax.random.key(seed), 20)
    return {
        "hidden_in": normal_values(splits[0], (SEQS, LEN, D), 1.0, 6.0, ((1, 16),)),
        "teacher": normal_values(splits[1], (SEQS, LEN, D), 1.0, 6.0, ((1, 16), (2, 2))),
        "loss_mask": draw_loss_mask(jax.random.fold_in(splits[19], 71), 0),
        "lengths": draw_lengths(jax.random.fold_in(splits[19], 71), 0),
        "dealing": jax.random.permutation(splits[4], SEQS).astype(jnp.int32),
        "norm_gain": jnp.clip(1.0 + 0.1 * jax.random.normal(splits[5], (D,), jnp.float32), 0.5, 1.5),
        "w_gate": normal_values(splits[6], (D, INNER), D ** -0.5, 0.21875, ((1, 2),)),
        "w_value": normal_values(splits[7], (D, INNER), D ** -0.5, 0.21875, ((1, 2),)),
        "w_state": normal_values(splits[8], (D, 4 * N), D ** -0.5, 0.21875),
        "w_step": normal_values(splits[9], (D, 2, H), D ** -0.5, 0.21875, ((2, 2),)),
        "step_bias": jnp.clip(-4.0 + 3.0 * jax.random.uniform(splits[10], (2, H), jnp.float32) ** level_of(splits[10], (2, H), ((1, 2),), -0.2, 0.2), -4.0, -1.0),
        "conv_value": jnp.clip(jax.random.uniform(splits[11], (KW, INNER), jnp.float32, -0.5, 0.5) * level_of(splits[11], (KW, INNER), ((1, 2),), -0.4, 0.0), -0.5, 0.5),
        "conv_vbias": jnp.clip(jax.random.uniform(splits[12], (INNER,), jnp.float32, -0.5, 0.5) * level_of(splits[12], (INNER,), ((0, 2),), -0.4, 0.0), -0.5, 0.5),
        "conv_state": jnp.clip(jax.random.uniform(splits[13], (KW, 4 * N), jnp.float32, -0.5, 0.5), -0.5, 0.5),
        "conv_sbias": jnp.clip(jax.random.uniform(splits[14], (4 * N,), jnp.float32, -0.5, 0.5), -0.5, 0.5),
        "decay_log": jnp.clip(-4.0 + 6.0 * jax.random.uniform(splits[15], (H,), jnp.float32) ** level_of(splits[15], (H,), ((0, 2),), -0.2, 0.2), -4.0, 2.0),
        "skip_gain": jnp.clip(0.5 + 1.0 * jax.random.uniform(splits[16], (H,), jnp.float32) ** level_of(splits[16], (H,), ((0, 2),), -0.2, 0.2), 0.5, 1.5),
        "out_gain": jnp.clip(1.0 + 0.1 * jax.random.normal(splits[17], (INNER,), jnp.float32), 0.5, 1.5),
        "w_out": normal_values(splits[18], (INNER, D), INNER ** -0.5, 0.15625, ((0, 2),)),
    }


EPSILON = 1e-05
HIGH = lax.Precision.HIGHEST

@jax.custom_vjp
def low(v):
    return lax.optimization_barrier(v.astype(jnp.bfloat16)).astype(jnp.float32)

@jax.custom_vjp
def low_back(v):
    return v

def low_keep(v):
    return (low(v), None)

def low_pass(kept, grad):
    return (grad,)

def back_keep(v):
    return (v, None)

def back_low(kept, grad):
    return (low(grad),)
low.defvjp(low_keep, low_pass)
low_back.defvjp(back_keep, back_low)

def causal_conv(inputs, kernel, shift_bias):
    conv_width = kernel.shape[0]
    extent = inputs.shape[-2]
    widths = [(0, 0)] * (inputs.ndim - 2) + [(conv_width - 1, 0), (0, 0)]
    padded = jnp.pad(inputs, widths)
    summed = shift_bias + jnp.zeros_like(inputs)
    for offset in range(conv_width):
        summed = summed + kernel[offset] * lax.slice_in_dim(padded, offset, offset + extent, axis=inputs.ndim - 2)
    return summed

def span_scan(values, inputs_b, outputs_c, dt_steps, decay_rate):
    extent = values.shape[0]
    blocks = extent // Q
    heads_here = values.shape[1]
    log_decay = (dt_steps * decay_rate[None, :]).reshape(blocks, Q, heads_here)
    cumulative = jnp.cumsum(log_decay, axis=1)
    scaled = (values * dt_steps[:, :, None]).reshape(blocks, Q, heads_here, P_SIZE)
    keys_b = inputs_b.reshape(blocks, Q, N)
    query_c = outputs_c.reshape(blocks, Q, N)
    scores = jnp.einsum('ctn,csn->cts', query_c, keys_b, precision=HIGH)
    lower_mask = (lax.broadcasted_iota(jnp.int32, (Q, Q), 0) >= lax.broadcasted_iota(jnp.int32, (Q, Q), 1))[None, :, :, None]
    log_gaps = cumulative[:, :, None, :] - cumulative[:, None, :, :]
    within = jnp.where(lower_mask, jnp.exp(jnp.where(lower_mask, log_gaps, 0.0)), 0.0)
    inside = jnp.einsum('ctsh,cshp->cthp', scores[:, :, :, None] * within, scaled, precision=HIGH)
    closing = cumulative[:, -1:, :]
    states = jnp.einsum('csn,cshp->chnp', keys_b, jnp.exp(closing - cumulative)[:, :, :, None] * scaled, precision=HIGH)
    passing = jnp.exp(closing[:, 0, :])

    def advance(running, element):
        block_state, factor = element
        return (factor[:, None, None] * running + block_state, running)
    _, entering = lax.scan(advance, jnp.zeros((heads_here, N, P_SIZE), jnp.float32), (states, passing))
    across = jnp.einsum('ctn,chnp->cthp', query_c, entering, precision=HIGH) * jnp.exp(cumulative)[:, :, :, None]
    return (inside + across).reshape(extent, heads_here, P_SIZE)

def mix_sequence(values, states_in, dt_steps, decay_log, skip_gain):
    heads_here = decay_log.shape[0]
    decay_rate = -jnp.exp(decay_log)
    per_head = values.reshape(values.shape[0], heads_here, P_SIZE)
    forward_part = span_scan(per_head, states_in[:, :N], states_in[:, N:2 * N], dt_steps[:, 0], decay_rate)
    reverse_part = jnp.flip(span_scan(jnp.flip(per_head, 0), jnp.flip(states_in[:, 2 * N:3 * N], 0), jnp.flip(states_in[:, 3 * N:], 0), jnp.flip(dt_steps[:, 1], 0), decay_rate), 0)
    nothing = jnp.zeros_like(forward_part[:1])
    mixed = jnp.concatenate([nothing, forward_part[:-1]], 0) + jnp.concatenate([reverse_part[1:], nothing], 0) + skip_gain[None, :, None] * per_head
    return mixed.reshape(values.shape[0], -1)

def forward_seq(params, inputs, live_tok):
    norm_gain, w_gate, w_value, w_state, w_step, step_bias, conv_value, conv_vbias, conv_state, conv_sbias, decay_log, skip_gain, out_gain, w_out = params
    inv_rms = lax.rsqrt(lax.optimization_barrier(jnp.mean(inputs * inputs, -1, keepdims=True)) + EPSILON)
    normed = low(inputs * inv_rms * norm_gain)
    gate_pre = low_back(jnp.dot(normed, w_gate, precision=HIGH))
    value_pre = low_back(jnp.dot(normed, w_value, precision=HIGH))
    state_pre = low_back(jnp.dot(normed, w_state, precision=HIGH))
    step_pre = low_back(jnp.einsum('ld,dkh->lkh', normed, w_step, precision=HIGH))
    conv_in = jnp.concatenate([value_pre, state_pre], -1)
    pre_act = causal_conv(conv_in, jnp.concatenate([conv_value, conv_state], -1), jnp.concatenate([conv_vbias, conv_sbias], -1))
    activated = low(jax.nn.silu(pre_act))
    dt_steps = jax.nn.softplus(step_pre + step_bias) * live_tok[:, None, None]
    mixed = mix_sequence(activated[:, :INNER], activated[:, INNER:], dt_steps, decay_log, skip_gain)
    gated = mixed * jax.nn.silu(gate_pre)
    out_inv = lax.rsqrt(lax.optimization_barrier(jnp.mean(gated * gated, -1, keepdims=True)) + EPSILON)
    branch = low(gated * out_inv * out_gain)
    output = low_back(jnp.dot(branch, w_out, precision=HIGH))
    return inputs + output

def seq_loss(params_now, seq_in, seq_target, seq_marks, seq_live):
    layer = forward_seq(params_now, seq_in, seq_live)
    differ = layer - seq_target
    return (0.5 * jnp.sum(seq_marks[:, None] * differ * differ), layer)

def reference(hidden_in, teacher, loss_mask, lengths, dealing, norm_gain, w_gate, w_value, w_state, w_step, step_bias, conv_value, conv_vbias, conv_state, conv_sbias, decay_log, skip_gain, out_gain, w_out):
    positions = lax.broadcasted_iota(jnp.int32, (SEQS, LEN), 1)
    live_tok = (positions < lengths[:, None]).astype(jnp.float32)
    marks_all = loss_mask.astype(jnp.float32) * live_tok
    token_total = jnp.sum(marks_all)
    factor_scale = SEQ_DEV * LEN / token_total
    params = tuple((weight_in.astype(jnp.float32) for weight_in in (norm_gain, w_gate, w_value, w_state, w_step, step_bias, conv_value, conv_vbias, conv_state, conv_sbias, decay_log, skip_gain, out_gain, w_out)))
    inputs = hidden_in.astype(jnp.float32)
    targets = teacher.astype(jnp.float32)
    checked = jax.checkpoint(seq_loss)

    def total_loss(params_now, inputs_now):

        def advance(summed, element):
            seq_in, seq_target, seq_marks, seq_live = element
            part_loss, layer = checked(params_now, seq_in, seq_target, seq_marks, seq_live)
            return (summed + part_loss, layer)
        summed, layers = lax.scan(advance, jnp.zeros((), jnp.float32), (inputs_now, targets, marks_all, live_tok))
        return (summed * factor_scale, layers)
    _, pullback, layers = jax.vjp(total_loss, params, inputs, has_aux=True)
    grads, grad_inputs = pullback(jnp.ones((), jnp.float32))
    return (layers[dealing].astype(jnp.bfloat16), grad_inputs.astype(jnp.bfloat16), grads[0], grads[1], grads[2], grads[3], grads[4], grads[5], grads[6], grads[7], grads[8], grads[9], grads[10], grads[11], grads[12], grads[13])
```

```python
import jax
import jax.numpy as jnp
from jax import lax
from jax.experimental import pallas as pl
from jax.experimental.pallas import tpu as pltpu
from jax.sharding import PartitionSpec as P

D = 768
INNER = 1536
PS = 64
N = 64
Q = 128
EPS = 1e-5
NOMARK = 256.0
BF = jnp.bfloat16
F32 = jnp.float32
HI = lax.Precision.HIGHEST
VMEM_LIMIT = 58 * 1024 * 1024

NN = (((1,), (0,)), ((), ()))
NT = (((1,), (1,)), ((), ()))


def mm(a, b, dims=NN):
    return lax.dot_general(a, b, dims, preferred_element_type=F32)


def mm_hi(a, b):
    return lax.dot_general(a, b, NN, precision=HI, preferred_element_type=F32)


def lanes(c, width=Q):
    return pl.ds(pl.multiple_of(c * width, width), width)


def iota2(shape, dim):
    return lax.broadcasted_iota(jnp.int32, shape, dim)


def log1p_exp(z):
    w = 1.0 + z
    return jnp.where(w == 1.0, z, jnp.log(w) * (z / jnp.where(w == 1.0, 1.0, w - 1.0)))


RAW, DT, CUM, CUE, ROWV, INV = 0, 24, 48, 72, 96, 120


def deal_kernel(dealing, src, dst):
    count, _, width = dst.shape
    if src.shape[2] == width:
        col = pl.ds(0, width)
    else:
        col = pl.ds(pl.multiple_of(lax.axis_index("tensor") * width, width), width)

    @pl.loop(0, count)
    def _(j):
        dst[j] = src[dealing[j], :, col]


def undeal_kernel(dealing, src, dst):
    @pl.loop(0, dst.shape[0])
    def _(j):
        dst[dealing[j]] = src[j]


def forward_kernel(
    length, xo, xs, wt, wot, cc, cd, rc,
    xT, nT, rows, dec, gate, uO, preO, act, cs, eO, mixed, sin, pO, pF,
    u_s, raw_s, w_s, dS, run, vw, bu,
):
    T = xo.shape[0]
    CH = T // Q
    C = gate.shape[0]
    HH = C // PS
    half = xo.shape[1]
    m = lax.axis_index("tensor")
    own = pl.multiple_of(m * half, half)
    other = pl.multiple_of((1 - m) * half, half)

    @pl.loop(0, CH)
    def _(c):
        l = lanes(c)
        xT[pl.ds(own, half), l] = xo[l, :].astype(F32).T.astype(BF)
        xT[pl.ds(other, half), l] = xs[l, :].astype(F32).T.astype(BF)
        x = xT[:, l].astype(F32)
        inv = lax.rsqrt(jnp.sum(x * x, 0, keepdims=True) / D + EPS)
        rows[INV : INV + 8, l] = jnp.broadcast_to(inv, (8, Q))
        nT[:, l] = (x * inv * cd[:, 0:1]).astype(BF)

    @pl.loop(0, T // 256)
    def _(j):
        l = lanes(j, 256)
        n = nT[:, l]
        gate[:, l] = mm(wt[0:C, :], n)
        u_s[:, l] = mm(wt[C : 2 * C + 256, :], n)
        raw_s[:, l] = mm(wt[2 * C + 256 : 2 * C + 288, :], n)

    raw = raw_s[0:24, :] + rc[:, 0:1]
    live = (iota2((1, T), 1) < length[0]).astype(F32)
    dt = (jnp.maximum(raw, 0.0) + log1p_exp(jnp.exp(-jnp.abs(raw)))) * live
    la = dt * rc[:, 1:2]
    rows[RAW : RAW + 24, :] = raw
    rows[DT : DT + 24, :] = dt
    upper = (iota2((Q, Q), 0) <= iota2((Q, Q), 1)).astype(F32)
    lower = (iota2((Q, Q), 0) >= iota2((Q, Q), 1)).astype(F32)
    stacked = jnp.concatenate([la[:, c * Q : (c + 1) * Q] for c in range(CH)], 0)
    cum_f = mm_hi(stacked, upper)
    cum_b = mm_hi(stacked, lower)
    first = iota2((24, Q), 0) < HH
    for c in range(CH):
        r = slice(24 * c, 24 * c + 24)
        k = slice(Q * c, Q * c + Q)
        cum = jnp.where(first, cum_f[r], cum_b[r])
        dtc = dt[:, k]
        rows[CUM : CUM + 24, k] = cum
        rows[CUE : CUE + 24, k] = cum - la[:, k]
        rows[ROWV : ROWV + 24, k] = jnp.where(
            dtc > 0.0, cum - jnp.log(jnp.where(dtc > 0.0, dtc, 1.0)), 1e30
        )
        tot = jnp.broadcast_to(jnp.sum(la[:, k], 1, keepdims=True), (24, Q))
        dec[c] = jnp.exp(tot)
        w_s[:, k] = jnp.exp(tot - cum) * dtc

    at = iota2((64, T), 1)

    @pl.loop(0, u_s.shape[0] // 64)
    def _(b):
        r = pl.ds(pl.multiple_of(b * 64, 64), 64)
        uu = u_s[r, :]
        col = cc[r, :]
        pre = col[:, 4:5] + col[:, 3:4] * uu
        for back in (1, 2, 3):
            shifted = jnp.where(at >= back, pltpu.roll(uu, back, 1), 0.0)
            pre = pre + col[:, 3 - back : 4 - back] * shifted
        uO[r, :] = uu.astype(BF)
        preO[r, :] = pre.astype(BF)
        act[r, :] = (pre * jax.nn.sigmoid(pre)).astype(BF)

    cs[0:64, :] = pltpu.roll(act[C + 64 : C + 128, :].astype(F32), 1, 1).astype(BF)
    cs[64:128, :] = pltpu.roll(act[C + 192 : C + 256, :].astype(F32), T - 1, 1).astype(BF)

    zeros = jnp.zeros((64, Q), BF)

    @pl.loop(0, CH)
    def _(c):
        l = lanes(c)
        for h in range(HH):
            v = act[64 * h : 64 * h + 64, l].astype(F32)
            vw[64 * h : 64 * h + 64, 0:Q] = (v * w_s[h : h + 1, l]).astype(BF)
            vw[64 * h : 64 * h + 64, Q : 2 * Q] = (v * w_s[HH + h : HH + h + 1, l]).astype(BF)
        both = jnp.concatenate(
            [
                jnp.concatenate([act[C : C + 64, l], zeros], 1),
                jnp.concatenate([zeros, act[C + 128 : C + 192, l]], 1),
            ],
            0,
        )
        dS[c] = mm(vw[...], both, NT)

    run[...] = jnp.zeros_like(run)
    low = iota2((64, Q), 1) < 64
    low_h = iota2((HH, Q), 1) < 64

    @pl.loop(0, CH)
    def _(i):
        d = jnp.where(low_h, dec[i][0:HH], dec[CH - 1 - i][HH : 2 * HH])
        for h in range(HH):
            r = slice(64 * h, 64 * h + 64)
            now = run[r, :]
            sin[i, r, :] = now.astype(BF)
            run[r, :] = now * d[h : h + 1] + jnp.where(low, dS[i, r, :], dS[CH - 1 - i, r, :])

    before = iota2((Q, Q), 1) < iota2((Q, Q), 0)
    after = iota2((Q, Q), 1) > iota2((Q, Q), 0)
    top = iota2((Q, Q), 0) < 64

    @pl.loop(0, CH)
    def _(c):
        l = lanes(c)
        bf = act[C : C + 64, l]
        bb = act[C + 128 : C + 192, l]
        cf = cs[0:64, l]
        cb = cs[64:128, l]
        gf = mm(cf.astype(F32).T.astype(BF), bf)
        gb = mm(cb.astype(F32).T.astype(BF), bb)
        g = jnp.where(before, gf, jnp.where(after, gb, 0.0))
        cue = rows[CUE : CUE + 24, l]
        cols = jnp.concatenate([cue, jnp.zeros((Q - 24, Q), F32)], 0).T
        ecue = jnp.exp(cue)
        zc = jnp.zeros((64, Q), BF)
        yf = mm(sin[c], jnp.concatenate([cf, zc], 0))
        yb = mm(sin[CH - 1 - c], jnp.concatenate([zc, cb], 0))
        total = jnp.zeros((1, Q), F32)
        for j in range(HH // 2):
            ms = []
            for h in (2 * j, 2 * j + 1):
                gap = jnp.where(
                    before,
                    cols[:, h : h + 1] - rows[ROWV + h : ROWV + h + 1, l],
                    cols[:, HH + h : HH + h + 1] - rows[ROWV + HH + h : ROWV + HH + h + 1, l],
                )
                e = jnp.exp(jnp.where(before | after, gap, -1e30))
                eO[c, h] = e.astype(BF)
                ms.append((e * g).astype(BF))
            v = act[128 * j : 128 * j + 128, l]
            vz = jnp.zeros_like(v)
            pair = jnp.concatenate([jnp.where(top, v, vz), jnp.where(top, vz, v)], 1)
            y = mm(pair, jnp.concatenate(ms, 1), NT)
            for k in (0, 1):
                h = 2 * j + k
                r = slice(64 * h, 64 * h + 64)
                mix = (
                    y[64 * k : 64 * k + 64]
                    + ecue[h : h + 1] * yf[r]
                    + ecue[HH + h : HH + h + 1] * yb[r]
                    + cc[r, 5:6] * v[64 * k : 64 * k + 64].astype(F32)
                )
                mixed[r, l] = mix
                gt = gate[r, l]
                gated = mix * (gt * jax.nn.sigmoid(gt))
                total = total + jnp.sum(gated * gated, 0, keepdims=True)
                bu[r, l] = (gated * cc[r, 6:7]).astype(BF)
        pF[D : D + 8, l] = jnp.broadcast_to(total, (8, Q))
        top_part = total.astype(BF).astype(F32)
        pO[D : D + 16, l] = jnp.where(
            iota2((16, Q), 0) == 0, top_part, jnp.where(iota2((16, Q), 0) == 1, total - top_part, 0.0)
        ).astype(BF)

    @pl.loop(0, T // 256)
    def _(j):
        l = lanes(j, 256)
        part = mm(wot[...], bu[:, l])
        pF[0:D, l] = part
        pO[0:D, l] = part.astype(BF)


def middle_kernel(
    scale, p0, p1, xT, to, ts, wo, wg, nT, gate, mixed, act, cc, cd,
    lo, doT, dyT, dgate, small, m0, m1, m2, m3,
    res_s, tea_s, branch, dbr, dot_s, acc_g, acc_s, q_s,
):
    T = to.shape[0]
    CH = T // Q
    C = gate.shape[0]
    half = to.shape[1]
    m = lax.axis_index("tensor")
    own = pl.multiple_of(m * half, half)
    other = pl.multiple_of((1 - m) * half, half)

    @pl.loop(0, CH)
    def _(c):
        l = lanes(c)
        tea_s[pl.ds(own, half), :] = to[l, :].astype(F32).T
        tea_s[pl.ds(other, half), :] = ts[l, :].astype(F32).T
        pt = p0[0:D, l] + p1[0:D, l].astype(F32)
        sums = p1[D : D + 16, l].astype(F32)
        q = lax.rsqrt((p0[D : D + 1, l] + (sums[0:1] + sums[1:2])) / INNER + EPS)
        q_s[:, l] = jnp.broadcast_to(q, (8, Q))
        res = xT[:, l].astype(F32) + q * pt
        res_s[...] = res
        tea = tea_s[...]
        do = jnp.where(tea < 0.5 * NOMARK, (res - tea) * scale[0], 0.0).astype(BF)
        doT[:, l] = do
        dot_s[:, l] = jnp.broadcast_to(jnp.sum(do.astype(F32) * pt, 0, keepdims=True), (8, Q))
        lo[l, :] = res_s[pl.ds(own, half), :].T.astype(BF)

    acc_g[...] = jnp.zeros_like(acc_g)
    acc_s[...] = jnp.zeros_like(acc_s)

    @pl.loop(0, T // 256)
    def _(j):
        l = lanes(j, 256)
        dbr[...] = mm(wo[...], doT[:, l])
        q = q_s[0:1, l]
        q3 = q * q * q * dot_s[0:1, l] / INNER

        @pl.loop(0, C // 64)
        def _(b):
            r = pl.ds(pl.multiple_of(b * 64, 64), 64)
            d = dbr[r, :]
            g = gate[r, l]
            mix = mixed[r, l]
            sg = jax.nn.sigmoid(g)
            si = g * sg
            gated = mix * si
            gain = cc[r, 6:7]
            gq = gated * q
            branch[r, l] = (gq * gain).astype(BF)
            pg = d * gq
            acc_g[r, :] += pg[:, 0:Q] + pg[:, Q : 2 * Q]
            dgt = q * (d * gain) - gated * q3
            dy = dgt * si
            dyT[r, l] = dy
            ps = dy * act[r, l].astype(F32)
            acc_s[r, :] += ps[:, 0:Q] + ps[:, Q : 2 * Q]
            dgate[r, l] = (dgt * mix * (sg * (1.0 + g * (1.0 - sg)))).astype(BF)

    lane = iota2((C, Q), 1)
    small[...] = jnp.where(
        lane == 37,
        jnp.sum(acc_s[...], 1, keepdims=True),
        jnp.where(lane == 38, jnp.sum(acc_g[...], 1, keepdims=True), 0.0),
    )

    place = lax.axis_index("dp") % 4
    share = m0.shape[0]
    for k, ref in enumerate((m0, m1, m2, m3)):
        r = pl.ds(pl.multiple_of((place ^ k) * share, share), share)
        ref[:, 0:D] = mm(branch[r, :], doT[...], NT).astype(BF)
        gg = mm(nT[r, :], dgate[...], NT)
        ref[:, D : D + C] = gg.astype(BF)
        part = jnp.sum(gg * wg[r, :].astype(F32), 1, keepdims=True) / cd[r, 0:1]
        small[r, :] = jnp.where(iota2((share, Q), 1) == 41, part, small[r, :])


def backward_kernel(
    act, cs, rows, dec, e_in, sin, dyT, cc,
    dact, c_rows, r_rows, ci_rows, ri_rows, kk,
    dA, ain, run, vw, dye,
):
    T = act.shape[1]
    CH = T // Q
    C = dyT.shape[0]
    HH = C // PS
    zeros = jnp.zeros((64, Q), BF)

    @pl.loop(0, CH)
    def _(c):
        l = lanes(c)
        ecue = jnp.exp(rows[CUE : CUE + 24, l])
        for h in range(HH):
            dy = dyT[64 * h : 64 * h + 64, l]
            dye[64 * h : 64 * h + 64, 0:Q] = (dy * ecue[h : h + 1]).astype(BF)
            dye[64 * h : 64 * h + 64, Q : 2 * Q] = (dy * ecue[HH + h : HH + h + 1]).astype(BF)
        both = jnp.concatenate(
            [
                jnp.concatenate([cs[0:64, l], zeros], 1),
                jnp.concatenate([zeros, cs[64:128, l]], 1),
            ],
            0,
        )
        dA[c] = mm(dye[...], both, NT)

    run[...] = jnp.zeros_like(run)
    low = iota2((64, Q), 1) < 64
    low_h = iota2((HH, Q), 1) < 64

    @pl.loop(0, CH)
    def _(i):
        f = CH - 1 - i
        d = jnp.where(low_h, dec[f][0:HH], dec[i][HH : 2 * HH])
        for h in range(HH):
            r = slice(64 * h, 64 * h + 64)
            now = run[r, :]
            ain[i, r, :] = now.astype(BF)
            flow = jnp.sum(now * sin[f, r, :].astype(F32), 0, keepdims=True) * d[h : h + 1]
            kk[i, h : h + 1, :] = flow
            run[r, :] = now * d[h : h + 1] + jnp.where(low, dA[f, r, :], dA[i, r, :])

    before = iota2((Q, Q), 1) < iota2((Q, Q), 0)
    after = iota2((Q, Q), 1) > iota2((Q, Q), 0)
    left = iota2((Q, Q), 1) < 64
    top = iota2((Q, Q), 0) < 64
    lane = iota2((Q, Q), 1)

    @pl.loop(0, CH)
    def _(c):
        l = lanes(c)
        bf = act[C : C + 64, l]
        bb = act[C + 128 : C + 192, l]
        cf = cs[0:64, l]
        cb = cs[64:128, l]
        gf = mm(cf.astype(F32).T.astype(BF), bf)
        gb = mm(cb.astype(F32).T.astype(BF), bb)
        g = jnp.where(before, gf, jnp.where(after, gb, 0.0))
        ecue = jnp.exp(rows[CUE : CUE + 24, l])
        w = jnp.exp(
            jnp.where(
                iota2((24, Q), 0) < HH,
                rows[CUM : CUM + 24, l][:, Q - 1 : Q],
                rows[CUM : CUM + 24, l][:, 0:1],
            )
            - rows[CUM : CUM + 24, l]
        ) * rows[DT : DT + 24, l]
        for h in range(HH):
            r = slice(64 * h, 64 * h + 64)
            dy = dyT[r, l]
            v = act[r, l].astype(F32)
            dye[r, 0:Q] = (dy * ecue[h : h + 1]).astype(BF)
            dye[r, Q : 2 * Q] = (dy * ecue[HH + h : HH + h + 1]).astype(BF)
            vw[r, 0:Q] = (v * w[h : h + 1]).astype(BF)
            vw[r, Q : 2 * Q] = (v * w[HH + h : HH + h + 1]).astype(BF)
        zc = jnp.zeros((64, Q), BF)
        sf = sin[c]
        sb = sin[CH - 1 - c]
        af = ain[CH - 1 - c]
        ab = ain[c]
        yf = mm(sf, jnp.concatenate([cf, zc], 0))
        yb = mm(sb, jnp.concatenate([zc, cb], 0))
        vf = mm(af, jnp.concatenate([bf, zc], 0))
        vb = mm(ab, jnp.concatenate([zc, bb], 0))
        dcf = mm(sf.astype(F32).T.astype(BF)[0:64], dye[:, 0:Q])
        dcb = mm(sb.astype(F32).T.astype(BF)[64:128], dye[:, Q : 2 * Q])
        dbf = mm(af.astype(F32).T.astype(BF)[0:64], vw[:, 0:Q])
        dbb = mm(ab.astype(F32).T.astype(BF)[64:128], vw[:, Q : 2 * Q])
        dg = jnp.zeros((Q, Q), F32)
        rc_cols = jnp.zeros((Q, Q), F32)
        for j in range(HH // 2):
            r2 = slice(128 * j, 128 * j + 128)
            v = act[r2, l]
            dy_f = dyT[r2, l]
            dyt = dy_f.T.astype(BF)
            dy = dy_f.astype(BF)
            zb = jnp.zeros_like(dyt)
            dm2 = mm(jnp.concatenate([jnp.where(left, dyt, zb), jnp.where(left, zb, dyt)], 0), v)
            ms = []
            for k in (0, 1):
                h = 2 * j + k
                e = e_in[c, h].astype(F32)
                x = e * dm2[Q * k : Q * k + Q]
                dg = dg + x
                t = x * g
                tf = jnp.where(before, t, 0.0)
                ms.append((e * g).astype(BF))
                c_all = jnp.sum(t, 0, keepdims=True)
                c_f = jnp.sum(tf, 0, keepdims=True)
                c_rows[h : h + 1, l] = c_f
                c_rows[HH + h : HH + h + 1, l] = c_all - c_f
                r_all = jnp.sum(t, 1, keepdims=True)
                r_f = jnp.sum(tf, 1, keepdims=True)
                rc_cols = jnp.where(lane == h, r_f, rc_cols)
                rc_cols = jnp.where(lane == HH + h, r_all - r_f, rc_cols)
            dv = mm(
                jnp.concatenate([jnp.where(top, dy, zb), jnp.where(top, zb, dy)], 1),
                jnp.concatenate(ms, 0),
            )
            for k in (0, 1):
                h = 2 * j + k
                r = slice(64 * h, 64 * h + 64)
                v1 = v[64 * k : 64 * k + 64].astype(F32)
                dy1 = dy_f[64 * k : 64 * k + 64]
                f_in = vf[r] * w[h : h + 1]
                b_in = vb[r] * w[HH + h : HH + h + 1]
                ci_rows[h : h + 1, l] = jnp.sum(f_in * v1, 0, keepdims=True)
                ci_rows[HH + h : HH + h + 1, l] = jnp.sum(b_in * v1, 0, keepdims=True)
                ri_rows[h : h + 1, l] = jnp.sum(yf[r] * dy1, 0, keepdims=True) * ecue[h : h + 1]
                ri_rows[HH + h : HH + h + 1, l] = (
                    jnp.sum(yb[r] * dy1, 0, keepdims=True) * ecue[HH + h : HH + h + 1]
                )
                dact[r, l] = dv[64 * k : 64 * k + 64] + f_in + b_in + cc[r, 5:6] * dy1
        r_rows[:, l] = rc_cols.T[0:24, :]
        dgf = jnp.where(before, dg, 0.0).astype(BF)
        dgb = jnp.where(after, dg, 0.0).astype(BF)
        dact[C : C + 64, l] = dbf + mm(cf, dgf)
        dact[C + 64 : C + 128, l] = dcf + mm(bf, dgf, NT)
        dact[C + 128 : C + 192, l] = dbb + mm(cb, dgb)
        dact[C + 192 : C + 256, l] = dcb + mm(bb, dgb, NT)

    dact[C + 64 : C + 128, :] = pltpu.roll(dact[C + 64 : C + 128, :], T - 1, 1)
    dact[C + 192 : C + 256, :] = pltpu.roll(dact[C + 192 : C + 256, :], 1, 1)


def weights_kernel(
    length, dact, c_rows, r_rows, ci_rows, ri_rows, kk, rows, u_in, pre_in, dgate, nT, wcat, cc, cd, rc, small,
    dproj, b0, b1, b2, b3,
    small_s, dla_s,
):
    T = dact.shape[1]
    CH = T // Q
    C = dgate.shape[0]
    HH = C // PS
    low_h = iota2((HH, Q), 1) < 64

    ii, jj = iota2((Q, Q), 0), iota2((Q, Q), 1)
    gt = (ii > jj).astype(F32)
    ge = (ii >= jj).astype(F32)
    lt = (ii < jj).astype(F32)
    le = (ii <= jj).astype(F32)
    first = iota2((24, Q), 0) < HH
    cat = lambda ref: jnp.concatenate([ref[:, c * Q : (c + 1) * Q] for c in range(CH)], 0)
    r_in, c_in, c_x, r_x = cat(r_rows), cat(c_rows), cat(ci_rows), cat(ri_rows)
    rt = r_in + r_x
    as_f = mm_hi(rt, gt) - mm_hi(c_in, ge) + mm_hi(c_x, lt)
    as_b = mm_hi(rt, lt) - mm_hi(c_in, le) + mm_hi(c_x, gt)
    for c in range(CH):
        k = slice(24 * c, 24 * c + 24)
        l = slice(Q * c, Q * c + Q)
        kf = jnp.sum(jnp.where(low_h, kk[CH - 1 - c], 0.0), 1, keepdims=True)
        kb = jnp.sum(jnp.where(low_h, 0.0, kk[c]), 1, keepdims=True)
        dla_s[0:HH, l] = as_f[k][0:HH] + kf
        dla_s[HH : 2 * HH, l] = as_b[k][HH : 2 * HH] + kb
    dla = dla_s[...]
    dt = rows[DT : DT + 24, :]
    rate = rc[:, 1:2]
    live = (iota2((1, T), 1) < length[0]).astype(F32)
    sig = jax.nn.sigmoid(rows[RAW : RAW + 24, :])
    direct = (c_rows[...] + ci_rows[...]) * jnp.where(dt > 0.0, sig / jnp.where(dt > 0.0, dt, 1.0), 0.0)
    draw = (direct + rate * dla * sig) * live
    g_bias = jnp.sum(draw, 1, keepdims=True)
    g_decay = jnp.sum(dla * dt, 1, keepdims=True) * rate
    dproj[0:C, :] = dgate[...]
    dproj[2 * C + 256 : 2 * C + 384, :] = jnp.concatenate([draw, jnp.zeros((104, T), F32)], 0).astype(BF)

    at = iota2((64, T), 1)
    lane64 = iota2((64, Q), 1)

    @pl.loop(0, (C + 256) // 64)
    def _(b):
        r = pl.ds(pl.multiple_of(b * 64, 64), 64)
        pre = pre_in[r, :].astype(F32)
        sg = jax.nn.sigmoid(pre)
        dp = dact[r, :] * (sg * (1.0 + pre * (1.0 - sg)))
        uu = u_in[r, :].astype(F32)
        col = cc[r, :]
        du = col[:, 3:4] * dp
        base = jnp.where(b < C // 64, 32, 42)
        out = jnp.where(lane64 == base + 4, jnp.sum(dp, 1, keepdims=True), 0.0)
        out = jnp.where(lane64 == base + 3, jnp.sum(dp * uu, 1, keepdims=True), out)
        for back in (1, 2, 3):
            shifted = jnp.where(at >= back, pltpu.roll(uu, back, 1), 0.0)
            out = jnp.where(lane64 == base + 3 - back, jnp.sum(dp * shifted, 1, keepdims=True), out)
            ahead = jnp.where(at < T - back, pltpu.roll(dp, T - back, 1), 0.0)
            du = du + col[:, 3 - back : 4 - back] * ahead
        small_s[r, :] = out
        dproj[pl.ds(pl.multiple_of(b * 64 + C, 64), 64), :] = du.astype(BF)

    head_lane = iota2((24, Q), 1)
    sm = small[...] + small_s[0:C, :]
    small_s[0:C, :] = sm
    small_s[0:24, :] += jnp.where(head_lane == 39, g_bias, jnp.where(head_lane == 40, g_decay, 0.0))
    small_s[0:256, :] += small_s[C : C + 256, :]
    place = lax.axis_index("dp") % 4
    share = b0.shape[0]
    W = 2 * C + 256
    for k, ref in enumerate((b0, b1, b2, b3)):
        r = pl.ds(pl.multiple_of((place ^ k) * share, share), share)
        n = nT[r, :]
        gv = mm(n, dproj[C : 2 * C, :], NT)
        gs = mm(n, dproj[2 * C : W, :], NT)
        gt = mm(n, dproj[W : W + Q, :], NT)
        wide = (
            jnp.sum(gv * wcat[r, C : 2 * C].astype(F32), 1, keepdims=True)
            + jnp.sum(gs * wcat[r, 2 * C : W].astype(F32), 1, keepdims=True)
            + jnp.sum(gt * wcat[r, W : W + Q].astype(F32), 1, keepdims=True)
        ) / cd[r, 0:1]
        ref[:, 0:C] = gv.astype(BF)
        extra = jnp.where(iota2((share, Q), 1) == 41, wide, 0.0)
        fine = gt + small_s[r, :] + extra
        upper = fine.astype(BF)
        ref[:, C : C + Q] = upper + pltpu.roll(fine - upper.astype(F32), 64, 1).astype(BF)
        ref[:, C + Q : C + Q + 256] = gs.astype(BF)


def through_kernel(wcat, dproj, xT, cd, dno, dnx, dots, dn_s):
    T = xT.shape[1]
    half = dno.shape[0]
    m = lax.axis_index("tensor")
    own = pl.multiple_of(m * half, half)
    other = pl.multiple_of((1 - m) * half, half)
    gain = cd[:, 0:1]

    @pl.loop(0, T // 256)
    def _(j):
        l = lanes(j, 256)
        dn = mm(wcat[...], dproj[:, l])
        dot = jnp.sum(dn * xT[:, l].astype(F32) * gain, 0, keepdims=True)
        dots[:, l] = jnp.broadcast_to(dot, (8, 256))
        dn_s[...] = dn
        dno[:, l] = dn_s[pl.ds(own, half), :].astype(BF)
        dnx[0:half, l] = dn_s[pl.ds(other, half), :].astype(BF)
        top_part = dot.astype(BF).astype(F32)
        row = iota2((16, 256), 0)
        dnx[half : half + 16, l] = jnp.where(
            row == 0, top_part, jnp.where(row == 1, dot - top_part, 0.0)
        ).astype(BF)


def last_kernel(dno, dnr, d0, xT, doT, rows, cd, out):
    T = xT.shape[1]
    half = dno.shape[0]
    own = pl.multiple_of(lax.axis_index("tensor") * half, half)
    gain = cd[pl.ds(own, half), 0:1]

    @pl.loop(0, T // Q)
    def _(c):
        l = lanes(c)
        inv = rows[INV : INV + 1, l]
        sent = dnr[half : half + 16, l].astype(F32)
        k3 = inv * inv * inv * (d0[0:1, l] + sent[0:1] + sent[1:2]) / D
        e2 = (dno[:, l].astype(F32) + dnr[0:half, l].astype(F32)) * gain
        x = xT[pl.ds(own, half), l].astype(F32)
        dx = inv * e2 - x * k3 + doT[pl.ds(own, half), l].astype(F32)
        out[l, :] = dx.T.astype(BF)


def unpack_kernel(g0, g1, g2, g3, gv, gt, gs, ng, cv, vb, cst, sb, dl, sk, og, bias, sm):
    share = g0.shape[0]
    C = gv.shape[1]
    HH = C // PS
    place = lax.axis_index("dp") % 4
    for k, ref in enumerate((g0, g1, g2, g3)):
        r = pl.ds(pl.multiple_of((place ^ k) * share, share), share)
        gv[r, :] = ref[:, 0:C].astype(F32)
        mid = ref[:, C : C + Q].astype(F32)
        mid = mid + pltpu.roll(mid, 64, 1)
        gt[r, :] = mid[:, 0 : 2 * HH]
        sm[r, :] = mid
        gs[r, :] = ref[:, C + Q : C + Q + 256].astype(F32)
    turned = sm[...].T
    ng[...] = turned[41]
    cv[...] = turned[32:36]
    vb[...] = turned[36]
    cst[...] = turned[42:46, 0:256]
    sb[...] = turned[46, 0:256]
    og[...] = turned[38]
    dl[...] = turned[40, 0:HH] + turned[40, HH : 2 * HH]
    bias[0:1, :] = turned[39:40, 0:HH]
    bias[1:2, :] = turned[39:40, HH : 2 * HH]
    pick = (iota2((C, HH), 0) // PS == iota2((C, HH), 1)).astype(F32)
    sk[...] = mm_hi(turned[32:40], pick)[5]


def call(body, outs, scratch, args, smem, name, us=1.0):
    specs = [
        pl.BlockSpec(memory_space=pltpu.SMEM if i < smem else pltpu.VMEM) for i in range(len(args))
    ]
    return pl.pallas_call(
        body,
        out_shape=[jax.ShapeDtypeStruct(s, d) for s, d in outs],
        in_specs=specs,
        out_specs=[pl.BlockSpec(memory_space=pltpu.VMEM) for _ in outs],
        scratch_shapes=[pltpu.VMEM(s, d) for s, d in scratch],
        compiler_params=pltpu.CompilerParams(vmem_limit_bytes=VMEM_LIMIT),
        cost_estimate=pl.CostEstimate(
            flops=int(us * 9e8), bytes_accessed=int(us * 3e6), transcendentals=0
        ),
        name=name,
    )(*args)


def swap(x):
    return lax.ppermute(x, "tensor", [(0, 1), (1, 0)])


def across(x, groups, bit):
    return lax.ppermute(x, "dp", [(i, i ^ bit) for i in range(groups)])


def phases_of(groups):
    found, weight = [], 1
    while weight < groups:
        members = min(4, groups // weight)
        found.append((weight, members))
        weight *= members
    return found


def send_round(blocks, groups, weight):
    return [blocks[0]] + [across(b, groups, k * weight) for k, b in enumerate(blocks) if k]


def resplit(x, at):
    value = x[:, at : at + 64] + x[:, at + 64 : at + 128]
    upper = lax.reduce_precision(value, 8, 7)
    return jnp.concatenate([x[:, :at], upper, value - upper, x[:, at + 128 :]], 1)


def split(x, rank, weight, members):
    rows = x.shape[0] // members
    place = (rank // weight) % members
    return [lax.dynamic_slice_in_dim(x, (place ^ k) * rows, rows, 0) for k in range(members)]


def assemble(got, rank, weight):
    members = len(got)
    place = (rank // weight) % members
    parts = []
    for i in range(members):
        now = got[i]
        for p in range(1, members):
            now = jnp.where(place == p, got[i ^ p], now)
        parts.append(now)
    return jnp.concatenate(parts, 0)


def on_device(
    hidden_in, teacher, loss_mask, lengths, dealing, norm_gain, w_gate, w_value, w_state, w_step,
    step_bias, conv_value, conv_vbias, conv_state, conv_sbias, decay_log, skip_gain, out_gain, w_out,
):
    groups = lax.axis_size("dp")
    rank = lax.axis_index("dp")
    member = lax.axis_index("tensor")
    seqs, local, _ = hidden_in.shape
    half = teacher.shape[2]
    T = local * groups
    C = w_gate.shape[1]
    HH = decay_log.shape[0]
    CH = T // Q

    [dealt] = call(deal_kernel, [((seqs, local, half), BF)], [], (dealing, hidden_in), 1, "deal", 3.0)
    xo = lax.all_to_all(dealt, "dp", split_axis=0, concat_axis=0, tiled=True).reshape(T, half)

    pos = rank * local + lax.broadcasted_iota(jnp.int32, (seqs, local), 1)
    marks = (loss_mask > 0) & (pos < lengths[:, None])
    total = jnp.broadcast_to(jnp.sum(marks.astype(F32)), (8, Q))
    for bit in range(groups.bit_length() - 1):
        total = total + across(total, groups, 1 << bit)
    scale = (T / total[0, 0:1]).astype(F32)
    goal = jnp.where(marks[:, :, None], teacher, jnp.asarray(NOMARK, BF))
    [goal] = call(deal_kernel, [((seqs, local, half), BF)], [], (dealing, goal), 1, "deal_goal", 2.0)
    length = lax.dynamic_slice_in_dim(lengths, dealing[rank], 1, 0)

    wcat = jnp.concatenate(
        [w_gate, w_value, w_state, w_step.reshape(D, 2 * HH), jnp.zeros((D, Q - 2 * HH), BF)], 1
    )
    wt = wcat.T
    wot = w_out.T
    zc = jnp.zeros((256,), F32)
    cc = jnp.concatenate(
        [
            jnp.concatenate([conv_value, conv_state], 1),
            jnp.concatenate([conv_vbias, conv_sbias])[None],
            jnp.concatenate([jnp.repeat(skip_gain, PS), zc])[None],
            jnp.concatenate([out_gain, zc])[None],
            jnp.zeros((1, C + 256), F32),
        ],
        0,
    ).T
    cd = norm_gain[:, None]
    rate = -jnp.exp(decay_log)
    rc = jnp.stack([step_bias.reshape(-1), jnp.concatenate([rate, rate])], 1)

    xo, goal, wcat, wt, wot, cc, cd, rc, scale, length = lax.optimization_barrier(
        (xo, goal, wcat, wt, wot, cc, cd, rc, scale, length)
    )
    xs = swap(xo)
    to = lax.all_to_all(goal, "dp", split_axis=0, concat_axis=0, tiled=True).reshape(T, half)
    ts = swap(to)

    full = lambda n: ((n, T), BF)
    fullf = lambda n: ((n, T), F32)
    xT, nT, rows, dec, gate, u, pre, act, cs, e, mixed, sin, p_send, p0 = call(
        forward_kernel,
        [
            full(D), full(D), fullf(128), ((CH, 24, Q), F32), fullf(C), full(C + 256), full(C + 256),
            full(C + 256), full(128), ((CH, HH, Q, Q), BF), fullf(C), ((CH, C, Q), BF), full(D + 16),
            fullf(D + 8),
        ],
        [
            ((C + 256, T), F32), ((32, T), F32), ((24, T), F32), ((CH, C, Q), F32), ((C, Q), F32),
            ((C, 2 * Q), BF), ((C, T), BF),
        ],
        (length, xo, xs, wt, wot, cc, cd, rc),
        1,
        "forward",
        37.0,
    )
    p1 = swap(p_send)
    lo, doT, dyT, dgate, small, *mids = call(
        middle_kernel,
        [((T, half), BF), full(D), fullf(C), full(C), ((C, Q), F32)] + [((D // 4, D + C), BF)] * 4,
        [
            ((D, Q), F32), ((D, Q), F32), ((C, T), BF), ((C, 256), F32), ((8, T), F32), ((C, Q), F32),
            ((C, Q), F32), ((8, T), F32),
        ],
        (scale, p0, p1, xT, to, ts, w_out, w_gate, nT, gate, mixed, act, cc, cd),
        1,
        "middle",
        20.0,
    )
    phases = phases_of(groups)
    got_m = send_round(mids, groups, 1)
    rowsf = ((24, T), F32)
    dact, c_rows, r_rows, ci_rows, ri_rows, kk = call(
        backward_kernel,
        [fullf(C + 256), rowsf, rowsf, rowsf, rowsf, ((CH, HH, Q), F32)],
        [((CH, C, Q), F32), ((CH, C, Q), BF), ((C, Q), F32), ((C, 2 * Q), BF), ((C, 2 * Q), BF)],
        (act, cs, rows, dec, e, sin, dyT, cc),
        0,
        "backward",
        30.0,
    )
    now_m = sum(g.astype(F32) for g in got_m)
    now_m, dact = lax.optimization_barrier((now_m, dact))
    for weight, members in phases[1:]:
        blocks = split(now_m, rank, weight, members)
        got_m = send_round([b if k == 0 else b.astype(BF) for k, b in enumerate(blocks)], groups, weight)
        now_m = sum(g.astype(F32) for g in got_m)
    width = C + Q + 256
    dproj, b0, b1, b2, b3 = call(
        weights_kernel,
        [full(2 * C + 384)] + [((D // 4, width), BF)] * 4,
        [((C + 256, Q), F32), rowsf],
        (length, dact, c_rows, r_rows, ci_rows, ri_rows, kk, rows, u, pre, dgate, nT, wcat, cc, cd, rc, small),
        1,
        "weights",
        16.0,
    )
    gathered = lax.all_gather(now_m.astype(BF), "dp", axis=0, tiled=False)
    digits = [members for _, members in phases]
    count = len(digits)
    gathered = gathered.reshape(*reversed(digits), -1, D + C)
    order = tuple(reversed(range(count))) + (count, count + 1)
    gathered = gathered.transpose(order).reshape(D, D + C).astype(F32)
    got = send_round([b0, b1, b2, b3], groups, 1)
    dno, dnx, dots = call(
        through_kernel,
        [full(half), full(half + 16), ((8, T), F32)],
        [((D, 256), F32)],
        (wcat, dproj, xT, cd),
        0,
        "through",
        6.0,
    )
    dnr = swap(dnx)
    [dx] = call(
        last_kernel, [((T, half), BF)], [], (dno, dnr, dots, xT, doT, rows, cd), 0, "last", 5.0
    )
    dx, *got = lax.optimization_barrier((dx, *got))
    back = lax.all_to_all(dx.reshape(seqs, local, half), "dp", split_axis=0, concat_axis=0, tiled=True)
    [grad_in] = call(undeal_kernel, [((seqs, local, half), BF)], [], (dealing, back), 1, "undeal", 2.0)

    now = resplit(sum(g.astype(F32) for g in got), C)
    for weight, members in phases[1:]:
        blocks = split(now, rank, weight, members)
        got = send_round([b if k == 0 else b.astype(BF) for k, b in enumerate(blocks)], groups, weight)
        now = resplit(sum(g.astype(F32) for g in got), C)
    lane = lax.broadcasted_iota(jnp.int32, (1, Q + 256), 1)
    both = (lane >= Q) | ((lane % 64 >= 41) & (lane % 64 < 47))
    tail = now[:, C:]
    tail = resplit(tail + jnp.where(both, swap(tail.astype(BF)).astype(F32), 0.0), 0)
    now = jnp.concatenate([now[:, :C], tail], 1).astype(BF)
    for weight, members in reversed(phases[1:]):
        now = assemble(send_round([now] * members, groups, weight), rank, weight)
    got = send_round([now] * 4, groups, 1)
    gv, gt, gs, ng, cv, vb, cst, sb, dl, sk, og, bias = call(
        unpack_kernel,
        [
            ((D, C), F32), ((D, 2 * HH), F32), ((D, 256), F32), ((D,), F32), ((4, C), F32), ((C,), F32),
            ((4, 256), F32), ((256,), F32), ((HH,), F32), ((HH,), F32), ((C,), F32), ((2, HH), F32),
        ],
        [((D, Q), F32)],
        got,
        0,
        "unpack",
        3.0,
    )
    return (
        lo[None], grad_in, ng, gathered[:, D:], gv, gs, gt.reshape(D, 2, HH), bias, cv, vb, cst,
        sb, dl, sk, og, gathered[:, :D],
    )


def solution(mesh):
    dp, tp = "dp", "tensor"
    return jax.shard_map(
        on_device,
        mesh=mesh,
        in_specs=(
            P(None, dp, None), P(None, dp, tp), P(None, dp), P(), P(), P(), P(None, tp), P(None, tp), P(),
            P(None, None, tp), P(None, tp), P(None, tp), P(tp), P(), P(), P(tp), P(tp), P(tp), P(tp, None),
        ),
        out_specs=(
            P(dp, None, tp), P(None, dp, tp), P(), P(None, tp), P(None, tp), P(), P(None, None, tp),
            P(None, tp), P(None, tp), P(tp), P(), P(), P(tp), P(tp), P(tp), P(tp, None),
        ),
        check_vma=False,
    )
```

```python
import functools
import inspect

import jax
import jax.numpy as jnp
from jax import lax
from jax.experimental import pallas as pl
from jax.experimental.pallas import tpu as pltpu
from jax.sharding import PartitionSpec as P

D = 768
INNER = 1536
PS = 64
N = 64
Q = 128
EPS = 1e-5
NOMARK = 256.0
BF = jnp.bfloat16
F32 = jnp.float32
HI = lax.Precision.HIGHEST


def pairs(count, before=None, after=None):
    def run(body):
        @pl.loop(0, count // 2)
        def _(k):
            if before:
                before(k)
            body(2 * k)
            body(2 * k + 1)
            if after:
                after(k)

    return run


ROWS = 32

NN = (((1,), (0,)), ((), ()))
NT = (((1,), (1,)), ((), ()))


def mm(a, b, dims=NN):
    return lax.dot_general(a, b, dims, preferred_element_type=F32)


def mm_hi(a, b):
    return lax.dot_general(a, b, NN, precision=HI, preferred_element_type=F32)


def lanes(c, width=Q):
    return pl.ds(pl.multiple_of(c * width, width), width)


def iota2(shape, dim):
    return lax.broadcasted_iota(jnp.int32, shape, dim)


def log1p_exp(z):
    w = 1.0 + z
    return jnp.where(w == 1.0, z, jnp.log(w) * (z / jnp.where(w == 1.0, 1.0, w - 1.0)))


RAW, DT, CUM, CUE, ROWV = 0, 24, 48, 72, 96


def deal_kernel(io, dealing, src, dst):
    count, _, width = dst.shape
    if src.shape[2] == width:
        col = pl.ds(0, width)
    else:
        col = pl.ds(pl.multiple_of(lax.axis_index("tensor") * width, width), width)

    @pl.loop(0, count)
    def _(j):
        dst[j] = src[dealing[j], :, col]


def prepare_kernel(io, wg, wv, ws, wst, wo, ng, wcat, wt, wot, cd):
    C = wg.shape[1]
    W = 2 * C + 256
    wcat[:, 0:C] = wg[...]
    wcat[:, C : 2 * C] = wv[...]
    wcat[:, 2 * C : W] = ws[...]
    wcat[:, W : W + Q] = jnp.concatenate([wst[...], jnp.zeros((D, Q - wst.shape[1]), BF)], 1)
    io.put("wcat")

    @pl.loop(0, (W + Q) // Q)
    def _(c):
        wt[lanes(c), :] = wcat[:, lanes(c)].astype(F32).T.astype(BF)

    io.put("wt")

    @pl.loop(0, D // Q)
    def _(c):
        wot[lanes(c), :] = wo[:, lanes(c)].astype(F32).T.astype(BF)

    cd[...] = jnp.broadcast_to(ng[...], (8, D)).T


def forward_kernel(
    io, length, xo, xs, wt, wot, cc, cd, rc,
    xT, nT, rows, dec, gate, uO, preO, act, cs, eO, mixed, sin, pO, inv_o,
    u_s, raw_s, w_s, dS, run, vw, bu,
):
    T = xo.shape[0]
    CH = T // Q
    C = gate.shape[0]
    HH = C // PS
    half = xo.shape[1]
    m = lax.axis_index("tensor")
    own = pl.multiple_of(m * half, half)
    other = pl.multiple_of((1 - m) * half, half)

    def arrive(k):
        io.need("xo", k)
        io.need("xs", k)

    @pairs(CH, arrive)
    def _(c):
        l = lanes(c)
        xT[pl.ds(own, half), l] = xo[l, :].astype(F32).T.astype(BF)
        xT[pl.ds(other, half), l] = xs[l, :].astype(F32).T.astype(BF)
        x = xT[:, l].astype(F32)
        inv = lax.rsqrt(jnp.sum(x * x, 0, keepdims=True) / D + EPS)
        inv_o[:, l] = jnp.broadcast_to(inv, (8, Q))
        nT[:, l] = (x * inv * cd[:, 0:1]).astype(BF)

    io.put("xT")
    io.put("nT")
    io.need("wt")

    @pl.loop(0, T // 256, unroll=2)
    def _(j):
        l = lanes(j, 256)
        n = nT[:, l]
        gate[:, l] = mm(wt[0:C, :], n)
        u_s[:, l] = mm(wt[C : 2 * C + 256, :], n)
        raw_s[:, l] = mm(wt[2 * C + 256 : 2 * C + 288, :], n)

    io.put("gate")

    raw = raw_s[0:24, :] + rc[:, 0:1]
    live = (iota2((1, T), 1) < length[0]).astype(F32)
    dt = (jnp.maximum(raw, 0.0) + log1p_exp(jnp.exp(-jnp.abs(raw)))) * live
    la = dt * rc[:, 1:2]
    rows[RAW : RAW + 24, :] = raw
    rows[DT : DT + 24, :] = dt
    upper = (iota2((Q, Q), 0) <= iota2((Q, Q), 1)).astype(F32)
    lower = (iota2((Q, Q), 0) >= iota2((Q, Q), 1)).astype(F32)
    stacked = jnp.concatenate([la[:, c * Q : (c + 1) * Q] for c in range(CH)], 0)
    cum_f = mm_hi(stacked, upper)
    cum_b = mm_hi(stacked, lower)
    first = iota2((24, Q), 0) < HH
    for c in range(CH):
        r = slice(24 * c, 24 * c + 24)
        k = slice(Q * c, Q * c + Q)
        cum = jnp.where(first, cum_f[r], cum_b[r])
        dtc = dt[:, k]
        rows[CUM : CUM + 24, k] = cum
        rows[CUE : CUE + 24, k] = cum - la[:, k]
        rows[ROWV : ROWV + 24, k] = jnp.where(
            dtc > 0.0, cum - jnp.log(jnp.where(dtc > 0.0, dtc, 1.0)), 1e30
        )
        tot = jnp.broadcast_to(jnp.sum(la[:, k], 1, keepdims=True), (24, Q))
        dec[c] = jnp.exp(tot)
        w_s[:, k] = jnp.exp(tot - cum) * dtc

    io.put("rows")
    io.put("dec")
    io.need("cc")

    at = iota2((ROWS, Q), 1)

    @pl.loop(0, u_s.shape[0] // ROWS, unroll=2)
    def _(b):
        r = pl.ds(pl.multiple_of(b * ROWS, ROWS), ROWS)
        col = cc[r, :]
        ks = [jnp.broadcast_to(col[:, k : k + 1], (ROWS, Q)) for k in range(5)]
        earlier = [jnp.zeros((ROWS, Q), F32)] * 4
        for c in range(CH):
            l = slice(c * Q, c * Q + Q)
            uu = u_s[r, l]
            pre = ks[4] + ks[3] * uu
            for back in (1, 2, 3):
                moved = pltpu.roll(uu, back, 1)
                pre = pre + ks[3 - back] * jnp.where(at >= back, moved, earlier[back])
                earlier[back] = moved
            uO[r, l] = uu.astype(BF)
            preO[r, l] = pre.astype(BF)
            act[r, l] = (pre * jax.nn.sigmoid(pre)).astype(BF)

    cs[0:64, :] = pltpu.roll(act[C + 64 : C + 128, :].astype(F32), 1, 1).astype(BF)
    cs[64:128, :] = pltpu.roll(act[C + 192 : C + 256, :].astype(F32), T - 1, 1).astype(BF)

    io.put("uO")
    io.put("preO")
    io.put("act")
    io.put("cs")

    zeros = jnp.zeros((64, Q), BF)

    @pairs(CH)
    def _(c):
        l = lanes(c)
        for h in range(HH):
            v = act[64 * h : 64 * h + 64, l].astype(F32)
            vw[64 * h : 64 * h + 64, 0:Q] = (v * w_s[h : h + 1, l]).astype(BF)
            vw[64 * h : 64 * h + 64, Q : 2 * Q] = (v * w_s[HH + h : HH + h + 1, l]).astype(BF)
        both = jnp.concatenate(
            [
                jnp.concatenate([act[C : C + 64, l], zeros], 1),
                jnp.concatenate([zeros, act[C + 128 : C + 192, l]], 1),
            ],
            0,
        )
        dS[c] = mm(vw[...], both, NT)

    run[...] = jnp.zeros_like(run)
    low = iota2((64, Q), 1) < 64
    low_h = iota2((HH, Q), 1) < 64

    @pairs(CH)
    def _(i):
        d = jnp.where(low_h, dec[i][0:HH], dec[CH - 1 - i][HH : 2 * HH])
        for h in range(HH):
            r = slice(64 * h, 64 * h + 64)
            now = run[r, :]
            sin[i, r, :] = now.astype(BF)
            run[r, :] = now * d[h : h + 1] + jnp.where(low, dS[i, r, :], dS[CH - 1 - i, r, :])

    io.put("sin")

    before = iota2((Q, Q), 1) < iota2((Q, Q), 0)
    after = iota2((Q, Q), 1) > iota2((Q, Q), 0)
    top = iota2((Q, Q), 0) < 64

    def leave(k):
        io.put("eO", k)
        io.put("mixed", k)

    @pairs(CH, after=leave)
    def _(c):
        l = lanes(c)
        bf = act[C : C + 64, l]
        bb = act[C + 128 : C + 192, l]
        cf = cs[0:64, l]
        cb = cs[64:128, l]
        gf = mm(cf.astype(F32).T.astype(BF), bf)
        gb = mm(cb.astype(F32).T.astype(BF), bb)
        g = jnp.where(before, gf, jnp.where(after, gb, 0.0))
        cue = rows[CUE : CUE + 24, l]
        cols = jnp.concatenate([cue, jnp.zeros((Q - 24, Q), F32)], 0).T
        ecue = jnp.exp(cue)
        zc = jnp.zeros((64, Q), BF)
        yf = mm(sin[c], jnp.concatenate([cf, zc], 0))
        yb = mm(sin[CH - 1 - c], jnp.concatenate([zc, cb], 0))
        total = jnp.zeros((1, Q), F32)
        for j in range(HH // 2):
            ms = []
            for h in (2 * j, 2 * j + 1):
                gap = jnp.where(
                    before,
                    cols[:, h : h + 1] - rows[ROWV + h : ROWV + h + 1, l],
                    cols[:, HH + h : HH + h + 1] - rows[ROWV + HH + h : ROWV + HH + h + 1, l],
                )
                e = jnp.exp(jnp.minimum(gap, 30.0))
                eO[c, h] = e.astype(BF)
                ms.append((e * g).astype(BF))
            v = act[128 * j : 128 * j + 128, l]
            vz = jnp.zeros_like(v)
            pair = jnp.concatenate([jnp.where(top, v, vz), jnp.where(top, vz, v)], 1)
            y = mm(pair, jnp.concatenate(ms, 1), NT)
            for k in (0, 1):
                h = 2 * j + k
                r = slice(64 * h, 64 * h + 64)
                mix = (
                    y[64 * k : 64 * k + 64]
                    + ecue[h : h + 1] * yf[r]
                    + ecue[HH + h : HH + h + 1] * yb[r]
                    + cc[r, 5:6] * v[64 * k : 64 * k + 64].astype(F32)
                )
                mixed[r, l] = mix
                gt = gate[r, l]
                gated = mix * (gt * jax.nn.sigmoid(gt))
                total = total + jnp.sum(gated * gated, 0, keepdims=True)
                bu[r, l] = (gated * cc[r, 6:7]).astype(BF)
        top_part = total.astype(BF).astype(F32)
        pO[D : D + 16, l] = jnp.where(
            iota2((16, Q), 0) == 0, top_part, jnp.where(iota2((16, Q), 0) == 1, total - top_part, 0.0)
        ).astype(BF)

    io.need("wot")

    @pl.loop(0, T // 256)
    def _(j):
        l = lanes(j, 256)
        pO[0:D, l] = mm(wot[...], bu[:, l]).astype(BF)
        io.put("pO", j)


def middle_kernel(
    io, p0, p1, xT, to, ts, wo, nT, gate, mixed, cc,
    lo, doh, dyT, dgate, small, m0, m1, m2, m3,
    res_s, tea_s, branch, dbr, dot_s, acc_g, q_s, doT,
):
    T = to.shape[0]
    CH = T // Q
    C = gate.shape[0]
    half = to.shape[1]
    m = lax.axis_index("tensor")
    own = pl.multiple_of(m * half, half)
    other = pl.multiple_of((1 - m) * half, half)

    def arrive(k):
        for n in ("p0", "p1", "xT", "to", "ts"):
            io.need(n, k)

    @pairs(CH, arrive)
    def _(c):
        l = lanes(c)
        tea_s[pl.ds(own, half), :] = to[l, :].astype(F32).T
        tea_s[pl.ds(other, half), :] = ts[l, :].astype(F32).T
        pt = p0[0:D, l].astype(F32) + p1[0:D, l].astype(F32)
        sums = p0[D : D + 16, l].astype(F32) + p1[D : D + 16, l].astype(F32)
        q = lax.rsqrt((sums[0:1] + sums[1:2]) / INNER + EPS)
        q_s[:, l] = jnp.broadcast_to(q, (8, Q))
        res = xT[:, l].astype(F32) + q * pt
        res_s[...] = res
        tea = tea_s[...]
        do = jnp.where(tea < 0.5 * NOMARK, res - tea, 0.0).astype(BF)
        doT[:, l] = do
        dot_s[:, l] = jnp.broadcast_to(jnp.sum(do.astype(F32) * pt, 0, keepdims=True), (8, Q))
        lo[l, :] = res_s[pl.ds(own, half), :].T.astype(BF)
        doh[:, l] = doT[pl.ds(own, half), l]

    io.put("doh")
    io.put("lo")
    acc_g[...] = jnp.zeros_like(acc_g)

    for n in ("wo", "cc"):
        io.need(n)

    @pl.loop(0, T // 256)
    def _(j):
        l = lanes(j, 256)
        io.need("gate", j)
        io.need("mixed", j)
        dbr[...] = mm(wo[...], doT[:, l])
        q = q_s[0:1, l]
        q3 = q * q * q * dot_s[0:1, l] / INNER

        @pl.loop(0, C // 64, unroll=2)
        def _(b):
            r = pl.ds(pl.multiple_of(b * 64, 64), 64)
            gain = jnp.broadcast_to(cc[r, 6:7], (64, Q))
            acc = acc_g[r, :]
            for t in (0, 1):
                k = slice(t * Q, t * Q + Q)
                l1 = pl.ds(pl.multiple_of(j * 256 + t * Q, Q), Q)
                d = dbr[r, k]
                g = gate[r, l1]
                mix = mixed[r, l1]
                sg = jax.nn.sigmoid(g)
                si = g * sg
                gated = mix * si
                gq = gated * q[:, k]
                branch[r, l1] = (gq * gain).astype(BF)
                acc = acc + d * gq
                dgt = q[:, k] * (d * gain) - gated * q3[:, k]
                dyT[r, l1] = (dgt * si).astype(BF)
                dgate[r, l1] = (dgt * mix * (sg * (1.0 + g * (1.0 - sg)))).astype(BF)
            acc_g[r, :] = acc

        io.put("dyT", j)

    io.put("dgate")
    io.need("nT")
    place = lax.axis_index("dp") % 4
    share = m0.shape[0]
    for k, ref in enumerate((m0, m1, m2, m3)):
        r = pl.ds(pl.multiple_of((place ^ k) * share, share), share)
        ref[:, 0:D] = mm(branch[r, :], doT[...], NT).astype(BF)
        ref[:, D : D + C] = mm(nT[r, :], dgate[...], NT).astype(BF)
        io.put("m%d" % k)
    small[...] = jnp.where(iota2((C, Q), 1) == 38, jnp.sum(acc_g[...], 1, keepdims=True), 0.0)


def backward_kernel(
    io, length, count, act, cs, rows, dec, e_in, sin, dyT, u_in, pre_in, dgate, nT, wcat, cc, cd, rc, small,
    b0, b1, b2, b3, dno, dnx, dots,
    acc, sk_rows, dact, c_rows, r_rows, ci_rows, ri_rows, kk, dA, ain, run, vw, dye, small_s, dla_s, sums, dproj, dn_s,
):
    T = act.shape[1]
    CH = T // Q
    C = dyT.shape[0]
    HH = C // PS
    zeros = jnp.zeros((64, Q), BF)

    io.need("rows")
    io.need("cs")

    @pairs(CH, lambda k: io.need("dyT", k))
    def _(c):
        l = lanes(c)
        ecue = jnp.exp(rows[CUE : CUE + 24, l])
        for h in range(HH):
            dy = dyT[64 * h : 64 * h + 64, l].astype(F32)
            dye[64 * h : 64 * h + 64, 0:Q] = (dy * ecue[h : h + 1]).astype(BF)
            dye[64 * h : 64 * h + 64, Q : 2 * Q] = (dy * ecue[HH + h : HH + h + 1]).astype(BF)
        both = jnp.concatenate(
            [
                jnp.concatenate([cs[0:64, l], zeros], 1),
                jnp.concatenate([zeros, cs[64:128, l]], 1),
            ],
            0,
        )
        dA[c] = mm(dye[...], both, NT)

    io.need("dec")
    io.need("sin")
    run[...] = jnp.zeros_like(run)
    low = iota2((64, Q), 1) < 64
    low_h = iota2((HH, Q), 1) < 64

    @pl.loop(0, CH)
    def _(i):
        f = CH - 1 - i
        d = jnp.where(low_h, dec[f][0:HH], dec[i][HH : 2 * HH])
        for h in range(HH):
            r = slice(64 * h, 64 * h + 64)
            now = run[r, :]
            ain[i, r, :] = now.astype(BF)
            flow = jnp.sum(now * sin[f, r, :].astype(F32), 0, keepdims=True) * d[h : h + 1]
            kk[i, h : h + 1, :] = flow
            run[r, :] = now * d[h : h + 1] + jnp.where(low, dA[f, r, :], dA[i, r, :])

    io.need("act")
    io.need("cc")
    sk_rows[...] = jnp.zeros_like(sk_rows)
    before = iota2((Q, Q), 1) < iota2((Q, Q), 0)
    after = iota2((Q, Q), 1) > iota2((Q, Q), 0)
    left = iota2((Q, Q), 1) < 64
    top = iota2((Q, Q), 0) < 64
    lane = iota2((Q, Q), 1)

    @pl.loop(0, CH)
    def _(c):
        l = lanes(c)

        @pl.when(c % 2 == 0)
        def _():
            io.need("e_in", c // 2)

        bf = act[C : C + 64, l]
        bb = act[C + 128 : C + 192, l]
        cf = cs[0:64, l]
        cb = cs[64:128, l]
        gf = mm(cf.astype(F32).T.astype(BF), bf)
        gb = mm(cb.astype(F32).T.astype(BF), bb)
        g = jnp.where(before, gf, jnp.where(after, gb, 0.0))
        ecue = jnp.exp(rows[CUE : CUE + 24, l])
        w = jnp.exp(
            jnp.where(
                iota2((24, Q), 0) < HH,
                rows[CUM : CUM + 24, l][:, Q - 1 : Q],
                rows[CUM : CUM + 24, l][:, 0:1],
            )
            - rows[CUM : CUM + 24, l]
        ) * rows[DT : DT + 24, l]
        for h in range(HH):
            r = slice(64 * h, 64 * h + 64)
            dy = dyT[r, l].astype(F32)
            v = act[r, l].astype(F32)
            dye[r, 0:Q] = (dy * ecue[h : h + 1]).astype(BF)
            dye[r, Q : 2 * Q] = (dy * ecue[HH + h : HH + h + 1]).astype(BF)
            vw[r, 0:Q] = (v * w[h : h + 1]).astype(BF)
            vw[r, Q : 2 * Q] = (v * w[HH + h : HH + h + 1]).astype(BF)
        zc = jnp.zeros((64, Q), BF)
        sf = sin[c]
        sb = sin[CH - 1 - c]
        af = ain[CH - 1 - c]
        ab = ain[c]
        yf = mm(sf, jnp.concatenate([cf, zc], 0))
        yb = mm(sb, jnp.concatenate([zc, cb], 0))
        vf = mm(af, jnp.concatenate([bf, zc], 0))
        vb = mm(ab, jnp.concatenate([zc, bb], 0))
        dcf = mm(sf.astype(F32).T.astype(BF)[0:64], dye[:, 0:Q])
        dcb = mm(sb.astype(F32).T.astype(BF)[64:128], dye[:, Q : 2 * Q])
        dbf = mm(af.astype(F32).T.astype(BF)[0:64], vw[:, 0:Q])
        dbb = mm(ab.astype(F32).T.astype(BF)[64:128], vw[:, Q : 2 * Q])
        dg = jnp.zeros((Q, Q), F32)
        rc_cols = jnp.zeros((Q, Q), F32)
        for j in range(HH // 2):
            r2 = slice(128 * j, 128 * j + 128)
            v = act[r2, l]
            dy = dyT[r2, l]
            dy_f = dy.astype(F32)
            dyt = dy_f.T.astype(BF)
            zb = jnp.zeros_like(dyt)
            dm2 = mm(jnp.concatenate([jnp.where(left, dyt, zb), jnp.where(left, zb, dyt)], 0), v)
            ms = []
            for k in (0, 1):
                h = 2 * j + k
                e = e_in[c, h].astype(F32)
                x = e * dm2[Q * k : Q * k + Q]
                dg = dg + x
                t = x * g
                tf = jnp.where(before, t, 0.0)
                ms.append((e * g).astype(BF))
                c_all = jnp.sum(t, 0, keepdims=True)
                c_f = jnp.sum(tf, 0, keepdims=True)
                c_rows[h : h + 1, l] = c_f
                c_rows[HH + h : HH + h + 1, l] = c_all - c_f
                r_all = jnp.sum(t, 1, keepdims=True)
                r_f = jnp.sum(tf, 1, keepdims=True)
                rc_cols = jnp.where(lane == h, r_f, rc_cols)
                rc_cols = jnp.where(lane == HH + h, r_all - r_f, rc_cols)
            dv = mm(
                jnp.concatenate([jnp.where(top, dy, zb), jnp.where(top, zb, dy)], 1),
                jnp.concatenate(ms, 0),
            )
            for k in (0, 1):
                h = 2 * j + k
                r = slice(64 * h, 64 * h + 64)
                v1 = v[64 * k : 64 * k + 64].astype(F32)
                dy1 = dy_f[64 * k : 64 * k + 64]
                sk_rows[h : h + 1, l] = jnp.sum(v1 * dy1, 0, keepdims=True)
                f_in = vf[r] * w[h : h + 1]
                b_in = vb[r] * w[HH + h : HH + h + 1]
                ci_rows[h : h + 1, l] = jnp.sum(f_in * v1, 0, keepdims=True)
                ci_rows[HH + h : HH + h + 1, l] = jnp.sum(b_in * v1, 0, keepdims=True)
                ri_rows[h : h + 1, l] = jnp.sum(yf[r] * dy1, 0, keepdims=True) * ecue[h : h + 1]
                ri_rows[HH + h : HH + h + 1, l] = (
                    jnp.sum(yb[r] * dy1, 0, keepdims=True) * ecue[HH + h : HH + h + 1]
                )
                dact[r, l] = dv[64 * k : 64 * k + 64] + f_in + b_in + cc[r, 5:6] * dy1
        r_rows[:, l] = rc_cols.T[0:24, :]
        dgf = jnp.where(before, dg, 0.0).astype(BF)
        dgb = jnp.where(after, dg, 0.0).astype(BF)
        dact[C : C + 64, l] = dbf + mm(cf, dgf)
        dact[C + 64 : C + 128, l] = dcf + mm(bf, dgf, NT)
        dact[C + 128 : C + 192, l] = dbb + mm(cb, dgb)
        dact[C + 192 : C + 256, l] = dcb + mm(bb, dgb, NT)

    dact[C + 64 : C + 128, :] = pltpu.roll(dact[C + 64 : C + 128, :], T - 1, 1)
    dact[C + 192 : C + 256, :] = pltpu.roll(dact[C + 192 : C + 256, :], 1, 1)

    ii, jj = iota2((Q, Q), 0), iota2((Q, Q), 1)
    gt = (ii > jj).astype(F32)
    ge = (ii >= jj).astype(F32)
    lt = (ii < jj).astype(F32)
    le = (ii <= jj).astype(F32)
    first = iota2((24, Q), 0) < HH
    cat = lambda ref: jnp.concatenate([ref[:, c * Q : (c + 1) * Q] for c in range(CH)], 0)
    r_in, c_in, c_x, r_x = cat(r_rows), cat(c_rows), cat(ci_rows), cat(ri_rows)
    rt = r_in + r_x
    as_f = mm_hi(rt, gt) - mm_hi(c_in, ge) + mm_hi(c_x, lt)
    as_b = mm_hi(rt, lt) - mm_hi(c_in, le) + mm_hi(c_x, gt)
    for c in range(CH):
        k = slice(24 * c, 24 * c + 24)
        l = slice(Q * c, Q * c + Q)
        kf = jnp.sum(jnp.where(low_h, kk[CH - 1 - c], 0.0), 1, keepdims=True)
        kb = jnp.sum(jnp.where(low_h, 0.0, kk[c]), 1, keepdims=True)
        dla_s[0:HH, l] = as_f[k][0:HH] + kf
        dla_s[HH : 2 * HH, l] = as_b[k][HH : 2 * HH] + kb
    dla = dla_s[...]
    dt = rows[DT : DT + 24, :]
    rate = rc[:, 1:2]
    live = (iota2((1, T), 1) < length[0]).astype(F32)
    sig = jax.nn.sigmoid(rows[RAW : RAW + 24, :])
    direct = (c_rows[...] + ci_rows[...]) * jnp.where(dt > 0.0, sig / jnp.where(dt > 0.0, dt, 1.0), 0.0)
    draw = (direct + rate * dla * sig) * live
    g_bias = jnp.sum(draw, 1, keepdims=True)
    g_decay = jnp.sum(dla * dt, 1, keepdims=True) * rate
    g_skip = jnp.sum(sk_rows[...], 1, keepdims=True)
    io.need("dgate")
    dproj[0:C, :] = dgate[...]
    dproj[2 * C + 256 : 2 * C + 384, :] = jnp.concatenate([draw, jnp.zeros((104, T), F32)], 0).astype(BF)

    io.need("u_in")
    io.need("pre_in")
    at = iota2((ROWS, Q), 1)

    @pl.loop(0, (C + 256) // ROWS, unroll=2)
    def _(b):
        r = pl.ds(pl.multiple_of(b * ROWS, ROWS), ROWS)
        r_out = pl.ds(pl.multiple_of(b * ROWS + C, ROWS), ROWS)
        col = cc[r, :]
        ks = [jnp.broadcast_to(col[:, k : k + 1], (ROWS, Q)) for k in range(4)]
        later = [jnp.zeros((ROWS, Q), F32)] * 4
        totals = [jnp.zeros((ROWS, Q), F32)] * 5
        for c in reversed(range(CH)):
            l = slice(c * Q, c * Q + Q)
            pre = pre_in[r, l].astype(F32)
            sg = jax.nn.sigmoid(pre)
            dp = dact[r, l] * (sg * (1.0 + pre * (1.0 - sg)))
            uu = u_in[r, l].astype(F32)
            du = ks[3] * dp
            totals[4] = totals[4] + dp
            totals[3] = totals[3] + dp * uu
            for back in (1, 2, 3):
                moved = pltpu.roll(dp, Q - back, 1)
                ahead = jnp.where(at < Q - back, moved, later[back])
                later[back] = moved
                totals[3 - back] = totals[3 - back] + ahead * uu
                du = du + ks[3 - back] * ahead
            dproj[r_out, l] = du.astype(BF)
        for k in range(5):
            sums[r, k * Q : k * Q + Q] = totals[k]

    def lane_sums(part, first_lane):
        upper = part.astype(BF)
        lower = (part - upper.astype(F32)).astype(BF)
        pick = (iota2((5 * Q, Q), 0) // Q + first_lane == iota2((5 * Q, Q), 1)).astype(BF)
        return mm(upper, pick) + mm(lower, pick)

    io.need("small")
    small_s[0:C, :] = lane_sums(sums[0:C, :], 32) + small[...]
    small_s[0:256, :] += lane_sums(sums[C : C + 256, :], 42)
    head_lane = iota2((24, Q), 1)
    heads_part = jnp.where(head_lane == 39, g_bias, jnp.where(head_lane == 40, g_decay, 0.0))
    small_s[0:24, :] += jnp.where(head_lane == 37, g_skip, heads_part)
    counted = (iota2((8, Q), 1) == 48) & (iota2((8, Q), 0) == 0)
    for k in range(4):
        at_row = k * (D // 4)
        small_s[at_row : at_row + 8, :] += jnp.where(counted, count[0], 0.0)
    io.need("nT")
    io.need("wcat")
    io.need("cd")
    half = dno.shape[0]
    m = lax.axis_index("tensor")
    own = pl.multiple_of(m * half, half)
    other = pl.multiple_of((1 - m) * half, half)
    W = 2 * C + 256
    acc[...] = jnp.zeros_like(acc)

    @pl.loop(0, T // 256, unroll=2)
    def _(j):
        l = lanes(j, 256)
        dn = mm(wcat[...], dproj[:, l])
        dn_s[...] = dn * cd[:, 0:1]
        part = dn * nT[:, l].astype(F32)
        acc[...] += part[:, 0:Q] + part[:, Q : 2 * Q]
        dot = jnp.sum(part, 0, keepdims=True)
        dots[:, l] = jnp.broadcast_to(dot, (8, 256))
        dno[:, l] = dn_s[pl.ds(own, half), :].astype(BF)
        dnx[0:half, l] = dn_s[pl.ds(other, half), :].astype(BF)
        top_part = dot.astype(BF).astype(F32)
        row = iota2((16, 256), 0)
        dnx[half : half + 16, l] = jnp.where(
            row == 0, top_part, jnp.where(row == 1, dot - top_part, 0.0)
        ).astype(BF)
        io.put("dno", j)
        io.put("dnx", j)

    wide = jnp.sum(acc[...], 1, keepdims=True) / cd[:, 0:1]
    small_s[...] += jnp.where(iota2((D, Q), 1) == 41, wide, 0.0)
    place = lax.axis_index("dp") % 4
    share = b0.shape[0]
    for k, ref in enumerate((b0, b1, b2, b3)):
        r = pl.ds(pl.multiple_of((place ^ k) * share, share), share)
        n = nT[r, :]
        ref[:, 0:C] = mm(n, dproj[C : 2 * C, :], NT).astype(BF)
        ref[:, C + Q : C + Q + 256] = mm(n, dproj[2 * C : W, :], NT).astype(BF)
        fine = mm(n, dproj[W : W + Q, :], NT) + small_s[r, :]
        upper = fine.astype(BF)
        ref[:, C : C + Q] = upper + pltpu.roll(fine - upper.astype(F32), 64, 1).astype(BF)
        io.put("b%d" % k)


def last_kernel(io, dno, dnr, do_s, d0, inv_s, xT, out, x_s, sems):
    T = xT.shape[1]
    half = dno.shape[0]
    own = pl.multiple_of(lax.axis_index("tensor") * half, half)

    def copy(k):
        return pltpu.make_async_copy(xT.at[pl.ds(own, half), lanes(k, 512)], x_s.at[:, lanes(k, 512)], sems.at[k])

    for k in range(T // 512):
        copy(k).start()

    def arrive(k):
        copy(k).wait()
        for n in ("dno", "dnr", "do_s"):
            io.need(n, k)

    @pairs(T // 256, arrive, lambda k: io.put("out", k))
    def _(c):
        l = lanes(c, 256)
        inv = inv_s[0:1, l]
        sent = dnr[half : half + 16, l].astype(F32)
        k3 = inv * inv * (d0[0:1, l] + sent[0:1] + sent[1:2]) / D
        e2 = dno[:, l].astype(F32) + dnr[0:half, l].astype(F32)
        dx = inv * e2 - x_s[:, l].astype(F32) * k3 + do_s[:, l].astype(F32)
        out[l, :] = dx.astype(BF).T


def finish_first_kernel(io, own, h0, h1, h2, h3, wo, wg, *, full_len):
    share = h0.shape[0]
    C = wg.shape[1]
    place = lax.axis_index("dp") % 4
    mid = own[...].astype(F32)
    scale = full_len / (mid + pltpu.roll(mid, 64, 1))[0:1, 48:49]
    for k, ref in enumerate((h0, h1, h2, h3)):
        io.need("h%d" % k)
        r = pl.ds(pl.multiple_of((place ^ k) * share, share), share)
        wo[r, :] = ref[:, 0:D].astype(F32) * scale
        wg[r, :] = ref[:, D : D + C].astype(F32) * scale
    io.put("wo")
    io.put("wg")


def finish_kernel(
    io, dealing, g0, g1, g2, g3, back,
    gv, gt, gs, ng, cv, vb, cst, sb, dl, sk, og, bias, grad_in,
    sm, *, full_len
):
    share = g0.shape[0]
    C = gv.shape[1]
    HH = C // PS
    place = lax.axis_index("dp") % 4
    scale = None
    for k, ref in enumerate((g0, g1, g2, g3)):
        r = pl.ds(pl.multiple_of((place ^ k) * share, share), share)
        io.need("g%d" % k)
        mid = ref[:, C : C + Q].astype(F32)
        mid = mid + pltpu.roll(mid, 64, 1)
        scale = full_len / mid[0:1, 48:49]
        sm[r, :] = mid * scale
        gv[r, :] = ref[:, 0:C].astype(F32) * scale
        gs[r, :] = ref[:, C + Q : C + Q + 256].astype(F32) * scale
    io.put("gv")
    io.put("gs")
    io.need("back")

    @pl.loop(0, grad_in.shape[0])
    def _(k):
        grad_in[dealing[k]] = (back[k].astype(F32) * scale).astype(BF)

    io.put("grad_in")
    scaled = sm[...]
    gt[...] = scaled[:, 0 : 2 * HH]
    turned = scaled.T
    ng[...] = turned[41]
    cv[...] = turned[32:36]
    vb[...] = turned[36]
    cst[...] = turned[42:46, 0:256]
    sb[...] = turned[46, 0:256]
    og[...] = turned[38]
    dl[...] = turned[40, 0:HH] + turned[40, HH : 2 * HH]
    bias[0:1, :] = turned[39:40, 0:HH]
    bias[1:2, :] = turned[39:40, HH : 2 * HH]
    sk[...] = turned[37, 0:HH]


class Flow:
    def __init__(self, sems):
        self.sems, self.table, self.used = sems, {}, 0

    def add(self, name, src, dst, axis, count):
        self.table[name] = (src, dst, axis, count, self.used)
        self.used += count

    def copy(self, name, piece):
        src, dst, axis, count, first = self.table[name]
        if count > 1:
            width = src.shape[axis] // count
            at = pl.ds(pl.multiple_of(piece * width, width), width)
            where = (at,) if axis == 0 else (slice(None), at)
            src, dst = src.at[where], dst.at[where]
        return pltpu.make_async_copy(src, dst, self.sems.at[first + piece])

    def put(self, name, piece=0):
        self.copy(name, piece).start()

    def need(self, name, piece=0):
        self.copy(name, piece).wait()


def call(body, outs, scratch, args, smem, name, us=1.0, late=None, early=None, raw=(), limit=58, static=None):
    late, early = late or {}, early or {}
    kinds = [pltpu.VMEM(*x) if isinstance(x, tuple) else x for x in scratch]
    names = list(inspect.signature(body).parameters)[1:]
    body = functools.partial(body, **static) if static else body
    n_in, n_out, n_own = len(args), len(outs), len(scratch)
    late_at = {n: names.index(n) for n in late}
    early_at = {n: names.index(n) - n_in for n in early}
    total = sum(c for _, c in late.values()) + sum(c for _, c in early.values())

    def wrapped(*refs):
        refs = list(refs)
        sems = refs.pop() if total else None
        flow = Flow(sems)
        bufs = refs[n_in + n_out + n_own :]
        for n, buf in zip([*late, *early], bufs):
            if n in late:
                at = late_at[n]
                flow.add(n, refs[at], buf, *late[n])
            else:
                at = n_in + early_at[n]
                flow.add(n, buf, refs[at], *early[n])
            refs[at] = buf
        waiting = list(late)
        while waiting:
            count = late[waiting[0]][1]
            group = []
            while waiting and late[waiting[0]][1] == count:
                group.append(waiting.pop(0))
            for piece in range(count):
                for n in group:
                    flow.put(n, piece)
        body(flow, *refs[: n_in + n_out + n_own])
        for n, (_, count) in early.items():
            for piece in range(count):
                flow.need(n, piece)

    vmem, any_ = pltpu.VMEM, pl.ANY
    in_specs = [
        pl.BlockSpec(
            memory_space=pltpu.SMEM if i < smem else any_ if i in late_at.values() or names[i] in raw else vmem
        )
        for i in range(n_in)
    ]
    out_specs = [
        pl.BlockSpec(memory_space=any_ if i in early_at.values() or names[n_in + i] in raw else vmem)
        for i in range(n_out)
    ]
    bufs = [pltpu.VMEM(args[late_at[n]].shape, args[late_at[n]].dtype) for n in late]
    bufs += [pltpu.VMEM(*outs[early_at[n]]) for n in early]
    return pl.pallas_call(
        wrapped,
        out_shape=[jax.ShapeDtypeStruct(s, d) for s, d in outs],
        in_specs=in_specs,
        out_specs=out_specs,
        scratch_shapes=kinds
        + bufs
        + ([pltpu.SemaphoreType.DMA((total,))] if total else []),
        compiler_params=pltpu.CompilerParams(vmem_limit_bytes=limit * 1024 * 1024),
        cost_estimate=pl.CostEstimate(
            flops=int(us * 9e8), bytes_accessed=int(us * 3e6), transcendentals=0
        ),
        name=name,
    )(*args)


def swap(x):
    return lax.ppermute(x, "tensor", [(0, 1), (1, 0)])


def across(x, groups, bit):
    return lax.ppermute(x, "dp", [(i, i ^ bit) for i in range(groups)])


def phases_of(groups):
    found, weight = [], 1
    while weight < groups:
        members = min(4, groups // weight)
        found.append((weight, members))
        weight *= members
    return found


def send_round(blocks, groups, weight):
    return [blocks[0]] + [across(b, groups, k * weight) for k, b in enumerate(blocks) if k]


def resplit(x, at):
    value = x[:, at : at + 64] + x[:, at + 64 : at + 128]
    upper = lax.reduce_precision(value, 8, 7)
    return jnp.concatenate([x[:, :at], upper, value - upper, x[:, at + 128 :]], 1)


def split(x, rank, weight, members):
    rows = x.shape[0] // members
    place = (rank // weight) % members
    return [lax.dynamic_slice_in_dim(x, (place ^ k) * rows, rows, 0) for k in range(members)]


def assemble(got, rank, weight):
    members = len(got)
    place = (rank // weight) % members
    parts = []
    for i in range(members):
        now = got[i]
        for p in range(1, members):
            now = jnp.where(place == p, got[i ^ p], now)
        parts.append(now)
    return jnp.concatenate(parts, 0)


def on_device(
    hidden_in, teacher, loss_mask, lengths, dealing, norm_gain, w_gate, w_value, w_state, w_step,
    step_bias, conv_value, conv_vbias, conv_state, conv_sbias, decay_log, skip_gain, out_gain, w_out,
):
    groups = lax.axis_size("dp")
    rank = lax.axis_index("dp")
    member = lax.axis_index("tensor")
    seqs, local, _ = hidden_in.shape
    half = teacher.shape[2]
    T = local * groups
    C = w_gate.shape[1]
    HH = decay_log.shape[0]
    CH = T // Q

    [dealt] = call(deal_kernel, [((seqs, local, half), BF)], [], (dealing, hidden_in), 1, "deal", 3.0)
    dealt, loss_mask, teacher, w_gate = lax.optimization_barrier((dealt, loss_mask, teacher, w_gate))
    xo = lax.all_to_all(dealt, "dp", split_axis=0, concat_axis=0, tiled=True).reshape(T, half)

    pos = rank * local + lax.broadcasted_iota(jnp.int32, (seqs, local), 1)
    marks = (loss_mask > 0) & (pos < lengths[:, None])
    count = jnp.sum(marks.astype(F32)).reshape(1)
    goal = jnp.where(marks[:, :, None], teacher, jnp.asarray(NOMARK, BF))
    [goal] = call(deal_kernel, [((seqs, local, half), BF)], [], (dealing, goal), 1, "deal_goal", 2.0)
    length = lax.dynamic_slice_in_dim(lengths, dealing[rank], 1, 0)

    wcat, wt, wot, cd = call(
        prepare_kernel,
        [((D, 2 * C + 384), BF), ((2 * C + 384, D), BF), ((D, C), BF), ((D, 8), F32)],
        [],
        (w_gate, w_value, w_state, w_step.reshape(D, 2 * HH), w_out, norm_gain[None]),
        0,
        "prepare",
        6.0,
        early={"wcat": (0, 1), "wt": (0, 1)},
    )
    zc = jnp.zeros((256,), F32)
    cc = jnp.concatenate(
        [
            jnp.concatenate([conv_value, conv_state], 1),
            jnp.concatenate([conv_vbias, conv_sbias])[None],
            jnp.concatenate([jnp.repeat(skip_gain, PS), zc])[None],
            jnp.concatenate([out_gain, zc])[None],
            jnp.zeros((1, C + 256), F32),
        ],
        0,
    ).T
    rate = -jnp.exp(decay_log)
    rc = jnp.stack([step_bias.reshape(-1), jnp.concatenate([rate, rate])], 1)

    xo, goal, wcat, wt, wot, cc, cd, rc, count, length = lax.optimization_barrier(
        (xo, goal, wcat, wt, wot, cc, cd, rc, count, length)
    )
    xs = swap(xo)
    to = lax.all_to_all(goal, "dp", split_axis=0, concat_axis=0, tiled=True).reshape(T, half)
    ts = swap(to)

    full = lambda n: ((n, T), BF)
    fullf = lambda n: ((n, T), F32)
    xT, nT, rows, dec, gate, u, pre, act, cs, e, mixed, sin, p0, inv = call(
        forward_kernel,
        [
            full(D), full(D), fullf(120), ((CH, 24, Q), F32), fullf(C), full(C + 256), full(C + 256),
            full(C + 256), full(128), ((CH, HH, Q, Q), BF), fullf(C), ((CH, C, Q), BF), full(D + 16), fullf(8),
        ],
        [
            ((C + 256, T), F32), ((32, T), F32), ((24, T), F32), ((CH, C, Q), F32), ((C, Q), F32),
            ((C, 2 * Q), BF), ((C, T), BF),
        ],
        (length, xo, xs, wt, wot, cc, cd, rc),
        1,
        "forward",
        26.0,
        late={"xo": (0, CH // 2), "xs": (0, CH // 2), "wt": (0, 1), "cc": (0, 1), "wot": (0, 1)},
        early={
            **{n: (0, 1) for n in ("xT", "nT", "rows", "dec", "gate", "uO", "preO", "act", "cs", "sin")},
            "mixed": (1, CH // 2),
            "eO": (0, CH // 2), "pO": (1, T // 256),
        },
    )
    p1 = swap(p0)
    lo, doh, dyT, dgate, small, *mids = call(
        middle_kernel,
        [((T, half), BF), full(half), full(C), full(C), ((C, Q), F32)] + [((D // 4, D + C), BF)] * 4,
        [
            ((D, Q), F32), ((D, Q), F32), ((C, T), BF), ((C, 256), F32), ((8, T), F32), ((C, Q), F32),
            ((8, T), F32), full(D),
        ],
        (p0, p1, xT, to, ts, w_out, nT, gate, mixed, cc),
        0,
        "middle",
        14.0,
        late={
            **{n: (1, CH // 2) for n in ("p0", "p1", "xT")}, "to": (0, CH // 2), "ts": (0, CH // 2),
            "wo": (0, 1), "cc": (0, 1), "gate": (1, T // 256), "mixed": (1, T // 256), "nT": (0, 1),
        },
        early={
            "dyT": (1, T // 256), **{n: (0, 1) for n in ("doh", "lo", "dgate", "m0", "m1", "m2", "m3")},
        },
    )
    phases = phases_of(groups)
    got_m = send_round(mids, groups, 1)
    rowsf = ((24, T), F32)
    width = C + Q + 256
    b0, b1, b2, b3, dno, dnx, dots = call(
        backward_kernel,
        [((D // 4, width), BF)] * 4 + [full(half), full(half + 16), fullf(8)],
        [
            ((D, Q), F32), rowsf, fullf(C + 256), rowsf, rowsf, rowsf, rowsf, ((CH, HH, Q), F32), ((CH, C, Q), F32),
            ((CH, C, Q), BF), ((C, Q), F32), ((C, 2 * Q), BF), ((C, 2 * Q), BF), ((C, Q), F32), rowsf,
            ((C + 256, 5 * Q), F32), full(2 * C + 384), ((D, 256), F32),
        ],
        (length, count, act, cs, rows, dec, e, sin, dyT, u, pre, dgate, nT, wcat, cc, cd, rc, small),
        2,
        "backward",
        30.0,
        late={
            **{n: (0, 1) for n in ("rows", "cs")},
            "dyT": (1, CH // 2),
            **{n: (0, 1) for n in ("dec", "sin", "act", "cc")},
            "e_in": (0, CH // 2),
            **{n: (0, 1) for n in ("dgate", "u_in", "pre_in", "small", "nT", "wcat", "cd")},
        },
        early={
            "dno": (1, T // 256), "dnx": (1, T // 256), **{n: (0, 1) for n in ("b0", "b1", "b2", "b3")},
        },
    )
    now_m = sum(g.astype(F32) for g in got_m)
    dnr = swap(dnx)
    now_m, dnr = lax.optimization_barrier((now_m, dnr))
    blocks = split(now_m, rank, *phases[1])
    got_m = send_round([b if k == 0 else b.astype(BF) for k, b in enumerate(blocks)], groups, phases[1][0])
    got = send_round([b0, b1, b2, b3], groups, 1)
    [dx] = call(
        last_kernel,
        [((T, half), BF)],
        [((half, T), BF), pltpu.SemaphoreType.DMA((CH,))],
        (dno, dnr, doh, dots, inv, xT),
        0,
        "last",
        3.0,
        late={n: (1, T // 512) for n in ("dno", "dnr", "do_s")},
        early={"out": (0, T // 512)},
        raw=("xT",),
    )
    dx, got, got_m = lax.optimization_barrier((dx, got, got_m))
    held = sum(g.astype(F32) for g in got_m)
    for weight, members in phases[2:]:
        blocks = split(held, rank, weight, members)
        got_m = send_round([b if k == 0 else b.astype(BF) for k, b in enumerate(blocks)], groups, weight)
        held = sum(g.astype(F32) for g in got_m)
    held = held.astype(BF)
    now = resplit(sum(g.astype(F32) for g in got), C)
    for weight, members in reversed(phases[1:]):
        pieces = send_round([held] * members, groups, weight)
        now, pieces = lax.optimization_barrier((now, pieces))
        held = assemble(pieces, rank, weight)
    held = send_round([held] * 4, groups, 1)
    for weight, members in phases[1:]:
        blocks = split(now, rank, weight, members)
        got = send_round([b if k == 0 else b.astype(BF) for k, b in enumerate(blocks)], groups, weight)
        now = resplit(sum(g.astype(F32) for g in got), C)
    lane = lax.broadcasted_iota(jnp.int32, (1, Q + 256), 1)
    both = (lane >= Q) | ((lane % 64 >= 41) & (lane % 64 < 47))
    tail = now[:, C:]
    tail = resplit(tail + jnp.where(both, swap(tail.astype(BF)).astype(F32), 0.0), 0)
    now = jnp.concatenate([now[:, :C], tail], 1).astype(BF)
    now, held = lax.optimization_barrier((now, held))
    for weight, members in reversed(phases[1:]):
        now = assemble(send_round([now] * members, groups, weight), rank, weight)
    got = send_round([now] * 4, groups, 1)
    back = lax.all_to_all(dx.reshape(seqs, local, half), "dp", split_axis=0, concat_axis=0, tiled=True)
    wo, wg = call(
        finish_first_kernel,
        [((C, D), F32), ((D, C), F32)],
        [],
        (now[0:8, C : C + Q], *held),
        0,
        "finish_first",
        5.0,
        late={n: (0, 1) for n in ("h0", "h1", "h2", "h3")},
        early={n: (0, 1) for n in ("wo", "wg")},
        static={"full_len": T},
    )
    gv, gt, gs, ng, cv, vb, cst, sb, dl, sk, og, bias, grad_in = call(
        finish_kernel,
        [
            ((D, C), F32), ((D, 2 * HH), F32), ((D, 256), F32), ((D,), F32), ((4, C), F32), ((C,), F32),
            ((4, 256), F32), ((256,), F32), ((HH,), F32), ((HH,), F32), ((C,), F32), ((2, HH), F32),
            ((seqs, local, half), BF),
        ],
        [((D, Q), F32)],
        (dealing, *got, back),
        1,
        "finish",
        4.0,
        late={n: (0, 1) for n in ("g0", "g1", "g2", "g3", "back")},
        early={n: (0, 1) for n in ("gv", "gs", "grad_in")},
        static={"full_len": T},
    )
    return (
        lo[None], grad_in, ng, wg, gv, gs, gt.reshape(D, 2, HH), bias, cv, vb, cst, sb, dl, sk, og, wo,
    )


def solution(mesh):
    dp, tp = "dp", "tensor"
    return jax.shard_map(
        on_device,
        mesh=mesh,
        in_specs=(
            P(None, dp, None), P(None, dp, tp), P(None, dp), P(), P(), P(), P(None, tp), P(None, tp), P(),
            P(None, None, tp), P(None, tp), P(None, tp), P(tp), P(), P(), P(tp), P(tp), P(tp), P(tp, None),
        ),
        out_specs=(
            P(dp, None, tp), P(None, dp, tp), P(), P(None, tp), P(None, tp), P(), P(None, None, tp),
            P(None, tp), P(None, tp), P(tp), P(), P(), P(tp), P(tp), P(tp), P(tp, None),
        ),
        check_vma=False,
    )
```

```python
import functools
import inspect

import jax
import jax.numpy as jnp
from jax import lax
from jax.experimental import pallas as pl
from jax.experimental.pallas import tpu as pltpu
from jax.sharding import PartitionSpec as P

D = 768
INNER = 1536
PS = 64
N = 64
Q = 128
EPS = 1e-5
NOMARK = 256.0
BF = jnp.bfloat16
F32 = jnp.float32
HI = lax.Precision.HIGHEST


def pairs(count, before=None, after=None):
    def run(body):
        @pl.loop(0, count // 2)
        def _(k):
            if before:
                before(k)
            body(2 * k)
            body(2 * k + 1)
            if after:
                after(k)

    return run


ROWS = 32

NN = (((1,), (0,)), ((), ()))
NT = (((1,), (1,)), ((), ()))


def mm(a, b, dims=NN):
    return lax.dot_general(a, b, dims, preferred_element_type=F32)


def mm_hi(a, b):
    return lax.dot_general(a, b, NN, precision=HI, preferred_element_type=F32)


def lanes(c, width=Q):
    return pl.ds(pl.multiple_of(c * width, width), width)


def iota2(shape, dim):
    return lax.broadcasted_iota(jnp.int32, shape, dim)


def log1p_exp(z):
    w = 1.0 + z
    return jnp.where(w == 1.0, z, jnp.log(w) * (z / jnp.where(w == 1.0, 1.0, w - 1.0)))


RAW, DT, CUM, CUE, ROWV = 0, 24, 48, 72, 96


def deal_kernel(io, dealing, src, dst):
    count, _, width = dst.shape
    if src.shape[2] == width:
        col = pl.ds(0, width)
    else:
        col = pl.ds(pl.multiple_of(lax.axis_index("tensor") * width, width), width)

    @pl.loop(0, count)
    def _(j):
        dst[j] = src[dealing[j], :, col]


def prepare_kernel(io, wg, wv, ws, wst, wo, ng, wcat, wt, wot, cd):
    C = wg.shape[1]
    W = 2 * C + 256
    wcat[:, 0:C] = wg[...]
    wcat[:, C : 2 * C] = wv[...]
    wcat[:, 2 * C : W] = ws[...]
    wcat[:, W : W + Q] = jnp.concatenate([wst[...], jnp.zeros((D, Q - wst.shape[1]), BF)], 1)
    io.put("wcat")

    @pl.loop(0, (W + Q) // Q)
    def _(c):
        wt[lanes(c), :] = wcat[:, lanes(c)].astype(F32).T.astype(BF)

    io.put("wt")

    @pl.loop(0, D // Q)
    def _(c):
        wot[lanes(c), :] = wo[:, lanes(c)].astype(F32).T.astype(BF)

    cd[...] = jnp.broadcast_to(ng[...], (8, D)).T


def forward_kernel(
    io, length, xo, xs, wt, wot, cc, cd, rc,
    xT, nT, rows, dec, gate, uO, preO, act, cs, eO, mixed, sin, pO, inv_o,
    u_s, raw_s, w_s, dS, run, vw, bu,
):
    T = xo.shape[0]
    CH = T // Q
    C = gate.shape[0]
    HH = C // PS
    half = xo.shape[1]
    m = lax.axis_index("tensor")
    own = pl.multiple_of(m * half, half)
    other = pl.multiple_of((1 - m) * half, half)

    def arrive(k):
        io.need("xo", k)
        io.need("xs", k)

    @pairs(CH, arrive)
    def _(c):
        l = lanes(c)
        xT[pl.ds(own, half), l] = xo[l, :].astype(F32).T.astype(BF)
        xT[pl.ds(other, half), l] = xs[l, :].astype(F32).T.astype(BF)
        x = xT[:, l].astype(F32)
        inv = lax.rsqrt(jnp.sum(x * x, 0, keepdims=True) / D + EPS)
        inv_o[:, l] = jnp.broadcast_to(inv, (8, Q))
        nT[:, l] = (x * inv * cd[:, 0:1]).astype(BF)

    io.put("xT")
    io.put("nT")
    io.need("wt")

    @pl.loop(0, T // 256, unroll=2)
    def _(j):
        l = lanes(j, 256)
        n = nT[:, l]
        gate[:, l] = mm(wt[0:C, :], n)
        u_s[:, l] = mm(wt[C : 2 * C + 256, :], n)
        raw_s[:, l] = mm(wt[2 * C + 256 : 2 * C + 288, :], n)

    io.put("gate")

    raw = raw_s[0:24, :] + rc[:, 0:1]
    live = (iota2((1, T), 1) < length[0]).astype(F32)
    dt = (jnp.maximum(raw, 0.0) + log1p_exp(jnp.exp(-jnp.abs(raw)))) * live
    la = dt * rc[:, 1:2]
    rows[RAW : RAW + 24, :] = raw
    rows[DT : DT + 24, :] = dt
    upper = (iota2((Q, Q), 0) <= iota2((Q, Q), 1)).astype(F32)
    lower = (iota2((Q, Q), 0) >= iota2((Q, Q), 1)).astype(F32)
    stacked = jnp.concatenate([la[:, c * Q : (c + 1) * Q] for c in range(CH)], 0)
    cum_f = mm_hi(stacked, upper)
    cum_b = mm_hi(stacked, lower)
    first = iota2((24, Q), 0) < HH
    for c in range(CH):
        r = slice(24 * c, 24 * c + 24)
        k = slice(Q * c, Q * c + Q)
        cum = jnp.where(first, cum_f[r], cum_b[r])
        dtc = dt[:, k]
        rows[CUM : CUM + 24, k] = cum
        rows[CUE : CUE + 24, k] = cum - la[:, k]
        rows[ROWV : ROWV + 24, k] = jnp.where(
            dtc > 0.0, cum - jnp.log(jnp.where(dtc > 0.0, dtc, 1.0)), 1e30
        )
        tot = jnp.broadcast_to(jnp.sum(la[:, k], 1, keepdims=True), (24, Q))
        dec[c] = jnp.exp(tot)
        w_s[:, k] = jnp.exp(tot - cum) * dtc

    io.put("rows")
    io.put("dec")
    io.need("cc")

    at = iota2((ROWS, Q), 1)

    @pl.loop(0, u_s.shape[0] // ROWS, unroll=2)
    def _(b):
        r = pl.ds(pl.multiple_of(b * ROWS, ROWS), ROWS)
        col = cc[r, :]
        ks = [jnp.broadcast_to(col[:, k : k + 1], (ROWS, Q)) for k in range(5)]
        earlier = [jnp.zeros((ROWS, Q), F32)] * 4
        for c in range(CH):
            l = slice(c * Q, c * Q + Q)
            uu = u_s[r, l]
            pre = ks[4] + ks[3] * uu
            for back in (1, 2, 3):
                moved = pltpu.roll(uu, back, 1)
                pre = pre + ks[3 - back] * jnp.where(at >= back, moved, earlier[back])
                earlier[back] = moved
            uO[r, l] = uu.astype(BF)
            preO[r, l] = pre.astype(BF)
            act[r, l] = (pre * jax.nn.sigmoid(pre)).astype(BF)

    cs[0:64, :] = pltpu.roll(act[C + 64 : C + 128, :].astype(F32), 1, 1).astype(BF)
    cs[64:128, :] = pltpu.roll(act[C + 192 : C + 256, :].astype(F32), T - 1, 1).astype(BF)

    io.put("uO")
    io.put("preO")
    io.put("act")
    io.put("cs")

    zeros = jnp.zeros((64, Q), BF)

    @pairs(CH)
    def _(c):
        l = lanes(c)
        for h in range(HH):
            v = act[64 * h : 64 * h + 64, l].astype(F32)
            vw[64 * h : 64 * h + 64, 0:Q] = (v * w_s[h : h + 1, l]).astype(BF)
            vw[64 * h : 64 * h + 64, Q : 2 * Q] = (v * w_s[HH + h : HH + h + 1, l]).astype(BF)
        both = jnp.concatenate(
            [
                jnp.concatenate([act[C : C + 64, l], zeros], 1),
                jnp.concatenate([zeros, act[C + 128 : C + 192, l]], 1),
            ],
            0,
        )
        dS[c] = mm(vw[...], both, NT)

    run[...] = jnp.zeros_like(run)
    low = iota2((64, Q), 1) < 64
    low_h = iota2((HH, Q), 1) < 64

    @pairs(CH)
    def _(i):
        d = jnp.where(low_h, dec[i][0:HH], dec[CH - 1 - i][HH : 2 * HH])
        for h in range(HH):
            r = slice(64 * h, 64 * h + 64)
            now = run[r, :]
            sin[i, r, :] = now.astype(BF)
            run[r, :] = now * d[h : h + 1] + jnp.where(low, dS[i, r, :], dS[CH - 1 - i, r, :])

    io.put("sin")

    before = iota2((Q, Q), 1) < iota2((Q, Q), 0)
    after = iota2((Q, Q), 1) > iota2((Q, Q), 0)
    top = iota2((Q, Q), 0) < 64

    def leave(k):
        io.put("eO", k)
        io.put("mixed", k)

    @pairs(CH, after=leave)
    def _(c):
        l = lanes(c)
        bf = act[C : C + 64, l]
        bb = act[C + 128 : C + 192, l]
        cf = cs[0:64, l]
        cb = cs[64:128, l]
        gf = mm(cf.astype(F32).T.astype(BF), bf)
        gb = mm(cb.astype(F32).T.astype(BF), bb)
        g = jnp.where(before, gf, jnp.where(after, gb, 0.0))
        cue = rows[CUE : CUE + 24, l]
        cols = jnp.concatenate([cue, jnp.zeros((Q - 24, Q), F32)], 0).T
        ecue = jnp.exp(cue)
        zc = jnp.zeros((64, Q), BF)
        yf = mm(sin[c], jnp.concatenate([cf, zc], 0))
        yb = mm(sin[CH - 1 - c], jnp.concatenate([zc, cb], 0))
        total = jnp.zeros((1, Q), F32)
        for j in range(HH // 2):
            ms = []
            for h in (2 * j, 2 * j + 1):
                gap = jnp.where(
                    before,
                    cols[:, h : h + 1] - rows[ROWV + h : ROWV + h + 1, l],
                    cols[:, HH + h : HH + h + 1] - rows[ROWV + HH + h : ROWV + HH + h + 1, l],
                )
                e = jnp.exp(jnp.minimum(gap, 30.0))
                eO[c, h] = e.astype(BF)
                ms.append((e * g).astype(BF))
            v = act[128 * j : 128 * j + 128, l]
            vz = jnp.zeros_like(v)
            pair = jnp.concatenate([jnp.where(top, v, vz), jnp.where(top, vz, v)], 1)
            y = mm(pair, jnp.concatenate(ms, 1), NT)
            for k in (0, 1):
                h = 2 * j + k
                r = slice(64 * h, 64 * h + 64)
                mix = (
                    y[64 * k : 64 * k + 64]
                    + ecue[h : h + 1] * yf[r]
                    + ecue[HH + h : HH + h + 1] * yb[r]
                    + cc[r, 5:6] * v[64 * k : 64 * k + 64].astype(F32)
                )
                mixed[r, l] = mix
                gt = gate[r, l]
                gated = mix * (gt * jax.nn.sigmoid(gt))
                total = total + jnp.sum(gated * gated, 0, keepdims=True)
                bu[r, l] = (gated * cc[r, 6:7]).astype(BF)
        top_part = total.astype(BF).astype(F32)
        pO[D : D + 16, l] = jnp.where(
            iota2((16, Q), 0) == 0, top_part, jnp.where(iota2((16, Q), 0) == 1, total - top_part, 0.0)
        ).astype(BF)

    io.need("wot")

    @pl.loop(0, T // 256)
    def _(j):
        l = lanes(j, 256)
        pO[0:D, l] = mm(wot[...], bu[:, l]).astype(BF)
        io.put("pO", j)


def middle_kernel(
    io, p0, p1, xT, to, ts, wo, nT, gate, mixed, cc,
    lo, doh, dyT, dgate, small, m0, m1, m2, m3,
    res_s, tea_s, branch, dbr, dot_s, acc_g, q_s, doT,
):
    T = to.shape[0]
    CH = T // Q
    C = gate.shape[0]
    half = to.shape[1]
    m = lax.axis_index("tensor")
    own = pl.multiple_of(m * half, half)
    other = pl.multiple_of((1 - m) * half, half)

    def arrive(k):
        for n in ("p0", "p1", "xT", "to", "ts"):
            io.need(n, k)

    @pairs(CH, arrive)
    def _(c):
        l = lanes(c)
        tea_s[pl.ds(own, half), :] = to[l, :].astype(F32).T
        tea_s[pl.ds(other, half), :] = ts[l, :].astype(F32).T
        pt = p0[0:D, l].astype(F32) + p1[0:D, l].astype(F32)
        sums = p0[D : D + 16, l].astype(F32) + p1[D : D + 16, l].astype(F32)
        q = lax.rsqrt((sums[0:1] + sums[1:2]) / INNER + EPS)
        q_s[:, l] = jnp.broadcast_to(q, (8, Q))
        res = xT[:, l].astype(F32) + q * pt
        res_s[...] = res
        tea = tea_s[...]
        do = jnp.where(tea < 0.5 * NOMARK, res - tea, 0.0).astype(BF)
        doT[:, l] = do
        dot_s[:, l] = jnp.broadcast_to(jnp.sum(do.astype(F32) * pt, 0, keepdims=True), (8, Q))
        lo[l, :] = res_s[pl.ds(own, half), :].T.astype(BF)
        doh[:, l] = doT[pl.ds(own, half), l]

    io.put("doh")
    io.put("lo")
    acc_g[...] = jnp.zeros_like(acc_g)

    for n in ("wo", "cc"):
        io.need(n)

    @pl.loop(0, T // 256)
    def _(j):
        l = lanes(j, 256)
        io.need("gate", j)
        io.need("mixed", j)
        dbr[...] = mm(wo[...], doT[:, l])
        q = q_s[0:1, l]
        q3 = q * q * q * dot_s[0:1, l] / INNER

        @pl.loop(0, C // 64, unroll=2)
        def _(b):
            r = pl.ds(pl.multiple_of(b * 64, 64), 64)
            gain = jnp.broadcast_to(cc[r, 6:7], (64, Q))
            acc = acc_g[r, :]
            for t in (0, 1):
                k = slice(t * Q, t * Q + Q)
                l1 = pl.ds(pl.multiple_of(j * 256 + t * Q, Q), Q)
                d = dbr[r, k]
                g = gate[r, l1]
                mix = mixed[r, l1]
                sg = jax.nn.sigmoid(g)
                si = g * sg
                gated = mix * si
                gq = gated * q[:, k]
                branch[r, l1] = (gq * gain).astype(BF)
                acc = acc + d * gq
                dgt = q[:, k] * (d * gain) - gated * q3[:, k]
                dyT[r, l1] = (dgt * si).astype(BF)
                dgate[r, l1] = (dgt * mix * (sg * (1.0 + g * (1.0 - sg)))).astype(BF)
            acc_g[r, :] = acc

        io.put("dyT", j)

    io.put("dgate")
    io.need("nT")
    place = lax.axis_index("dp") % 4
    share = m0.shape[0]
    for k, ref in enumerate((m0, m1, m2, m3)):
        r = pl.ds(pl.multiple_of((place ^ k) * share, share), share)
        ref[:, 0:D] = mm(branch[r, :], doT[...], NT).astype(BF)
        ref[:, D : D + C] = mm(nT[r, :], dgate[...], NT).astype(BF)
        io.put("m%d" % k)
    small[...] = jnp.where(iota2((C, Q), 1) == 38, jnp.sum(acc_g[...], 1, keepdims=True), 0.0)


def backward_kernel(
    io, length, count, act, cs, rows, dec, e_in, sin, dyT, u_in, pre_in, dgate, nT, wcat, cc, cd, rc, small,
    b0, b1, b2, b3, dno, dnx, dots,
    acc, sk_rows, dact, c_rows, r_rows, ci_rows, ri_rows, kk, dA, ain, run, vw, dye, small_s, dla_s, sums, dproj, dn_s,
):
    T = act.shape[1]
    CH = T // Q
    C = dyT.shape[0]
    HH = C // PS
    zeros = jnp.zeros((64, Q), BF)

    io.need("rows")
    io.need("cs")

    @pairs(CH, lambda k: io.need("dyT", k))
    def _(c):
        l = lanes(c)
        ecue = jnp.exp(rows[CUE : CUE + 24, l])
        for h in range(HH):
            dy = dyT[64 * h : 64 * h + 64, l].astype(F32)
            dye[64 * h : 64 * h + 64, 0:Q] = (dy * ecue[h : h + 1]).astype(BF)
            dye[64 * h : 64 * h + 64, Q : 2 * Q] = (dy * ecue[HH + h : HH + h + 1]).astype(BF)
        both = jnp.concatenate(
            [
                jnp.concatenate([cs[0:64, l], zeros], 1),
                jnp.concatenate([zeros, cs[64:128, l]], 1),
            ],
            0,
        )
        dA[c] = mm(dye[...], both, NT)

    io.need("dec")
    io.need("sin")
    run[...] = jnp.zeros_like(run)
    low = iota2((64, Q), 1) < 64
    low_h = iota2((HH, Q), 1) < 64

    @pl.loop(0, CH)
    def _(i):
        f = CH - 1 - i
        d = jnp.where(low_h, dec[f][0:HH], dec[i][HH : 2 * HH])
        for h in range(HH):
            r = slice(64 * h, 64 * h + 64)
            now = run[r, :]
            ain[i, r, :] = now.astype(BF)
            flow = jnp.sum(now * sin[f, r, :].astype(F32), 0, keepdims=True) * d[h : h + 1]
            kk[i, h : h + 1, :] = flow
            run[r, :] = now * d[h : h + 1] + jnp.where(low, dA[f, r, :], dA[i, r, :])

    io.need("act")
    io.need("cc")
    sk_rows[...] = jnp.zeros_like(sk_rows)
    before = iota2((Q, Q), 1) < iota2((Q, Q), 0)
    after = iota2((Q, Q), 1) > iota2((Q, Q), 0)
    left = iota2((Q, Q), 1) < 64
    top = iota2((Q, Q), 0) < 64
    lane = iota2((Q, Q), 1)

    @pl.loop(0, CH)
    def _(c):
        l = lanes(c)

        @pl.when(c % 2 == 0)
        def _():
            io.need("e_in", c // 2)

        bf = act[C : C + 64, l]
        bb = act[C + 128 : C + 192, l]
        cf = cs[0:64, l]
        cb = cs[64:128, l]
        gf = mm(cf.astype(F32).T.astype(BF), bf)
        gb = mm(cb.astype(F32).T.astype(BF), bb)
        g = jnp.where(before, gf, jnp.where(after, gb, 0.0))
        ecue = jnp.exp(rows[CUE : CUE + 24, l])
        w = jnp.exp(
            jnp.where(
                iota2((24, Q), 0) < HH,
                rows[CUM : CUM + 24, l][:, Q - 1 : Q],
                rows[CUM : CUM + 24, l][:, 0:1],
            )
            - rows[CUM : CUM + 24, l]
        ) * rows[DT : DT + 24, l]
        for h in range(HH):
            r = slice(64 * h, 64 * h + 64)
            dy = dyT[r, l].astype(F32)
            v = act[r, l].astype(F32)
            dye[r, 0:Q] = (dy * ecue[h : h + 1]).astype(BF)
            dye[r, Q : 2 * Q] = (dy * ecue[HH + h : HH + h + 1]).astype(BF)
            vw[r, 0:Q] = (v * w[h : h + 1]).astype(BF)
            vw[r, Q : 2 * Q] = (v * w[HH + h : HH + h + 1]).astype(BF)
        zc = jnp.zeros((64, Q), BF)
        sf = sin[c]
        sb = sin[CH - 1 - c]
        af = ain[CH - 1 - c]
        ab = ain[c]
        yf = mm(sf, jnp.concatenate([cf, zc], 0))
        yb = mm(sb, jnp.concatenate([zc, cb], 0))
        vf = mm(af, jnp.concatenate([bf, zc], 0))
        vb = mm(ab, jnp.concatenate([zc, bb], 0))
        dcf = mm(sf.astype(F32).T.astype(BF)[0:64], dye[:, 0:Q])
        dcb = mm(sb.astype(F32).T.astype(BF)[64:128], dye[:, Q : 2 * Q])
        dbf = mm(af.astype(F32).T.astype(BF)[0:64], vw[:, 0:Q])
        dbb = mm(ab.astype(F32).T.astype(BF)[64:128], vw[:, Q : 2 * Q])
        dg = jnp.zeros((Q, Q), F32)
        rc_cols = jnp.zeros((Q, Q), F32)
        for j in range(HH // 2):
            r2 = slice(128 * j, 128 * j + 128)
            v = act[r2, l]
            dy = dyT[r2, l]
            dy_f = dy.astype(F32)
            dyt = dy_f.T.astype(BF)
            zb = jnp.zeros_like(dyt)
            dm2 = mm(jnp.concatenate([jnp.where(left, dyt, zb), jnp.where(left, zb, dyt)], 0), v)
            ms = []
            for k in (0, 1):
                h = 2 * j + k
                e = e_in[c, h].astype(F32)
                x = e * dm2[Q * k : Q * k + Q]
                dg = dg + x
                t = x * g
                tf = jnp.where(before, t, 0.0)
                ms.append((e * g).astype(BF))
                c_all = jnp.sum(t, 0, keepdims=True)
                c_f = jnp.sum(tf, 0, keepdims=True)
                c_rows[h : h + 1, l] = c_f
                c_rows[HH + h : HH + h + 1, l] = c_all - c_f
                r_all = jnp.sum(t, 1, keepdims=True)
                r_f = jnp.sum(tf, 1, keepdims=True)
                rc_cols = jnp.where(lane == h, r_f, rc_cols)
                rc_cols = jnp.where(lane == HH + h, r_all - r_f, rc_cols)
            dv = mm(
                jnp.concatenate([jnp.where(top, dy, zb), jnp.where(top, zb, dy)], 1),
                jnp.concatenate(ms, 0),
            )
            for k in (0, 1):
                h = 2 * j + k
                r = slice(64 * h, 64 * h + 64)
                v1 = v[64 * k : 64 * k + 64].astype(F32)
                dy1 = dy_f[64 * k : 64 * k + 64]
                sk_rows[h : h + 1, l] = jnp.sum(v1 * dy1, 0, keepdims=True)
                f_in = vf[r] * w[h : h + 1]
                b_in = vb[r] * w[HH + h : HH + h + 1]
                ci_rows[h : h + 1, l] = jnp.sum(f_in * v1, 0, keepdims=True)
                ci_rows[HH + h : HH + h + 1, l] = jnp.sum(b_in * v1, 0, keepdims=True)
                ri_rows[h : h + 1, l] = jnp.sum(yf[r] * dy1, 0, keepdims=True) * ecue[h : h + 1]
                ri_rows[HH + h : HH + h + 1, l] = (
                    jnp.sum(yb[r] * dy1, 0, keepdims=True) * ecue[HH + h : HH + h + 1]
                )
                dact[r, l] = dv[64 * k : 64 * k + 64] + f_in + b_in + cc[r, 5:6] * dy1
        r_rows[:, l] = rc_cols.T[0:24, :]
        dgf = jnp.where(before, dg, 0.0).astype(BF)
        dgb = jnp.where(after, dg, 0.0).astype(BF)
        dact[C : C + 64, l] = dbf + mm(cf, dgf)
        dact[C + 64 : C + 128, l] = dcf + mm(bf, dgf, NT)
        dact[C + 128 : C + 192, l] = dbb + mm(cb, dgb)
        dact[C + 192 : C + 256, l] = dcb + mm(bb, dgb, NT)

    dact[C + 64 : C + 128, :] = pltpu.roll(dact[C + 64 : C + 128, :], T - 1, 1)
    dact[C + 192 : C + 256, :] = pltpu.roll(dact[C + 192 : C + 256, :], 1, 1)

    ii, jj = iota2((Q, Q), 0), iota2((Q, Q), 1)
    gt = (ii > jj).astype(F32)
    ge = (ii >= jj).astype(F32)
    lt = (ii < jj).astype(F32)
    le = (ii <= jj).astype(F32)
    first = iota2((24, Q), 0) < HH
    cat = lambda ref: jnp.concatenate([ref[:, c * Q : (c + 1) * Q] for c in range(CH)], 0)
    r_in, c_in, c_x, r_x = cat(r_rows), cat(c_rows), cat(ci_rows), cat(ri_rows)
    rt = r_in + r_x
    as_f = mm_hi(rt, gt) - mm_hi(c_in, ge) + mm_hi(c_x, lt)
    as_b = mm_hi(rt, lt) - mm_hi(c_in, le) + mm_hi(c_x, gt)
    for c in range(CH):
        k = slice(24 * c, 24 * c + 24)
        l = slice(Q * c, Q * c + Q)
        kf = jnp.sum(jnp.where(low_h, kk[CH - 1 - c], 0.0), 1, keepdims=True)
        kb = jnp.sum(jnp.where(low_h, 0.0, kk[c]), 1, keepdims=True)
        dla_s[0:HH, l] = as_f[k][0:HH] + kf
        dla_s[HH : 2 * HH, l] = as_b[k][HH : 2 * HH] + kb
    dla = dla_s[...]
    dt = rows[DT : DT + 24, :]
    rate = rc[:, 1:2]
    live = (iota2((1, T), 1) < length[0]).astype(F32)
    sig = jax.nn.sigmoid(rows[RAW : RAW + 24, :])
    direct = (c_rows[...] + ci_rows[...]) * jnp.where(dt > 0.0, sig / jnp.where(dt > 0.0, dt, 1.0), 0.0)
    draw = (direct + rate * dla * sig) * live
    g_bias = jnp.sum(draw, 1, keepdims=True)
    g_decay = jnp.sum(dla * dt, 1, keepdims=True) * rate
    g_skip = jnp.sum(sk_rows[...], 1, keepdims=True)
    io.need("dgate")
    dproj[0:C, :] = dgate[...]
    dproj[2 * C + 256 : 2 * C + 384, :] = jnp.concatenate([draw, jnp.zeros((104, T), F32)], 0).astype(BF)

    io.need("u_in")
    io.need("pre_in")
    at = iota2((ROWS, Q), 1)

    @pl.loop(0, (C + 256) // ROWS, unroll=2)
    def _(b):
        r = pl.ds(pl.multiple_of(b * ROWS, ROWS), ROWS)
        r_out = pl.ds(pl.multiple_of(b * ROWS + C, ROWS), ROWS)
        col = cc[r, :]
        ks = [jnp.broadcast_to(col[:, k : k + 1], (ROWS, Q)) for k in range(4)]
        later = [jnp.zeros((ROWS, Q), F32)] * 4
        totals = [jnp.zeros((ROWS, Q), F32)] * 5
        for c in reversed(range(CH)):
            l = slice(c * Q, c * Q + Q)
            pre = pre_in[r, l].astype(F32)
            sg = jax.nn.sigmoid(pre)
            dp = dact[r, l] * (sg * (1.0 + pre * (1.0 - sg)))
            uu = u_in[r, l].astype(F32)
            du = ks[3] * dp
            totals[4] = totals[4] + dp
            totals[3] = totals[3] + dp * uu
            for back in (1, 2, 3):
                moved = pltpu.roll(dp, Q - back, 1)
                ahead = jnp.where(at < Q - back, moved, later[back])
                later[back] = moved
                totals[3 - back] = totals[3 - back] + ahead * uu
                du = du + ks[3 - back] * ahead
            dproj[r_out, l] = du.astype(BF)
        for k in range(5):
            sums[r, k * Q : k * Q + Q] = totals[k]

    def lane_sums(part, first_lane):
        upper = part.astype(BF)
        lower = (part - upper.astype(F32)).astype(BF)
        pick = (iota2((5 * Q, Q), 0) // Q + first_lane == iota2((5 * Q, Q), 1)).astype(BF)
        return mm(upper, pick) + mm(lower, pick)

    io.need("small")
    small_s[0:C, :] = lane_sums(sums[0:C, :], 32) + small[...]
    small_s[0:256, :] += lane_sums(sums[C : C + 256, :], 42)
    head_lane = iota2((24, Q), 1)
    heads_part = jnp.where(head_lane == 39, g_bias, jnp.where(head_lane == 40, g_decay, 0.0))
    small_s[0:24, :] += jnp.where(head_lane == 37, g_skip, heads_part)
    counted = (iota2((8, Q), 1) == 48) & (iota2((8, Q), 0) == 0)
    for k in range(4):
        at_row = k * (D // 4)
        small_s[at_row : at_row + 8, :] += jnp.where(counted, count[0], 0.0)
    io.need("nT")
    io.need("wcat")
    io.need("cd")
    half = dno.shape[0]
    m = lax.axis_index("tensor")
    own = pl.multiple_of(m * half, half)
    other = pl.multiple_of((1 - m) * half, half)
    W = 2 * C + 256
    acc[...] = jnp.zeros_like(acc)

    @pl.loop(0, T // 256, unroll=2)
    def _(j):
        l = lanes(j, 256)
        dn = mm(wcat[...], dproj[:, l])
        dn_s[...] = dn * cd[:, 0:1]
        part = dn * nT[:, l].astype(F32)
        acc[...] += part[:, 0:Q] + part[:, Q : 2 * Q]
        dot = jnp.sum(part, 0, keepdims=True)
        dots[:, l] = jnp.broadcast_to(dot, (8, 256))
        dno[:, l] = dn_s[pl.ds(own, half), :].astype(BF)
        dnx[0:half, l] = dn_s[pl.ds(other, half), :].astype(BF)
        top_part = dot.astype(BF).astype(F32)
        row = iota2((16, 256), 0)
        dnx[half : half + 16, l] = jnp.where(
            row == 0, top_part, jnp.where(row == 1, dot - top_part, 0.0)
        ).astype(BF)
        io.put("dno", j)
        io.put("dnx", j)

    wide = jnp.sum(acc[...], 1, keepdims=True) / cd[:, 0:1]
    small_s[...] += jnp.where(iota2((D, Q), 1) == 41, wide, 0.0)
    place = lax.axis_index("dp") % 4
    share = b0.shape[0]
    for k, ref in enumerate((b0, b1, b2, b3)):
        r = pl.ds(pl.multiple_of((place ^ k) * share, share), share)
        n = nT[r, :]
        ref[:, 0:C] = mm(n, dproj[C : 2 * C, :], NT).astype(BF)
        ref[:, C + Q : C + Q + 256] = mm(n, dproj[2 * C : W, :], NT).astype(BF)
        fine = mm(n, dproj[W : W + Q, :], NT) + small_s[r, :]
        upper = fine.astype(BF)
        ref[:, C : C + Q] = upper + pltpu.roll(fine - upper.astype(F32), 64, 1).astype(BF)
        io.put("b%d" % k)


def last_kernel(io, dno, dnr, do_s, d0, inv_s, xT, out, x_s, sems):
    T = xT.shape[1]
    half = dno.shape[0]
    own = pl.multiple_of(lax.axis_index("tensor") * half, half)

    def copy(k):
        return pltpu.make_async_copy(xT.at[pl.ds(own, half), lanes(k, 512)], x_s.at[:, lanes(k, 512)], sems.at[k])

    for k in range(T // 512):
        copy(k).start()

    def arrive(k):
        copy(k).wait()
        for n in ("dno", "dnr", "do_s"):
            io.need(n, k)

    @pairs(T // 256, arrive, lambda k: io.put("out", k))
    def _(c):
        l = lanes(c, 256)
        inv = inv_s[0:1, l]
        sent = dnr[half : half + 16, l].astype(F32)
        k3 = inv * inv * (d0[0:1, l] + sent[0:1] + sent[1:2]) / D
        e2 = dno[:, l].astype(F32) + dnr[0:half, l].astype(F32)
        dx = inv * e2 - x_s[:, l].astype(F32) * k3 + do_s[:, l].astype(F32)
        out[l, :] = dx.astype(BF).T


def finish_first_kernel(io, dealing, own, h0, h1, h2, h3, back, wo, wg, grad_in, *, full_len):
    share = h0.shape[0]
    C = wg.shape[1]
    place = lax.axis_index("dp") % 4
    mid = own[...].astype(F32)
    scale = full_len / (mid + pltpu.roll(mid, 64, 1))[0:1, 48:49]
    for k, ref in enumerate((h0, h1, h2, h3)):
        io.need("h%d" % k)
        r = pl.ds(pl.multiple_of((place ^ k) * share, share), share)
        wo[r, :] = ref[:, 0:D].astype(F32) * scale
        wg[r, :] = ref[:, D : D + C].astype(F32) * scale
    io.put("wo")
    io.put("wg")
    io.need("back")

    @pl.loop(0, grad_in.shape[0])
    def _(k):
        grad_in[dealing[k]] = (back[k].astype(F32) * scale).astype(BF)

    io.put("grad_in")


def finish_kernel(
    io, g0, g1, g2, g3,
    gv, gt, gs, ng, cv, vb, cst, sb, dl, sk, og, bias,
    sm, *, full_len
):
    share = g0.shape[0]
    C = gv.shape[1]
    HH = C // PS
    place = lax.axis_index("dp") % 4
    scale = None
    for k, ref in enumerate((g0, g1, g2, g3)):
        r = pl.ds(pl.multiple_of((place ^ k) * share, share), share)
        io.need("g%d" % k)
        mid = ref[:, C : C + Q].astype(F32)
        mid = mid + pltpu.roll(mid, 64, 1)
        scale = full_len / mid[0:1, 48:49]
        sm[r, :] = mid * scale
        gv[r, :] = ref[:, 0:C].astype(F32) * scale
        gs[r, :] = ref[:, C + Q : C + Q + 256].astype(F32) * scale
    io.put("gv")
    io.put("gs")
    scaled = sm[...]
    gt[...] = scaled[:, 0 : 2 * HH]
    turned = scaled.T
    ng[...] = turned[41]
    cv[...] = turned[32:36]
    vb[...] = turned[36]
    cst[...] = turned[42:46, 0:256]
    sb[...] = turned[46, 0:256]
    og[...] = turned[38]
    dl[...] = turned[40, 0:HH] + turned[40, HH : 2 * HH]
    bias[0:1, :] = turned[39:40, 0:HH]
    bias[1:2, :] = turned[39:40, HH : 2 * HH]
    sk[...] = turned[37, 0:HH]


class Flow:
    def __init__(self, sems):
        self.sems, self.table, self.used = sems, {}, 0

    def add(self, name, src, dst, axis, count):
        self.table[name] = (src, dst, axis, count, self.used)
        self.used += count

    def copy(self, name, piece):
        src, dst, axis, count, first = self.table[name]
        if count > 1:
            width = src.shape[axis] // count
            at = pl.ds(pl.multiple_of(piece * width, width), width)
            where = (at,) if axis == 0 else (slice(None), at)
            src, dst = src.at[where], dst.at[where]
        return pltpu.make_async_copy(src, dst, self.sems.at[first + piece])

    def put(self, name, piece=0):
        self.copy(name, piece).start()

    def need(self, name, piece=0):
        self.copy(name, piece).wait()


def call(body, outs, scratch, args, smem, name, us=1.0, late=None, early=None, raw=(), limit=58, static=None):
    late, early = late or {}, early or {}
    kinds = [pltpu.VMEM(*x) if isinstance(x, tuple) else x for x in scratch]
    names = list(inspect.signature(body).parameters)[1:]
    body = functools.partial(body, **static) if static else body
    n_in, n_out, n_own = len(args), len(outs), len(scratch)
    late_at = {n: names.index(n) for n in late}
    early_at = {n: names.index(n) - n_in for n in early}
    total = sum(c for _, c in late.values()) + sum(c for _, c in early.values())

    def wrapped(*refs):
        refs = list(refs)
        sems = refs.pop() if total else None
        flow = Flow(sems)
        bufs = refs[n_in + n_out + n_own :]
        for n, buf in zip([*late, *early], bufs):
            if n in late:
                at = late_at[n]
                flow.add(n, refs[at], buf, *late[n])
            else:
                at = n_in + early_at[n]
                flow.add(n, buf, refs[at], *early[n])
            refs[at] = buf
        waiting = list(late)
        while waiting:
            count = late[waiting[0]][1]
            group = []
            while waiting and late[waiting[0]][1] == count:
                group.append(waiting.pop(0))
            for piece in range(count):
                for n in group:
                    flow.put(n, piece)
        body(flow, *refs[: n_in + n_out + n_own])
        for n, (_, count) in early.items():
            for piece in range(count):
                flow.need(n, piece)

    vmem, any_ = pltpu.VMEM, pl.ANY
    in_specs = [
        pl.BlockSpec(
            memory_space=pltpu.SMEM if i < smem else any_ if i in late_at.values() or names[i] in raw else vmem
        )
        for i in range(n_in)
    ]
    out_specs = [
        pl.BlockSpec(memory_space=any_ if i in early_at.values() or names[n_in + i] in raw else vmem)
        for i in range(n_out)
    ]
    bufs = [pltpu.VMEM(args[late_at[n]].shape, args[late_at[n]].dtype) for n in late]
    bufs += [pltpu.VMEM(*outs[early_at[n]]) for n in early]
    return pl.pallas_call(
        wrapped,
        out_shape=[jax.ShapeDtypeStruct(s, d) for s, d in outs],
        in_specs=in_specs,
        out_specs=out_specs,
        scratch_shapes=kinds
        + bufs
        + ([pltpu.SemaphoreType.DMA((total,))] if total else []),
        compiler_params=pltpu.CompilerParams(vmem_limit_bytes=limit * 1024 * 1024),
        cost_estimate=pl.CostEstimate(
            flops=int(us * 9e8), bytes_accessed=int(us * 3e6), transcendentals=0
        ),
        name=name,
    )(*args)


def swap(x):
    return lax.ppermute(x, "tensor", [(0, 1), (1, 0)])


def across(x, groups, bit):
    return lax.ppermute(x, "dp", [(i, i ^ bit) for i in range(groups)])


def phases_of(groups):
    found, weight = [], 1
    while weight < groups:
        members = min(4, groups // weight)
        found.append((weight, members))
        weight *= members
    return found


def send_round(blocks, groups, weight):
    return [blocks[0]] + [across(b, groups, k * weight) for k, b in enumerate(blocks) if k]


def resplit(x, at):
    value = x[:, at : at + 64] + x[:, at + 64 : at + 128]
    upper = lax.reduce_precision(value, 8, 7)
    return jnp.concatenate([x[:, :at], upper, value - upper, x[:, at + 128 :]], 1)


def split(x, rank, weight, members):
    rows = x.shape[0] // members
    place = (rank // weight) % members
    return [lax.dynamic_slice_in_dim(x, (place ^ k) * rows, rows, 0) for k in range(members)]


def assemble(got, rank, weight):
    members = len(got)
    place = (rank // weight) % members
    parts = []
    for i in range(members):
        now = got[i]
        for p in range(1, members):
            now = jnp.where(place == p, got[i ^ p], now)
        parts.append(now)
    return jnp.concatenate(parts, 0)


def on_device(
    hidden_in, teacher, loss_mask, lengths, dealing, norm_gain, w_gate, w_value, w_state, w_step,
    step_bias, conv_value, conv_vbias, conv_state, conv_sbias, decay_log, skip_gain, out_gain, w_out,
):
    groups = lax.axis_size("dp")
    rank = lax.axis_index("dp")
    member = lax.axis_index("tensor")
    seqs, local, _ = hidden_in.shape
    half = teacher.shape[2]
    T = local * groups
    C = w_gate.shape[1]
    HH = decay_log.shape[0]
    CH = T // Q

    [dealt] = call(deal_kernel, [((seqs, local, half), BF)], [], (dealing, hidden_in), 1, "deal", 3.0)
    dealt, loss_mask, teacher, w_gate = lax.optimization_barrier((dealt, loss_mask, teacher, w_gate))
    xo = lax.all_to_all(dealt, "dp", split_axis=0, concat_axis=0, tiled=True).reshape(T, half)

    pos = rank * local + lax.broadcasted_iota(jnp.int32, (seqs, local), 1)
    marks = (loss_mask > 0) & (pos < lengths[:, None])
    count = jnp.sum(marks.astype(F32)).reshape(1)
    goal = jnp.where(marks[:, :, None], teacher, jnp.asarray(NOMARK, BF))
    [goal] = call(deal_kernel, [((seqs, local, half), BF)], [], (dealing, goal), 1, "deal_goal", 2.0)
    length = lax.dynamic_slice_in_dim(lengths, dealing[rank], 1, 0)

    wcat, wt, wot, cd = call(
        prepare_kernel,
        [((D, 2 * C + 384), BF), ((2 * C + 384, D), BF), ((D, C), BF), ((D, 8), F32)],
        [],
        (w_gate, w_value, w_state, w_step.reshape(D, 2 * HH), w_out, norm_gain[None]),
        0,
        "prepare",
        6.0,
        early={"wcat": (0, 1), "wt": (0, 1)},
    )
    zc = jnp.zeros((256,), F32)
    cc = jnp.concatenate(
        [
            jnp.concatenate([conv_value, conv_state], 1),
            jnp.concatenate([conv_vbias, conv_sbias])[None],
            jnp.concatenate([jnp.repeat(skip_gain, PS), zc])[None],
            jnp.concatenate([out_gain, zc])[None],
            jnp.zeros((1, C + 256), F32),
        ],
        0,
    ).T
    rate = -jnp.exp(decay_log)
    rc = jnp.stack([step_bias.reshape(-1), jnp.concatenate([rate, rate])], 1)

    xo, goal, wcat, wt, wot, cc, cd, rc, count, length = lax.optimization_barrier(
        (xo, goal, wcat, wt, wot, cc, cd, rc, count, length)
    )
    xs = swap(xo)
    to = lax.all_to_all(goal, "dp", split_axis=0, concat_axis=0, tiled=True).reshape(T, half)
    ts = swap(to)

    full = lambda n: ((n, T), BF)
    fullf = lambda n: ((n, T), F32)
    xT, nT, rows, dec, gate, u, pre, act, cs, e, mixed, sin, p0, inv = call(
        forward_kernel,
        [
            full(D), full(D), fullf(120), ((CH, 24, Q), F32), fullf(C), full(C + 256), full(C + 256),
            full(C + 256), full(128), ((CH, HH, Q, Q), BF), fullf(C), ((CH, C, Q), BF), full(D + 16), fullf(8),
        ],
        [
            ((C + 256, T), F32), ((32, T), F32), ((24, T), F32), ((CH, C, Q), F32), ((C, Q), F32),
            ((C, 2 * Q), BF), ((C, T), BF),
        ],
        (length, xo, xs, wt, wot, cc, cd, rc),
        1,
        "forward",
        26.0,
        late={"xo": (0, CH // 2), "xs": (0, CH // 2), "wt": (0, 1), "cc": (0, 1), "wot": (0, 1)},
        early={
            **{n: (0, 1) for n in ("xT", "nT", "rows", "dec", "gate", "uO", "preO", "act", "cs", "sin")},
            "mixed": (1, CH // 2),
            "eO": (0, CH // 2), "pO": (1, T // 256),
        },
    )
    p1 = swap(p0)
    lo, doh, dyT, dgate, small, *mids = call(
        middle_kernel,
        [((T, half), BF), full(half), full(C), full(C), ((C, Q), F32)] + [((D // 4, D + C), BF)] * 4,
        [
            ((D, Q), F32), ((D, Q), F32), ((C, T), BF), ((C, 256), F32), ((8, T), F32), ((C, Q), F32),
            ((8, T), F32), full(D),
        ],
        (p0, p1, xT, to, ts, w_out, nT, gate, mixed, cc),
        0,
        "middle",
        14.0,
        late={
            **{n: (1, CH // 2) for n in ("p0", "p1", "xT")}, "to": (0, CH // 2), "ts": (0, CH // 2),
            "wo": (0, 1), "cc": (0, 1), "gate": (1, T // 256), "mixed": (1, T // 256), "nT": (0, 1),
        },
        early={
            "dyT": (1, T // 256), **{n: (0, 1) for n in ("doh", "lo", "dgate", "m0", "m1", "m2", "m3")},
        },
    )
    phases = phases_of(groups)
    got_m = send_round(mids, groups, 1)
    rowsf = ((24, T), F32)
    width = C + Q + 256
    b0, b1, b2, b3, dno, dnx, dots = call(
        backward_kernel,
        [((D // 4, width), BF)] * 4 + [full(half), full(half + 16), fullf(8)],
        [
            ((D, Q), F32), rowsf, fullf(C + 256), rowsf, rowsf, rowsf, rowsf, ((CH, HH, Q), F32), ((CH, C, Q), F32),
            ((CH, C, Q), BF), ((C, Q), F32), ((C, 2 * Q), BF), ((C, 2 * Q), BF), ((C, Q), F32), rowsf,
            ((C + 256, 5 * Q), F32), full(2 * C + 384), ((D, 256), F32),
        ],
        (length, count, act, cs, rows, dec, e, sin, dyT, u, pre, dgate, nT, wcat, cc, cd, rc, small),
        2,
        "backward",
        30.0,
        late={
            **{n: (0, 1) for n in ("rows", "cs")},
            "dyT": (1, CH // 2),
            **{n: (0, 1) for n in ("dec", "sin", "act", "cc")},
            "e_in": (0, CH // 2),
            **{n: (0, 1) for n in ("dgate", "u_in", "pre_in", "small", "nT", "wcat", "cd")},
        },
        early={
            "dno": (1, T // 256), "dnx": (1, T // 256), **{n: (0, 1) for n in ("b0", "b1", "b2", "b3")},
        },
    )
    now_m = sum(g.astype(F32) for g in got_m)
    dnr = swap(dnx)
    now_m, dnr = lax.optimization_barrier((now_m, dnr))
    blocks = split(now_m, rank, *phases[1])
    got_m = send_round([b if k == 0 else b.astype(BF) for k, b in enumerate(blocks)], groups, phases[1][0])
    got = send_round([b0, b1, b2, b3], groups, 1)
    [dx] = call(
        last_kernel,
        [((T, half), BF)],
        [((half, T), BF), pltpu.SemaphoreType.DMA((CH,))],
        (dno, dnr, doh, dots, inv, xT),
        0,
        "last",
        3.0,
        late={n: (1, T // 512) for n in ("dno", "dnr", "do_s")},
        early={"out": (0, T // 512)},
        raw=("xT",),
    )
    dx, got, got_m = lax.optimization_barrier((dx, got, got_m))
    held = sum(g.astype(F32) for g in got_m)
    for weight, members in phases[2:]:
        blocks = split(held, rank, weight, members)
        got_m = send_round([b if k == 0 else b.astype(BF) for k, b in enumerate(blocks)], groups, weight)
        held = sum(g.astype(F32) for g in got_m)
    held = held.astype(BF)
    now = resplit(sum(g.astype(F32) for g in got), C)
    for weight, members in reversed(phases[1:]):
        pieces = send_round([held] * members, groups, weight)
        now, pieces = lax.optimization_barrier((now, pieces))
        held = assemble(pieces, rank, weight)
    held = send_round([held] * 4, groups, 1)
    for weight, members in phases[1:]:
        blocks = split(now, rank, weight, members)
        got = send_round([b if k == 0 else b.astype(BF) for k, b in enumerate(blocks)], groups, weight)
        now = resplit(sum(g.astype(F32) for g in got), C)
    lane = lax.broadcasted_iota(jnp.int32, (1, Q + 256), 1)
    both = (lane >= Q) | ((lane % 64 >= 41) & (lane % 64 < 47))
    tail = now[:, C:]
    tail = resplit(tail + jnp.where(both, swap(tail.astype(BF)).astype(F32), 0.0), 0)
    now = jnp.concatenate([now[:, :C], tail], 1).astype(BF)
    now, held = lax.optimization_barrier((now, held))
    for weight, members in reversed(phases[1:]):
        now = assemble(send_round([now] * members, groups, weight), rank, weight)
    back = lax.all_to_all(dx.reshape(seqs, local, half), "dp", split_axis=0, concat_axis=0, tiled=True)
    now, back = lax.optimization_barrier((now, back))
    got = send_round([now] * 4, groups, 1)
    wo, wg, grad_in = call(
        finish_first_kernel,
        [((C, D), F32), ((D, C), F32), ((seqs, local, half), BF)],
        [],
        (dealing, now[0:8, C : C + Q], *held, back),
        1,
        "finish_first",
        5.0,
        late={n: (0, 1) for n in ("h0", "h1", "h2", "h3", "back")},
        early={n: (0, 1) for n in ("wo", "wg", "grad_in")},
        static={"full_len": T},
    )
    gv, gt, gs, ng, cv, vb, cst, sb, dl, sk, og, bias = call(
        finish_kernel,
        [
            ((D, C), F32), ((D, 2 * HH), F32), ((D, 256), F32), ((D,), F32), ((4, C), F32), ((C,), F32),
            ((4, 256), F32), ((256,), F32), ((HH,), F32), ((HH,), F32), ((C,), F32), ((2, HH), F32),
        ],
        [((D, Q), F32)],
        tuple(got),
        0,
        "finish",
        4.0,
        late={n: (0, 1) for n in ("g0", "g1", "g2", "g3")},
        early={n: (0, 1) for n in ("gv", "gs")},
        static={"full_len": T},
    )
    return (
        lo[None], grad_in, ng, wg, gv, gs, gt.reshape(D, 2, HH), bias, cv, vb, cst, sb, dl, sk, og, wo,
    )


def solution(mesh):
    dp, tp = "dp", "tensor"
    return jax.shard_map(
        on_device,
        mesh=mesh,
        in_specs=(
            P(None, dp, None), P(None, dp, tp), P(None, dp), P(), P(), P(), P(None, tp), P(None, tp), P(),
            P(None, None, tp), P(None, tp), P(None, tp), P(tp), P(), P(), P(tp), P(tp), P(tp), P(tp, None),
        ),
        out_specs=(
            P(dp, None, tp), P(None, dp, tp), P(), P(None, tp), P(None, tp), P(), P(None, None, tp),
            P(None, tp), P(None, tp), P(tp), P(), P(), P(tp), P(tp), P(tp), P(tp, None),
        ),
        check_vma=False,
    )
```

```python
import functools
import inspect

import jax
import jax.numpy as jnp
from jax import lax
from jax.experimental import pallas as pl
from jax.experimental.pallas import tpu as pltpu
from jax.sharding import PartitionSpec as P

D = 768
INNER = 1536
PS = 64
N = 64
Q = 128
EPS = 1e-5
NOMARK = 256.0
BF = jnp.bfloat16
F32 = jnp.float32
HI = lax.Precision.HIGHEST


def pairs(count, before=None, after=None):
    def run(body):
        @pl.loop(0, count // 2)
        def _(k):
            if before:
                before(k)
            body(2 * k)
            body(2 * k + 1)
            if after:
                after(k)

    return run


ROWS = 64

NN = (((1,), (0,)), ((), ()))
NT = (((1,), (1,)), ((), ()))


def mm(a, b, dims=NN):
    return lax.dot_general(a, b, dims, preferred_element_type=F32)


def mm_hi(a, b):
    return lax.dot_general(a, b, NN, precision=HI, preferred_element_type=F32)


def lanes(c, width=Q):
    return pl.ds(pl.multiple_of(c * width, width), width)


def iota2(shape, dim):
    return lax.broadcasted_iota(jnp.int32, shape, dim)


def log1p_exp(z):
    w = 1.0 + z
    return jnp.where(w == 1.0, z, jnp.log(w) * (z / jnp.where(w == 1.0, 1.0, w - 1.0)))


RAW, DT, CUM, CUE, ROWV = 0, 24, 48, 72, 96


def deal_kernel(io, dealing, src, dst):
    count, _, width = dst.shape
    if src.shape[2] == width:
        col = pl.ds(0, width)
    else:
        col = pl.ds(pl.multiple_of(lax.axis_index("tensor") * width, width), width)

    @pl.loop(0, count)
    def _(j):
        dst[j] = src[dealing[j], :, col]


def prepare_kernel(io, wg, wv, ws, wst, wo, ng, wcat, wt, wot, cd):
    C = wg.shape[1]
    W = 2 * C + 256
    wcat[:, 0:C] = wg[...]
    wcat[:, C : 2 * C] = wv[...]
    wcat[:, 2 * C : W] = ws[...]
    wcat[:, W : W + Q] = jnp.concatenate([wst[...], jnp.zeros((D, Q - wst.shape[1]), BF)], 1)
    io.put("wcat")

    @pl.loop(0, (W + Q) // Q)
    def _(c):
        wt[lanes(c), :] = wcat[:, lanes(c)].astype(F32).T.astype(BF)

    io.put("wt")

    @pl.loop(0, D // Q)
    def _(c):
        wot[lanes(c), :] = wo[:, lanes(c)].astype(F32).T.astype(BF)

    cd[...] = jnp.broadcast_to(ng[...], (8, D)).T


def forward_kernel(
    io, length, xo, xs, wt, wot, cc, cd, rc,
    xT, nT, rows, dec, gate, uO, preO, act, cs, eO, mixed, sin, pO, inv_o,
    u_s, raw_s, w_s, dS, run, vw, bu,
):
    T = xo.shape[0]
    CH = T // Q
    C = gate.shape[0]
    HH = C // PS
    half = xo.shape[1]
    m = lax.axis_index("tensor")
    own = pl.multiple_of(m * half, half)
    other = pl.multiple_of((1 - m) * half, half)

    def arrive(k):
        io.need("xo", k)
        io.need("xs", k)

    @pairs(CH, arrive)
    def _(c):
        l = lanes(c)
        xT[pl.ds(own, half), l] = xo[l, :].astype(F32).T.astype(BF)
        xT[pl.ds(other, half), l] = xs[l, :].astype(F32).T.astype(BF)
        x = xT[:, l].astype(F32)
        inv = lax.rsqrt(jnp.sum(x * x, 0, keepdims=True) / D + EPS)
        inv_o[:, l] = jnp.broadcast_to(inv, (8, Q))
        nT[:, l] = (x * inv * cd[:, 0:1]).astype(BF)

    io.put("xT")
    io.put("nT")
    io.need("wt")

    @pl.loop(0, T // 256, unroll=2)
    def _(j):
        l = lanes(j, 256)
        n = nT[:, l]
        gate[:, l] = mm(wt[0:C, :], n)
        u_s[:, l] = mm(wt[C : 2 * C + 256, :], n)
        raw_s[:, l] = mm(wt[2 * C + 256 : 2 * C + 288, :], n)

    io.put("gate")

    raw = raw_s[0:24, :] + rc[:, 0:1]
    live = (iota2((1, T), 1) < length[0]).astype(F32)
    dt = (jnp.maximum(raw, 0.0) + log1p_exp(jnp.exp(-jnp.abs(raw)))) * live
    la = dt * rc[:, 1:2]
    rows[RAW : RAW + 24, :] = raw
    rows[DT : DT + 24, :] = dt
    upper = (iota2((Q, Q), 0) <= iota2((Q, Q), 1)).astype(F32)
    lower = (iota2((Q, Q), 0) >= iota2((Q, Q), 1)).astype(F32)
    stacked = jnp.concatenate([la[:, c * Q : (c + 1) * Q] for c in range(CH)], 0)
    cum_f = mm_hi(stacked, upper)
    cum_b = mm_hi(stacked, lower)
    first = iota2((24, Q), 0) < HH
    for c in range(CH):
        r = slice(24 * c, 24 * c + 24)
        k = slice(Q * c, Q * c + Q)
        cum = jnp.where(first, cum_f[r], cum_b[r])
        dtc = dt[:, k]
        rows[CUM : CUM + 24, k] = cum
        rows[CUE : CUE + 24, k] = cum - la[:, k]
        rows[ROWV : ROWV + 24, k] = jnp.where(
            dtc > 0.0, cum - jnp.log(jnp.where(dtc > 0.0, dtc, 1.0)), 1e30
        )
        tot = jnp.broadcast_to(jnp.sum(la[:, k], 1, keepdims=True), (24, Q))
        dec[c] = jnp.exp(tot)
        w_s[:, k] = jnp.exp(tot - cum) * dtc

    io.put("rows")
    io.put("dec")
    io.need("cc")

    at = iota2((ROWS, Q), 1)

    @pl.loop(0, u_s.shape[0] // ROWS, unroll=2)
    def _(b):
        r = pl.ds(pl.multiple_of(b * ROWS, ROWS), ROWS)
        col = cc[r, :]
        ks = [jnp.broadcast_to(col[:, k : k + 1], (ROWS, Q)) for k in range(5)]
        earlier = [jnp.zeros((ROWS, Q), F32)] * 4
        for c in range(CH):
            l = slice(c * Q, c * Q + Q)
            uu = u_s[r, l]
            pre = ks[4] + ks[3] * uu
            for back in (1, 2, 3):
                moved = pltpu.roll(uu, back, 1)
                pre = pre + ks[3 - back] * jnp.where(at >= back, moved, earlier[back])
                earlier[back] = moved
            uO[r, l] = uu.astype(BF)
            preO[r, l] = pre.astype(BF)
            act[r, l] = (pre * jax.nn.sigmoid(pre)).astype(BF)

    cs[0:64, :] = pltpu.roll(act[C + 64 : C + 128, :].astype(F32), 1, 1).astype(BF)
    cs[64:128, :] = pltpu.roll(act[C + 192 : C + 256, :].astype(F32), T - 1, 1).astype(BF)

    io.put("uO")
    io.put("preO")
    io.put("act")
    io.put("cs")

    zeros = jnp.zeros((64, Q), BF)

    @pairs(CH)
    def _(c):
        l = lanes(c)
        for h in range(HH):
            v = act[64 * h : 64 * h + 64, l].astype(F32)
            vw[64 * h : 64 * h + 64, 0:Q] = (v * w_s[h : h + 1, l]).astype(BF)
            vw[64 * h : 64 * h + 64, Q : 2 * Q] = (v * w_s[HH + h : HH + h + 1, l]).astype(BF)
        both = jnp.concatenate(
            [
                jnp.concatenate([act[C : C + 64, l], zeros], 1),
                jnp.concatenate([zeros, act[C + 128 : C + 192, l]], 1),
            ],
            0,
        )
        dS[c] = mm(vw[...], both, NT)

    run[...] = jnp.zeros_like(run)
    low = iota2((64, Q), 1) < 64
    low_h = iota2((HH, Q), 1) < 64

    @pairs(CH)
    def _(i):
        d = jnp.where(low_h, dec[i][0:HH], dec[CH - 1 - i][HH : 2 * HH])
        for h in range(HH):
            r = slice(64 * h, 64 * h + 64)
            now = run[r, :]
            sin[i, r, :] = now.astype(BF)
            run[r, :] = now * d[h : h + 1] + jnp.where(low, dS[i, r, :], dS[CH - 1 - i, r, :])

    io.put("sin")

    before = iota2((Q, Q), 1) < iota2((Q, Q), 0)
    after = iota2((Q, Q), 1) > iota2((Q, Q), 0)
    top = iota2((Q, Q), 0) < 64

    def leave(k):
        io.put("eO", k)
        io.put("mixed", k)

    @pairs(CH, after=leave)
    def _(c):
        l = lanes(c)
        bf = act[C : C + 64, l]
        bb = act[C + 128 : C + 192, l]
        cf = cs[0:64, l]
        cb = cs[64:128, l]
        gf = mm(cf.astype(F32).T.astype(BF), bf)
        gb = mm(cb.astype(F32).T.astype(BF), bb)
        g = jnp.where(before, gf, jnp.where(after, gb, 0.0))
        cue = rows[CUE : CUE + 24, l]
        cols = jnp.concatenate([cue, jnp.zeros((Q - 24, Q), F32)], 0).T
        ecue = jnp.exp(cue)
        zc = jnp.zeros((64, Q), BF)
        yf = mm(sin[c], jnp.concatenate([cf, zc], 0))
        yb = mm(sin[CH - 1 - c], jnp.concatenate([zc, cb], 0))
        total = jnp.zeros((1, Q), F32)
        for j in range(HH // 2):
            ms = []
            for h in (2 * j, 2 * j + 1):
                gap = jnp.where(
                    before,
                    cols[:, h : h + 1] - rows[ROWV + h : ROWV + h + 1, l],
                    cols[:, HH + h : HH + h + 1] - rows[ROWV + HH + h : ROWV + HH + h + 1, l],
                )
                e = jnp.exp(jnp.minimum(gap, 30.0))
                eO[c, h] = e.astype(BF)
                ms.append((e * g).astype(BF))
            v = act[128 * j : 128 * j + 128, l]
            vz = jnp.zeros_like(v)
            pair = jnp.concatenate([jnp.where(top, v, vz), jnp.where(top, vz, v)], 1)
            y = mm(pair, jnp.concatenate(ms, 1), NT)
            for k in (0, 1):
                h = 2 * j + k
                r = slice(64 * h, 64 * h + 64)
                mix = (
                    y[64 * k : 64 * k + 64]
                    + ecue[h : h + 1] * yf[r]
                    + ecue[HH + h : HH + h + 1] * yb[r]
                    + cc[r, 5:6] * v[64 * k : 64 * k + 64].astype(F32)
                )
                mixed[r, l] = mix
                gt = gate[r, l]
                gated = mix * (gt * jax.nn.sigmoid(gt))
                total = total + jnp.sum(gated * gated, 0, keepdims=True)
                bu[r, l] = (gated * cc[r, 6:7]).astype(BF)
        top_part = total.astype(BF).astype(F32)
        pO[D : D + 16, l] = jnp.where(
            iota2((16, Q), 0) == 0, top_part, jnp.where(iota2((16, Q), 0) == 1, total - top_part, 0.0)
        ).astype(BF)

    io.need("wot")

    @pl.loop(0, T // 256)
    def _(j):
        l = lanes(j, 256)
        pO[0:D, l] = mm(wot[...], bu[:, l]).astype(BF)
        io.put("pO", j)


def middle_kernel(
    io, p0, p1, xT, to, ts, wo, nT, gate, mixed, cc,
    lo, doh, dyT, dgate, small, m0, m1, m2, m3,
    res_s, tea_s, branch, dbr, dot_s, acc_g, q_s, doT,
):
    T = to.shape[0]
    CH = T // Q
    C = gate.shape[0]
    half = to.shape[1]
    m = lax.axis_index("tensor")
    own = pl.multiple_of(m * half, half)
    other = pl.multiple_of((1 - m) * half, half)

    def arrive(k):
        for n in ("p0", "p1", "xT", "to", "ts"):
            io.need(n, k)

    @pairs(CH, arrive)
    def _(c):
        l = lanes(c)
        tea_s[pl.ds(own, half), :] = to[l, :].astype(F32).T
        tea_s[pl.ds(other, half), :] = ts[l, :].astype(F32).T
        pt = p0[0:D, l].astype(F32) + p1[0:D, l].astype(F32)
        sums = p0[D : D + 16, l].astype(F32) + p1[D : D + 16, l].astype(F32)
        q = lax.rsqrt((sums[0:1] + sums[1:2]) / INNER + EPS)
        q_s[:, l] = jnp.broadcast_to(q, (8, Q))
        res = xT[:, l].astype(F32) + q * pt
        res_s[...] = res
        tea = tea_s[...]
        do = jnp.where(tea < 0.5 * NOMARK, res - tea, 0.0).astype(BF)
        doT[:, l] = do
        dot_s[:, l] = jnp.broadcast_to(jnp.sum(do.astype(F32) * pt, 0, keepdims=True), (8, Q))
        lo[l, :] = res_s[pl.ds(own, half), :].T.astype(BF)
        doh[:, l] = doT[pl.ds(own, half), l]

    io.put("doh")
    io.put("lo")
    acc_g[...] = jnp.zeros_like(acc_g)

    for n in ("wo", "cc"):
        io.need(n)

    @pl.loop(0, T // 256)
    def _(j):
        l = lanes(j, 256)
        io.need("gate", j)
        io.need("mixed", j)
        dbr[...] = mm(wo[...], doT[:, l])
        q = q_s[0:1, l]
        q3 = q * q * q * dot_s[0:1, l] / INNER

        @pl.loop(0, C // 64, unroll=2)
        def _(b):
            r = pl.ds(pl.multiple_of(b * 64, 64), 64)
            gain = jnp.broadcast_to(cc[r, 6:7], (64, Q))
            acc = acc_g[r, :]
            for t in (0, 1):
                k = slice(t * Q, t * Q + Q)
                l1 = pl.ds(pl.multiple_of(j * 256 + t * Q, Q), Q)
                d = dbr[r, k]
                g = gate[r, l1]
                mix = mixed[r, l1]
                sg = jax.nn.sigmoid(g)
                si = g * sg
                gated = mix * si
                gq = gated * q[:, k]
                branch[r, l1] = (gq * gain).astype(BF)
                acc = acc + d * gq
                dgt = q[:, k] * (d * gain) - gated * q3[:, k]
                dyT[r, l1] = (dgt * si).astype(BF)
                dgate[r, l1] = (dgt * mix * (sg * (1.0 + g * (1.0 - sg)))).astype(BF)
            acc_g[r, :] = acc

        io.put("dyT", j)

    io.put("dgate")
    io.need("nT")
    place = lax.axis_index("dp") % 4
    share = m0.shape[0]
    for k, ref in enumerate((m0, m1, m2, m3)):
        r = pl.ds(pl.multiple_of((place ^ k) * share, share), share)
        ref[:, 0:D] = mm(branch[r, :], doT[...], NT).astype(BF)
        ref[:, D : D + C] = mm(nT[r, :], dgate[...], NT).astype(BF)
        io.put("m%d" % k)
    small[...] = jnp.where(iota2((C, Q), 1) == 38, jnp.sum(acc_g[...], 1, keepdims=True), 0.0)


def backward_kernel(
    io, length, count, act, cs, rows, dec, e_in, sin, dyT, u_in, pre_in, dgate, nT, wcat, cc, cd, rc, small,
    b0, b1, b2, b3, dno, dnx, dots,
    acc, sk_rows, dact, c_rows, r_rows, ci_rows, ri_rows, kk, dA, ain, run, vw, dye, small_s, dla_s, sums, dproj, dn_s,
):
    T = act.shape[1]
    CH = T // Q
    C = dyT.shape[0]
    HH = C // PS
    zeros = jnp.zeros((64, Q), BF)

    io.need("rows")
    io.need("cs")

    @pairs(CH, lambda k: io.need("dyT", k))
    def _(c):
        l = lanes(c)
        ecue = jnp.exp(rows[CUE : CUE + 24, l])
        for h in range(HH):
            dy = dyT[64 * h : 64 * h + 64, l].astype(F32)
            dye[64 * h : 64 * h + 64, 0:Q] = (dy * ecue[h : h + 1]).astype(BF)
            dye[64 * h : 64 * h + 64, Q : 2 * Q] = (dy * ecue[HH + h : HH + h + 1]).astype(BF)
        both = jnp.concatenate(
            [
                jnp.concatenate([cs[0:64, l], zeros], 1),
                jnp.concatenate([zeros, cs[64:128, l]], 1),
            ],
            0,
        )
        dA[c] = mm(dye[...], both, NT)

    io.need("dec")
    io.need("sin")
    run[...] = jnp.zeros_like(run)
    low = iota2((64, Q), 1) < 64
    low_h = iota2((HH, Q), 1) < 64

    @pl.loop(0, CH)
    def _(i):
        f = CH - 1 - i
        d = jnp.where(low_h, dec[f][0:HH], dec[i][HH : 2 * HH])
        for h in range(HH):
            r = slice(64 * h, 64 * h + 64)
            now = run[r, :]
            ain[i, r, :] = now.astype(BF)
            flow = jnp.sum(now * sin[f, r, :].astype(F32), 0, keepdims=True) * d[h : h + 1]
            kk[i, h : h + 1, :] = flow
            run[r, :] = now * d[h : h + 1] + jnp.where(low, dA[f, r, :], dA[i, r, :])

    io.need("act")
    io.need("cc")
    sk_rows[...] = jnp.zeros_like(sk_rows)
    before = iota2((Q, Q), 1) < iota2((Q, Q), 0)
    after = iota2((Q, Q), 1) > iota2((Q, Q), 0)
    left = iota2((Q, Q), 1) < 64
    top = iota2((Q, Q), 0) < 64
    lane = iota2((Q, Q), 1)

    @pl.loop(0, CH)
    def _(c):
        l = lanes(c)

        @pl.when(c % 2 == 0)
        def _():
            io.need("e_in", c // 2)

        bf = act[C : C + 64, l]
        bb = act[C + 128 : C + 192, l]
        cf = cs[0:64, l]
        cb = cs[64:128, l]
        gf = mm(cf.astype(F32).T.astype(BF), bf)
        gb = mm(cb.astype(F32).T.astype(BF), bb)
        g = jnp.where(before, gf, jnp.where(after, gb, 0.0))
        ecue = jnp.exp(rows[CUE : CUE + 24, l])
        w = jnp.exp(
            jnp.where(
                iota2((24, Q), 0) < HH,
                rows[CUM : CUM + 24, l][:, Q - 1 : Q],
                rows[CUM : CUM + 24, l][:, 0:1],
            )
            - rows[CUM : CUM + 24, l]
        ) * rows[DT : DT + 24, l]
        for h in range(HH):
            r = slice(64 * h, 64 * h + 64)
            dy = dyT[r, l].astype(F32)
            v = act[r, l].astype(F32)
            dye[r, 0:Q] = (dy * ecue[h : h + 1]).astype(BF)
            dye[r, Q : 2 * Q] = (dy * ecue[HH + h : HH + h + 1]).astype(BF)
            vw[r, 0:Q] = (v * w[h : h + 1]).astype(BF)
            vw[r, Q : 2 * Q] = (v * w[HH + h : HH + h + 1]).astype(BF)
        zc = jnp.zeros((64, Q), BF)
        sf = sin[c]
        sb = sin[CH - 1 - c]
        af = ain[CH - 1 - c]
        ab = ain[c]
        yf = mm(sf, jnp.concatenate([cf, zc], 0))
        yb = mm(sb, jnp.concatenate([zc, cb], 0))
        vf = mm(af, jnp.concatenate([bf, zc], 0))
        vb = mm(ab, jnp.concatenate([zc, bb], 0))
        dcf = mm(sf.astype(F32).T.astype(BF)[0:64], dye[:, 0:Q])
        dcb = mm(sb.astype(F32).T.astype(BF)[64:128], dye[:, Q : 2 * Q])
        dbf = mm(af.astype(F32).T.astype(BF)[0:64], vw[:, 0:Q])
        dbb = mm(ab.astype(F32).T.astype(BF)[64:128], vw[:, Q : 2 * Q])
        dg = jnp.zeros((Q, Q), F32)
        rc_cols = jnp.zeros((Q, Q), F32)
        for j in range(HH // 2):
            r2 = slice(128 * j, 128 * j + 128)
            v = act[r2, l]
            dy = dyT[r2, l]
            dy_f = dy.astype(F32)
            dyt = dy_f.T.astype(BF)
            zb = jnp.zeros_like(dyt)
            dm2 = mm(jnp.concatenate([jnp.where(left, dyt, zb), jnp.where(left, zb, dyt)], 0), v)
            ms = []
            for k in (0, 1):
                h = 2 * j + k
                e = e_in[c, h].astype(F32)
                x = e * dm2[Q * k : Q * k + Q]
                dg = dg + x
                t = x * g
                tf = jnp.where(before, t, 0.0)
                ms.append((e * g).astype(BF))
                c_all = jnp.sum(t, 0, keepdims=True)
                c_f = jnp.sum(tf, 0, keepdims=True)
                c_rows[h : h + 1, l] = c_f
                c_rows[HH + h : HH + h + 1, l] = c_all - c_f
                r_all = jnp.sum(t, 1, keepdims=True)
                r_f = jnp.sum(tf, 1, keepdims=True)
                rc_cols = jnp.where(lane == h, r_f, rc_cols)
                rc_cols = jnp.where(lane == HH + h, r_all - r_f, rc_cols)
            dv = mm(
                jnp.concatenate([jnp.where(top, dy, zb), jnp.where(top, zb, dy)], 1),
                jnp.concatenate(ms, 0),
            )
            for k in (0, 1):
                h = 2 * j + k
                r = slice(64 * h, 64 * h + 64)
                v1 = v[64 * k : 64 * k + 64].astype(F32)
                dy1 = dy_f[64 * k : 64 * k + 64]
                sk_rows[h : h + 1, l] = jnp.sum(v1 * dy1, 0, keepdims=True)
                f_in = vf[r] * w[h : h + 1]
                b_in = vb[r] * w[HH + h : HH + h + 1]
                ci_rows[h : h + 1, l] = jnp.sum(f_in * v1, 0, keepdims=True)
                ci_rows[HH + h : HH + h + 1, l] = jnp.sum(b_in * v1, 0, keepdims=True)
                ri_rows[h : h + 1, l] = jnp.sum(yf[r] * dy1, 0, keepdims=True) * ecue[h : h + 1]
                ri_rows[HH + h : HH + h + 1, l] = (
                    jnp.sum(yb[r] * dy1, 0, keepdims=True) * ecue[HH + h : HH + h + 1]
                )
                dact[r, l] = dv[64 * k : 64 * k + 64] + f_in + b_in + cc[r, 5:6] * dy1
        r_rows[:, l] = rc_cols.T[0:24, :]
        dgf = jnp.where(before, dg, 0.0).astype(BF)
        dgb = jnp.where(after, dg, 0.0).astype(BF)
        dact[C : C + 64, l] = dbf + mm(cf, dgf)
        dact[C + 64 : C + 128, l] = dcf + mm(bf, dgf, NT)
        dact[C + 128 : C + 192, l] = dbb + mm(cb, dgb)
        dact[C + 192 : C + 256, l] = dcb + mm(bb, dgb, NT)

    dact[C + 64 : C + 128, :] = pltpu.roll(dact[C + 64 : C + 128, :], T - 1, 1)
    dact[C + 192 : C + 256, :] = pltpu.roll(dact[C + 192 : C + 256, :], 1, 1)

    ii, jj = iota2((Q, Q), 0), iota2((Q, Q), 1)
    gt = (ii > jj).astype(F32)
    ge = (ii >= jj).astype(F32)
    lt = (ii < jj).astype(F32)
    le = (ii <= jj).astype(F32)
    first = iota2((24, Q), 0) < HH
    cat = lambda ref: jnp.concatenate([ref[:, c * Q : (c + 1) * Q] for c in range(CH)], 0)
    r_in, c_in, c_x, r_x = cat(r_rows), cat(c_rows), cat(ci_rows), cat(ri_rows)
    rt = r_in + r_x
    as_f = mm_hi(rt, gt) - mm_hi(c_in, ge) + mm_hi(c_x, lt)
    as_b = mm_hi(rt, lt) - mm_hi(c_in, le) + mm_hi(c_x, gt)
    for c in range(CH):
        k = slice(24 * c, 24 * c + 24)
        l = slice(Q * c, Q * c + Q)
        kf = jnp.sum(jnp.where(low_h, kk[CH - 1 - c], 0.0), 1, keepdims=True)
        kb = jnp.sum(jnp.where(low_h, 0.0, kk[c]), 1, keepdims=True)
        dla_s[0:HH, l] = as_f[k][0:HH] + kf
        dla_s[HH : 2 * HH, l] = as_b[k][HH : 2 * HH] + kb
    dla = dla_s[...]
    dt = rows[DT : DT + 24, :]
    rate = rc[:, 1:2]
    live = (iota2((1, T), 1) < length[0]).astype(F32)
    sig = jax.nn.sigmoid(rows[RAW : RAW + 24, :])
    direct = (c_rows[...] + ci_rows[...]) * jnp.where(dt > 0.0, sig / jnp.where(dt > 0.0, dt, 1.0), 0.0)
    draw = (direct + rate * dla * sig) * live
    g_bias = jnp.sum(draw, 1, keepdims=True)
    g_decay = jnp.sum(dla * dt, 1, keepdims=True) * rate
    g_skip = jnp.sum(sk_rows[...], 1, keepdims=True)
    io.need("dgate")
    dproj[0:C, :] = dgate[...]
    dproj[2 * C + 256 : 2 * C + 384, :] = jnp.concatenate([draw, jnp.zeros((104, T), F32)], 0).astype(BF)

    io.need("u_in")
    io.need("pre_in")
    at = iota2((ROWS, Q), 1)

    @pl.loop(0, (C + 256) // ROWS, unroll=2)
    def _(b):
        r = pl.ds(pl.multiple_of(b * ROWS, ROWS), ROWS)
        r_out = pl.ds(pl.multiple_of(b * ROWS + C, ROWS), ROWS)
        col = cc[r, :]
        ks = [jnp.broadcast_to(col[:, k : k + 1], (ROWS, Q)) for k in range(4)]
        later = [jnp.zeros((ROWS, Q), F32)] * 4
        totals = [jnp.zeros((ROWS, Q), F32)] * 5
        for c in reversed(range(CH)):
            l = slice(c * Q, c * Q + Q)
            pre = pre_in[r, l].astype(F32)
            sg = jax.nn.sigmoid(pre)
            dp = dact[r, l] * (sg * (1.0 + pre * (1.0 - sg)))
            uu = u_in[r, l].astype(F32)
            du = ks[3] * dp
            totals[4] = totals[4] + dp
            totals[3] = totals[3] + dp * uu
            for back in (1, 2, 3):
                moved = pltpu.roll(dp, Q - back, 1)
                ahead = jnp.where(at < Q - back, moved, later[back])
                later[back] = moved
                totals[3 - back] = totals[3 - back] + ahead * uu
                du = du + ks[3 - back] * ahead
            dproj[r_out, l] = du.astype(BF)
        for k in range(5):
            sums[r, k * Q : k * Q + Q] = totals[k]

    def lane_sums(part, first_lane):
        upper = part.astype(BF)
        lower = (part - upper.astype(F32)).astype(BF)
        pick = (iota2((5 * Q, Q), 0) // Q + first_lane == iota2((5 * Q, Q), 1)).astype(BF)
        return mm(upper, pick) + mm(lower, pick)

    io.need("small")
    small_s[0:C, :] = lane_sums(sums[0:C, :], 32) + small[...]
    small_s[0:256, :] += lane_sums(sums[C : C + 256, :], 42)
    head_lane = iota2((24, Q), 1)
    heads_part = jnp.where(head_lane == 39, g_bias, jnp.where(head_lane == 40, g_decay, 0.0))
    small_s[0:24, :] += jnp.where(head_lane == 37, g_skip, heads_part)
    counted = (iota2((8, Q), 1) == 48) & (iota2((8, Q), 0) == 0)
    for k in range(4):
        at_row = k * (D // 4)
        small_s[at_row : at_row + 8, :] += jnp.where(counted, count[0], 0.0)
    io.need("nT")
    io.need("wcat")
    io.need("cd")
    half = dno.shape[0]
    m = lax.axis_index("tensor")
    own = pl.multiple_of(m * half, half)
    other = pl.multiple_of((1 - m) * half, half)
    W = 2 * C + 256
    acc[...] = jnp.zeros_like(acc)

    @pl.loop(0, T // 256, unroll=2)
    def _(j):
        l = lanes(j, 256)
        dn = mm(wcat[...], dproj[:, l])
        dn_s[...] = dn * cd[:, 0:1]
        part = dn * nT[:, l].astype(F32)
        acc[...] += part[:, 0:Q] + part[:, Q : 2 * Q]
        dot = jnp.sum(part, 0, keepdims=True)
        dots[:, l] = jnp.broadcast_to(dot, (8, 256))
        dno[:, l] = dn_s[pl.ds(own, half), :].astype(BF)
        dnx[0:half, l] = dn_s[pl.ds(other, half), :].astype(BF)
        top_part = dot.astype(BF).astype(F32)
        row = iota2((16, 256), 0)
        dnx[half : half + 16, l] = jnp.where(
            row == 0, top_part, jnp.where(row == 1, dot - top_part, 0.0)
        ).astype(BF)
        io.put("dno", j)
        io.put("dnx", j)

    wide = jnp.sum(acc[...], 1, keepdims=True) / cd[:, 0:1]
    small_s[...] += jnp.where(iota2((D, Q), 1) == 41, wide, 0.0)
    place = lax.axis_index("dp") % 4
    share = b0.shape[0]
    for k, ref in enumerate((b0, b1, b2, b3)):
        r = pl.ds(pl.multiple_of((place ^ k) * share, share), share)
        n = nT[r, :]
        ref[:, 0:C] = mm(n, dproj[C : 2 * C, :], NT).astype(BF)
        ref[:, C + Q : C + Q + 256] = mm(n, dproj[2 * C : W, :], NT).astype(BF)
        fine = mm(n, dproj[W : W + Q, :], NT) + small_s[r, :]
        upper = fine.astype(BF)
        ref[:, C : C + Q] = upper + pltpu.roll(fine - upper.astype(F32), 64, 1).astype(BF)
        io.put("b%d" % k)


def last_kernel(io, dno, dnr, do_s, d0, inv_s, xT, out, x_s, sems):
    T = xT.shape[1]
    half = dno.shape[0]
    own = pl.multiple_of(lax.axis_index("tensor") * half, half)

    def copy(k):
        return pltpu.make_async_copy(xT.at[pl.ds(own, half), lanes(k, 512)], x_s.at[:, lanes(k, 512)], sems.at[k])

    for k in range(T // 512):
        copy(k).start()

    def arrive(k):
        copy(k).wait()
        for n in ("dno", "dnr", "do_s"):
            io.need(n, k)

    @pairs(T // 256, arrive, lambda k: io.put("out", k))
    def _(c):
        l = lanes(c, 256)
        inv = inv_s[0:1, l]
        sent = dnr[half : half + 16, l].astype(F32)
        k3 = inv * inv * (d0[0:1, l] + sent[0:1] + sent[1:2]) / D
        e2 = dno[:, l].astype(F32) + dnr[0:half, l].astype(F32)
        dx = inv * e2 - x_s[:, l].astype(F32) * k3 + do_s[:, l].astype(F32)
        out[l, :] = dx.astype(BF).T


def finish_first_kernel(io, dealing, own, h0, h1, h2, h3, back, wo, wg, grad_in, *, full_len):
    share = h0.shape[0]
    C = wg.shape[1]
    place = lax.axis_index("dp") % 4
    mid = own[...].astype(F32)
    scale = full_len / (mid + pltpu.roll(mid, 64, 1))[0:1, 48:49]
    for k, ref in enumerate((h0, h1, h2, h3)):
        io.need("h%d" % k)
        r = pl.ds(pl.multiple_of((place ^ k) * share, share), share)
        wo[r, :] = ref[:, 0:D].astype(F32) * scale
        wg[r, :] = ref[:, D : D + C].astype(F32) * scale
    io.put("wo")
    io.put("wg")
    io.need("back")

    @pl.loop(0, grad_in.shape[0])
    def _(k):
        grad_in[dealing[k]] = (back[k].astype(F32) * scale).astype(BF)

    io.put("grad_in")


def finish_kernel(
    io, g0, g1, g2, g3,
    gv, gt, gs, ng, cv, vb, cst, sb, dl, sk, og, bias,
    sm, *, full_len
):
    share = g0.shape[0]
    C = gv.shape[1]
    HH = C // PS
    place = lax.axis_index("dp") % 4
    scale = None
    for k, ref in enumerate((g0, g1, g2, g3)):
        r = pl.ds(pl.multiple_of((place ^ k) * share, share), share)
        io.need("g%d" % k)
        mid = ref[:, C : C + Q].astype(F32)
        mid = mid + pltpu.roll(mid, 64, 1)
        scale = full_len / mid[0:1, 48:49]
        sm[r, :] = mid * scale
        gv[r, :] = ref[:, 0:C].astype(F32) * scale
        gs[r, :] = ref[:, C + Q : C + Q + 256].astype(F32) * scale
    io.put("gv")
    io.put("gs")
    scaled = sm[...]
    gt[...] = scaled[:, 0 : 2 * HH]
    turned = scaled.T
    ng[...] = turned[41]
    cv[...] = turned[32:36]
    vb[...] = turned[36]
    cst[...] = turned[42:46, 0:256]
    sb[...] = turned[46, 0:256]
    og[...] = turned[38]
    dl[...] = turned[40, 0:HH] + turned[40, HH : 2 * HH]
    bias[0:1, :] = turned[39:40, 0:HH]
    bias[1:2, :] = turned[39:40, HH : 2 * HH]
    sk[...] = turned[37, 0:HH]


class Flow:
    def __init__(self, sems):
        self.sems, self.table, self.used = sems, {}, 0

    def add(self, name, src, dst, axis, count):
        self.table[name] = (src, dst, axis, count, self.used)
        self.used += count

    def copy(self, name, piece):
        src, dst, axis, count, first = self.table[name]
        if count > 1:
            width = src.shape[axis] // count
            at = pl.ds(pl.multiple_of(piece * width, width), width)
            where = (at,) if axis == 0 else (slice(None), at)
            src, dst = src.at[where], dst.at[where]
        return pltpu.make_async_copy(src, dst, self.sems.at[first + piece])

    def put(self, name, piece=0):
        self.copy(name, piece).start()

    def need(self, name, piece=0):
        self.copy(name, piece).wait()


def call(body, outs, scratch, args, smem, name, us=1.0, late=None, early=None, raw=(), limit=58, static=None):
    late, early = late or {}, early or {}
    kinds = [pltpu.VMEM(*x) if isinstance(x, tuple) else x for x in scratch]
    names = list(inspect.signature(body).parameters)[1:]
    body = functools.partial(body, **static) if static else body
    n_in, n_out, n_own = len(args), len(outs), len(scratch)
    late_at = {n: names.index(n) for n in late}
    early_at = {n: names.index(n) - n_in for n in early}
    total = sum(c for _, c in late.values()) + sum(c for _, c in early.values())

    def wrapped(*refs):
        refs = list(refs)
        sems = refs.pop() if total else None
        flow = Flow(sems)
        bufs = refs[n_in + n_out + n_own :]
        for n, buf in zip([*late, *early], bufs):
            if n in late:
                at = late_at[n]
                flow.add(n, refs[at], buf, *late[n])
            else:
                at = n_in + early_at[n]
                flow.add(n, buf, refs[at], *early[n])
            refs[at] = buf
        waiting = list(late)
        while waiting:
            count = late[waiting[0]][1]
            group = []
            while waiting and late[waiting[0]][1] == count:
                group.append(waiting.pop(0))
            for piece in range(count):
                for n in group:
                    flow.put(n, piece)
        body(flow, *refs[: n_in + n_out + n_own])
        for n, (_, count) in early.items():
            for piece in range(count):
                flow.need(n, piece)

    vmem, any_ = pltpu.VMEM, pl.ANY
    in_specs = [
        pl.BlockSpec(
            memory_space=pltpu.SMEM if i < smem else any_ if i in late_at.values() or names[i] in raw else vmem
        )
        for i in range(n_in)
    ]
    out_specs = [
        pl.BlockSpec(memory_space=any_ if i in early_at.values() or names[n_in + i] in raw else vmem)
        for i in range(n_out)
    ]
    bufs = [pltpu.VMEM(args[late_at[n]].shape, args[late_at[n]].dtype) for n in late]
    bufs += [pltpu.VMEM(*outs[early_at[n]]) for n in early]
    return pl.pallas_call(
        wrapped,
        out_shape=[jax.ShapeDtypeStruct(s, d) for s, d in outs],
        in_specs=in_specs,
        out_specs=out_specs,
        scratch_shapes=kinds
        + bufs
        + ([pltpu.SemaphoreType.DMA((total,))] if total else []),
        compiler_params=pltpu.CompilerParams(vmem_limit_bytes=limit * 1024 * 1024),
        cost_estimate=pl.CostEstimate(
            flops=int(us * 9e8), bytes_accessed=int(us * 3e6), transcendentals=0
        ),
        name=name,
    )(*args)


def swap(x):
    return lax.ppermute(x, "tensor", [(0, 1), (1, 0)])


def across(x, groups, bit):
    return lax.ppermute(x, "dp", [(i, i ^ bit) for i in range(groups)])


def phases_of(groups):
    found, weight = [], 1
    while weight < groups:
        members = min(4, groups // weight)
        found.append((weight, members))
        weight *= members
    return found


def send_round(blocks, groups, weight):
    return [blocks[0]] + [across(b, groups, k * weight) for k, b in enumerate(blocks) if k]


def resplit(x, at):
    value = x[:, at : at + 64] + x[:, at + 64 : at + 128]
    upper = lax.reduce_precision(value, 8, 7)
    return jnp.concatenate([x[:, :at], upper, value - upper, x[:, at + 128 :]], 1)


def split(x, rank, weight, members):
    rows = x.shape[0] // members
    place = (rank // weight) % members
    return [lax.dynamic_slice_in_dim(x, (place ^ k) * rows, rows, 0) for k in range(members)]


def assemble(got, rank, weight):
    members = len(got)
    place = (rank // weight) % members
    parts = []
    for i in range(members):
        now = got[i]
        for p in range(1, members):
            now = jnp.where(place == p, got[i ^ p], now)
        parts.append(now)
    return jnp.concatenate(parts, 0)


def on_device(
    hidden_in, teacher, loss_mask, lengths, dealing, norm_gain, w_gate, w_value, w_state, w_step,
    step_bias, conv_value, conv_vbias, conv_state, conv_sbias, decay_log, skip_gain, out_gain, w_out,
):
    groups = lax.axis_size("dp")
    rank = lax.axis_index("dp")
    member = lax.axis_index("tensor")
    seqs, local, _ = hidden_in.shape
    half = teacher.shape[2]
    T = local * groups
    C = w_gate.shape[1]
    HH = decay_log.shape[0]
    CH = T // Q

    [dealt] = call(deal_kernel, [((seqs, local, half), BF)], [], (dealing, hidden_in), 1, "deal", 3.0)
    dealt, loss_mask, teacher, w_gate = lax.optimization_barrier((dealt, loss_mask, teacher, w_gate))
    xo = lax.all_to_all(dealt, "dp", split_axis=0, concat_axis=0, tiled=True).reshape(T, half)

    pos = rank * local + lax.broadcasted_iota(jnp.int32, (seqs, local), 1)
    marks = (loss_mask > 0) & (pos < lengths[:, None])
    count = jnp.sum(marks.astype(F32)).reshape(1)
    goal = jnp.where(marks[:, :, None], teacher, jnp.asarray(NOMARK, BF))
    [goal] = call(deal_kernel, [((seqs, local, half), BF)], [], (dealing, goal), 1, "deal_goal", 2.0)
    length = lax.dynamic_slice_in_dim(lengths, dealing[rank], 1, 0)

    wcat, wt, wot, cd = call(
        prepare_kernel,
        [((D, 2 * C + 384), BF), ((2 * C + 384, D), BF), ((D, C), BF), ((D, 8), F32)],
        [],
        (w_gate, w_value, w_state, w_step.reshape(D, 2 * HH), w_out, norm_gain[None]),
        0,
        "prepare",
        6.0,
        early={"wcat": (0, 1), "wt": (0, 1)},
    )
    zc = jnp.zeros((256,), F32)
    cc = jnp.concatenate(
        [
            jnp.concatenate([conv_value, conv_state], 1),
            jnp.concatenate([conv_vbias, conv_sbias])[None],
            jnp.concatenate([jnp.repeat(skip_gain, PS), zc])[None],
            jnp.concatenate([out_gain, zc])[None],
            jnp.zeros((1, C + 256), F32),
        ],
        0,
    ).T
    rate = -jnp.exp(decay_log)
    rc = jnp.stack([step_bias.reshape(-1), jnp.concatenate([rate, rate])], 1)

    xo, goal, wcat, wt, wot, cc, cd, rc, count, length = lax.optimization_barrier(
        (xo, goal, wcat, wt, wot, cc, cd, rc, count, length)
    )
    xs = swap(xo)
    to = lax.all_to_all(goal, "dp", split_axis=0, concat_axis=0, tiled=True).reshape(T, half)
    ts = swap(to)

    full = lambda n: ((n, T), BF)
    fullf = lambda n: ((n, T), F32)
    xT, nT, rows, dec, gate, u, pre, act, cs, e, mixed, sin, p0, inv = call(
        forward_kernel,
        [
            full(D), full(D), fullf(120), ((CH, 24, Q), F32), fullf(C), full(C + 256), full(C + 256),
            full(C + 256), full(128), ((CH, HH, Q, Q), BF), fullf(C), ((CH, C, Q), BF), full(D + 16), fullf(8),
        ],
        [
            ((C + 256, T), F32), ((32, T), F32), ((24, T), F32), ((CH, C, Q), F32), ((C, Q), F32),
            ((C, 2 * Q), BF), ((C, T), BF),
        ],
        (length, xo, xs, wt, wot, cc, cd, rc),
        1,
        "forward",
        26.0,
        late={"xo": (0, CH // 2), "xs": (0, CH // 2), "wt": (0, 1), "cc": (0, 1), "wot": (0, 1)},
        early={
            **{n: (0, 1) for n in ("xT", "nT", "rows", "dec", "gate", "uO", "preO", "act", "cs", "sin")},
            "mixed": (1, CH // 2),
            "eO": (0, CH // 2), "pO": (1, T // 256),
        },
    )
    p1 = swap(p0)
    lo, doh, dyT, dgate, small, *mids = call(
        middle_kernel,
        [((T, half), BF), full(half), full(C), full(C), ((C, Q), F32)] + [((D // 4, D + C), BF)] * 4,
        [
            ((D, Q), F32), ((D, Q), F32), ((C, T), BF), ((C, 256), F32), ((8, T), F32), ((C, Q), F32),
            ((8, T), F32), full(D),
        ],
        (p0, p1, xT, to, ts, w_out, nT, gate, mixed, cc),
        0,
        "middle",
        14.0,
        late={
            **{n: (1, CH // 2) for n in ("p0", "p1", "xT")}, "to": (0, CH // 2), "ts": (0, CH // 2),
            "wo": (0, 1), "cc": (0, 1), "gate": (1, T // 256), "mixed": (1, T // 256), "nT": (0, 1),
        },
        early={
            "dyT": (1, T // 256), **{n: (0, 1) for n in ("doh", "lo", "dgate", "m0", "m1", "m2", "m3")},
        },
    )
    phases = phases_of(groups)
    got_m = send_round(mids, groups, 1)
    rowsf = ((24, T), F32)
    width = C + Q + 256
    b0, b1, b2, b3, dno, dnx, dots = call(
        backward_kernel,
        [((D // 4, width), BF)] * 4 + [full(half), full(half + 16), fullf(8)],
        [
            ((D, Q), F32), rowsf, fullf(C + 256), rowsf, rowsf, rowsf, rowsf, ((CH, HH, Q), F32), ((CH, C, Q), F32),
            ((CH, C, Q), BF), ((C, Q), F32), ((C, 2 * Q), BF), ((C, 2 * Q), BF), ((C, Q), F32), rowsf,
            ((C + 256, 5 * Q), F32), full(2 * C + 384), ((D, 256), F32),
        ],
        (length, count, act, cs, rows, dec, e, sin, dyT, u, pre, dgate, nT, wcat, cc, cd, rc, small),
        2,
        "backward",
        30.0,
        late={
            **{n: (0, 1) for n in ("rows", "cs")},
            "dyT": (1, CH // 2),
            **{n: (0, 1) for n in ("dec", "sin", "act", "cc")},
            "e_in": (0, CH // 2),
            **{n: (0, 1) for n in ("dgate", "u_in", "pre_in", "small", "nT", "wcat", "cd")},
        },
        early={
            "dno": (1, T // 256), "dnx": (1, T // 256), **{n: (0, 1) for n in ("b0", "b1", "b2", "b3")},
        },
    )
    now_m = sum(g.astype(F32) for g in got_m)
    dnr = swap(dnx)
    now_m, dnr = lax.optimization_barrier((now_m, dnr))
    blocks = split(now_m, rank, *phases[1])
    got_m = send_round([b if k == 0 else b.astype(BF) for k, b in enumerate(blocks)], groups, phases[1][0])
    got = send_round([b0, b1, b2, b3], groups, 1)
    [dx] = call(
        last_kernel,
        [((T, half), BF)],
        [((half, T), BF), pltpu.SemaphoreType.DMA((CH,))],
        (dno, dnr, doh, dots, inv, xT),
        0,
        "last",
        3.0,
        late={n: (1, T // 512) for n in ("dno", "dnr", "do_s")},
        early={"out": (0, T // 512)},
        raw=("xT",),
    )
    dx, got, got_m = lax.optimization_barrier((dx, got, got_m))
    held = sum(g.astype(F32) for g in got_m)
    for weight, members in phases[2:]:
        blocks = split(held, rank, weight, members)
        got_m = send_round([b if k == 0 else b.astype(BF) for k, b in enumerate(blocks)], groups, weight)
        held = sum(g.astype(F32) for g in got_m)
    held = held.astype(BF)
    now = resplit(sum(g.astype(F32) for g in got), C)
    for weight, members in reversed(phases[1:]):
        pieces = send_round([held] * members, groups, weight)
        now, pieces = lax.optimization_barrier((now, pieces))
        held = assemble(pieces, rank, weight)
    held = send_round([held] * 4, groups, 1)
    for weight, members in phases[1:]:
        blocks = split(now, rank, weight, members)
        got = send_round([b if k == 0 else b.astype(BF) for k, b in enumerate(blocks)], groups, weight)
        now = resplit(sum(g.astype(F32) for g in got), C)
    lane = lax.broadcasted_iota(jnp.int32, (1, Q + 256), 1)
    both = (lane >= Q) | ((lane % 64 >= 41) & (lane % 64 < 47))
    tail = now[:, C:]
    tail = resplit(tail + jnp.where(both, swap(tail.astype(BF)).astype(F32), 0.0), 0)
    now = jnp.concatenate([now[:, :C], tail], 1).astype(BF)
    now, held = lax.optimization_barrier((now, held))
    for weight, members in reversed(phases[1:]):
        now = assemble(send_round([now] * members, groups, weight), rank, weight)
    back = lax.all_to_all(dx.reshape(seqs, local, half), "dp", split_axis=0, concat_axis=0, tiled=True)
    now, back = lax.optimization_barrier((now, back))
    got = send_round([now] * 4, groups, 1)
    wo, wg, grad_in = call(
        finish_first_kernel,
        [((C, D), F32), ((D, C), F32), ((seqs, local, half), BF)],
        [],
        (dealing, now[0:8, C : C + Q], *held, back),
        1,
        "finish_first",
        5.0,
        late={n: (0, 1) for n in ("h0", "h1", "h2", "h3", "back")},
        early={n: (0, 1) for n in ("wo", "wg", "grad_in")},
        static={"full_len": T},
    )
    gv, gt, gs, ng, cv, vb, cst, sb, dl, sk, og, bias = call(
        finish_kernel,
        [
            ((D, C), F32), ((D, 2 * HH), F32), ((D, 256), F32), ((D,), F32), ((4, C), F32), ((C,), F32),
            ((4, 256), F32), ((256,), F32), ((HH,), F32), ((HH,), F32), ((C,), F32), ((2, HH), F32),
        ],
        [((D, Q), F32)],
        tuple(got),
        0,
        "finish",
        4.0,
        late={n: (0, 1) for n in ("g0", "g1", "g2", "g3")},
        early={n: (0, 1) for n in ("gv", "gs")},
        static={"full_len": T},
    )
    return (
        lo[None], grad_in, ng, wg, gv, gs, gt.reshape(D, 2, HH), bias, cv, vb, cst, sb, dl, sk, og, wo,
    )


def solution(mesh):
    dp, tp = "dp", "tensor"
    return jax.shard_map(
        on_device,
        mesh=mesh,
        in_specs=(
            P(None, dp, None), P(None, dp, tp), P(None, dp), P(), P(), P(), P(None, tp), P(None, tp), P(),
            P(None, None, tp), P(None, tp), P(None, tp), P(tp), P(), P(), P(tp), P(tp), P(tp), P(tp, None),
        ),
        out_specs=(
            P(dp, None, tp), P(None, dp, tp), P(), P(None, tp), P(None, tp), P(), P(None, None, tp),
            P(None, tp), P(None, tp), P(tp), P(), P(), P(tp), P(tp), P(tp), P(tp, None),
        ),
        check_vma=False,
    )
```
